512 devices in a mesh: seq: 64 (over y, z), head: 8 (over x, core).
Axes of the slice: x: 4, y: 4, z: 16, core: 2. Of those that a mesh axis runs over, the one named last changes fastest.
Arguments:
- queries: bfloat16 [65536, 16, 128], P(('seq', 'head')), may hold values from -6 to 6
- keys: bfloat16 [65536, 16, 2, 128], P(('seq', 'head')), may hold values from -6 to 6
- values: bfloat16 [65536, 16, 2, 128], P(('seq', 'head')), may hold values from -6 to 6
- betas: bfloat16 [65536, 16, 2], P(('seq', 'head')), may hold values from 0 to 2
- gate: bfloat16 [65536, 16, 128], P(('seq', 'head')), may hold values from -6 to 6
- gain: float32 [16, 128], P('head'), may hold values from 0.1 to 1.9
Outputs:
- mixed: bfloat16 [65536, 16, 128], P(('seq', 'head'))
The draws below stay inside these ranges and needn't reach their ends.
All inputs are finite; a program needn't handle non-finite values.
Results may differ from the reference program's by a relative error of at most 0.0012.
Values may be sent and summed in bfloat16 or wider, within the bound.
A program may use at most 128 MiB of HBM per device.

```python
import jax
import jax.numpy as jnp
from jax import lax

LOCAL_HEADS = 16
K = 128
REFLECTION_COUNT = 2
SEQ_ROWS = 1024
SEQUENCE_TOKENS = 65536


def log_uniform(key_one, shape, low_end, high_end):
    return jnp.exp(jax.random.uniform(key_one, shape, jnp.float32, jnp.log(low_end), jnp.log(high_end)))


def draw_betas(key, part):
    key = jax.random.fold_in(key, 7)
    every_key_vector = jax.random.split(key, 7)
    fast_share = 0.5
    jitter_low = 0.5
    jitter_high = 1.5
    fast_heads = jax.random.uniform(every_key_vector[0], (LOCAL_HEADS,)) < fast_share
    fast_base = log_uniform(every_key_vector[1], (LOCAL_HEADS,), 0.6, 1.1)
    slow_base = log_uniform(every_key_vector[2], (LOCAL_HEADS,), 0.0002, 0.0012)
    base_rate = jnp.where(fast_heads, fast_base, slow_base)
    segment_mod = log_uniform(every_key_vector[3], (SEQUENCE_TOKENS // SEQ_ROWS, LOCAL_HEADS), 0.5, 2.0)
    segment_mod = jnp.repeat(segment_mod, SEQ_ROWS, axis=0)
    jitter = jax.random.uniform(every_key_vector[4], (SEQUENCE_TOKENS, LOCAL_HEADS, REFLECTION_COUNT), jnp.float32, jitter_low, jitter_high)
    spike_intensity = base_rate[None, :, None] * segment_mod[:, :, None] * jitter
    spike_begin_points = jax.random.randint(every_key_vector[5], (3,), 0, SEQUENCE_TOKENS - 31)
    token_offset = jnp.arange(SEQUENCE_TOKENS)
    inside_spike = jnp.any((token_offset[:, None] >= spike_begin_points[None, :]) & (token_offset[:, None] < spike_begin_points[None, :] + 32), axis=1)
    spike_magnitudes = jax.random.uniform(every_key_vector[6], (SEQUENCE_TOKENS, LOCAL_HEADS, REFLECTION_COUNT), jnp.float32, 0.6, 1.2)
    spike_intensity = jnp.where(inside_spike[:, None, None], spike_magnitudes, spike_intensity)
    return jnp.clip(spike_intensity, 0.0001, 1.9).astype(jnp.bfloat16)


def levels(key, dims, cuts, least, top_value):
    level, own = 1.0, jax.random.fold_in(key, 6)
    for dim, shards_of in cuts:
        draws = jnp.exp(jax.random.uniform(jax.random.fold_in(own, dim), (shards_of,), jnp.float32, least / len(cuts), top_value / len(cuts)))
        level = level * jnp.repeat(draws, dims[dim] // shards_of).reshape([-1 if axis == dim else 1 for axis in range(len(dims))])
    return level


def centred(stream_key, extent, width, limit, cuts=(), kind=jnp.bfloat16):
    array = jax.random.normal(stream_key, extent, jnp.float32) * width
    if len(cuts) > 0:
        array = levels(stream_key, extent, cuts, -0.22, 0.18) * array
    return jnp.clip(array, min=-limit, max=limit).astype(kind)


def setup_inputs(seed: int = 0) -> dict:
    arg_keys = jax.random.split(jax.random.key(seed), 7)
    return {
        "queries": centred(arg_keys[0], (SEQUENCE_TOKENS, LOCAL_HEADS, K), 1.0, 6.0, ((0, 512),)),
        "keys": centred(arg_keys[1], (SEQUENCE_TOKENS, LOCAL_HEADS, REFLECTION_COUNT, K), 1.0, 6.0, ((0, 512),)),
        "values": centred(arg_keys[2], (SEQUENCE_TOKENS, LOCAL_HEADS, REFLECTION_COUNT, K), 1.0, 6.0, ((0, 512),)),
        "betas": draw_betas(jax.random.fold_in(arg_keys[6], 71), 0),
        "gate": centred(arg_keys[4], (SEQUENCE_TOKENS, LOCAL_HEADS, K), 1.0, 6.0, ((0, 512),)),
        "gain": jnp.clip(1.0 + 0.18 * jax.random.normal(arg_keys[5], (LOCAL_HEADS, K), jnp.float32), 0.1, 1.9),
    }


exact_prec = lax.Precision.HIGHEST

def unit_rows(matrix):
    return matrix * lax.rsqrt(lax.optimization_barrier(jnp.sum(matrix * matrix, axis=-1, keepdims=True)) + 1e-06)

def one_head(inputs):
    query_h, key_h, value_h, beta_h, gate_h, gain_h = inputs
    tok_count, steps_per, head_width = key_h.shape
    substeps = tok_count * steps_per
    block_len = min(128, substeps)
    group_count = substeps // block_len
    tok_block = block_len // steps_per
    keys_f = unit_rows(key_h.astype(jnp.float32).reshape(group_count, block_len, head_width))
    vals_f = value_h.astype(jnp.float32).reshape(group_count, block_len, head_width)
    spike_intensity = beta_h.astype(jnp.float32).reshape(group_count, block_len)
    query_f = query_h.astype(jnp.float32).reshape(group_count, tok_block, head_width)
    sub_index = jnp.arange(block_len)
    tok_index = jnp.arange(tok_block)
    strict_lower = sub_index[:, None] > sub_index[None, :]
    visible = sub_index[None, :] <= steps_per * tok_index[:, None] + steps_per - 1
    identity = jnp.eye(block_len, dtype=jnp.float32)

    def advance(memory, group):
        keys_c, vals_c, beta_c, query_c = group
        grams = jnp.dot(keys_c, keys_c.T, precision=exact_prec)
        system = identity + jnp.where(strict_lower, beta_c[:, None] * grams, 0.0)
        right_sides = jnp.concatenate([beta_c[:, None] * keys_c, beta_c[:, None] * vals_c], axis=1)
        solved = lax.linalg.triangular_solve(system, right_sides, left_side=True, lower=True, unit_diagonal=True)
        w_part = solved[:, :head_width]
        u_part = solved[:, head_width:]
        fresh_vals = u_part - jnp.dot(w_part, memory, precision=exact_prec)
        scores = jnp.where(visible, jnp.dot(query_c, keys_c.T, precision=exact_prec), 0.0)
        result = jnp.dot(query_c, memory, precision=exact_prec) + jnp.dot(scores, fresh_vals, precision=exact_prec)
        memory = memory + jnp.dot(keys_c.T, fresh_vals, precision=exact_prec)
        return (memory, result)
    start = jnp.zeros((head_width, head_width), jnp.float32)
    _, outputs = lax.scan(advance, start, (keys_f, vals_f, spike_intensity, query_f))
    outputs = outputs.reshape(tok_count, head_width)
    normed = outputs * lax.rsqrt(lax.optimization_barrier(jnp.mean(outputs * outputs, axis=-1, keepdims=True)) + 1e-06) * gain_h[None, :]
    return (normed * jax.nn.silu(gate_h.astype(jnp.float32))).astype(jnp.bfloat16)

def reference(queries, keys, values, betas, gate, gain):
    stacked = (jnp.swapaxes(queries, 0, 1), jnp.swapaxes(keys, 0, 1), jnp.swapaxes(values, 0, 1), jnp.swapaxes(betas, 0, 1), jnp.swapaxes(gate, 0, 1), gain)
    result = lax.map(one_head, stacked)
    return jnp.swapaxes(result, 0, 1)
```

```python
import functools
import jax, jax.numpy as jnp
from jax import lax
from jax.experimental import pallas as pl
from jax.experimental.pallas import tpu as pltpu
from jax.sharding import PartitionSpec as P
f32, bf16 = jnp.float32, jnp.bfloat16
D = 128
N = 256
T = 128
BASE = 16

def split(a):
    hi = a.astype(bf16)
    return hi, (a - hi.astype(f32)).astype(bf16)

def mm(a, b):
    return lax.dot_general(a, b, (((1,), (0,)), ((), ())), preferred_element_type=f32)

def mm_nt(a, b):
    return lax.dot_general(a, b, (((1,), (1,)), ((), ())), preferred_element_type=f32)

def mm_tn(a, b):
    return lax.dot_general(a, b, (((0,), (0,)), ((), ())), preferred_element_type=f32)

def dot3(a, b):
    ah, al = split(a)
    bh, bl = split(b)
    return dot3s(ah, al, bh, bl)

def dot3s(ah, al, bh, bl):
    if ah.shape[1] == 128:
        return mm(jnp.concatenate([ah, al], 1), jnp.concatenate([bh, bh], 0)) + mm(ah, bl)
    return mm(ah, bh) + (mm(al, bh) + mm(ah, bl))

def unit_lower_inverses(lows):
    n = len(lows)
    lane = lax.broadcasted_iota(jnp.int32, (BASE, 128), 1)
    row = lax.broadcasted_iota(jnp.int32, (BASE, 128), 0)
    blk = lane // BASE
    packed = []
    for low in lows:
        z = jnp.zeros((BASE, 128), f32)
        for b in range(128 // BASE):
            z = jnp.where(blk == b, low[BASE * b:BASE * (b + 1), :], z)
        packed.append(jnp.where(row > lane % BASE, z, 0.0))
    eye = jnp.where(row == lane % BASE, 1.0, 0.0).astype(f32)
    xs = [eye for _ in lows]
    for j in range(BASE - 1):
        idx = blk * BASE + j
        for i in range(n):
            lj = jnp.take_along_axis(packed[i], idx, axis=1, mode="promise_in_bounds")
            xs[i] = xs[i] - lj * xs[i][j:j + 1, :]
    fulls = []
    for x in xs:
        fulls.append(jnp.concatenate([jnp.where(blk == b, x, 0.0) for b in range(128 // BASE)], axis=0))
    m = BASE
    r2 = lax.broadcasted_iota(jnp.int32, (128, 128), 0)
    c2 = lax.broadcasted_iota(jnp.int32, (128, 128), 1)
    while m < 128:
        offmask = ((r2 // m) % 2 == 1) & (c2 // m == r2 // m - 1)
        out = []
        for i in range(n):
            x = fulls[i]
            odd = [x[m * (2 * b + 1):m * (2 * b + 2), :] for b in range(64 // m)]
            xo = jnp.concatenate(odd, 0) if len(odd) > 1 else odd[0]
            off = jnp.where(offmask, lows[i], 0.0)
            xh, xl = split(x)
            xoh, xol = split(xo)
            y = dot3s(xoh, xol, *split(off))
            z = xo - dot3s(*split(y), xh, xl)
            rows = []
            for b in range(64 // m):
                rows.append(x[m * 2 * b:m * (2 * b + 1), :])
                rows.append(z[m * b:m * (b + 1), :])
            out.append(jnp.concatenate(rows, 0))
        fulls = out
        m *= 2
    return fulls

def local_kernel(hb, k_ref, v_ref, q_ref, b_ref, ab_ref, qo_ref):
    g = pl.program_id(0)
    lane = lax.broadcasted_iota(jnp.int32, (N, 16), 1)
    betas = b_ref[...]
    r2 = lax.broadcasted_iota(jnp.int32, (128, 128), 0)
    c2 = lax.broadcasted_iota(jnp.int32, (128, 128), 1)
    vis = lax.broadcasted_iota(jnp.int32, (T, N), 1) <= 2 * lax.broadcasted_iota(jnp.int32, (T, N), 0) + 1
    eye = jnp.where(r2 == c2, 1.0, 0.0).astype(f32)
    lows, rest = [], []
    for h in range(hb):
        k = k_ref[h]
        kf = k.astype(f32)
        ssq = jnp.sum(kf * kf, axis=1, keepdims=True) + 1e-6
        beta = jnp.sum(jnp.where(lane == g * hb + h, betas, 0.0), axis=1, keepdims=True)
        p = beta / ssq
        bs = beta * lax.rsqrt(ssq)
        gram = mm_nt(k, k)
        l11 = jnp.where(r2 > c2, p[:128] * gram[:128, :128], 0.0)
        l22 = jnp.where(r2 > c2, p[128:] * gram[128:, 128:], 0.0)
        l21 = p[128:] * gram[128:, :128]
        rhs = jnp.concatenate([p * kf, bs * v_ref[h].astype(f32)], axis=1)
        lows += [l11, l22]
        rest.append((k, l21, rhs))
    invs = unit_lower_inverses(lows)
    for h in range(hb):
        k, l21, rhs = rest[h]
        t1, t2 = invs[2 * h], invs[2 * h + 1]
        y1 = dot3(t1, rhs[:128])
        y2 = dot3(t2, rhs[128:] - dot3(l21, y1))
        yh, yl = split(jnp.concatenate([y1, y2], 0))
        ky = mm_tn(k, yh) + mm_tn(k, yl)
        ab_ref[h, :, :128] = eye - ky[:, :128]
        ab_ref[h, :, 128:] = ky[:, 128:]
        q = q_ref[h]
        s = jnp.where(vis, mm_nt(q, k), 0.0)
        sh, sl = split(s)
        sy = dot3s(sh, sl, yh, yl)
        qo_ref[h, :, :128] = q.astype(f32) - sy[:, :128]
        qo_ref[h, :, 128:] = sy[:, 128:]

def local_maps(keys, values, queries, betas, hb=2):
    H = keys.shape[0]
    return pl.pallas_call(
        functools.partial(local_kernel, hb),
        grid=(H // hb,),
        in_specs=[
            pl.BlockSpec((hb, N, D), lambda i: (i, 0, 0)),
            pl.BlockSpec((hb, N, D), lambda i: (i, 0, 0)),
            pl.BlockSpec((hb, T, D), lambda i: (i, 0, 0)),
            pl.BlockSpec((N, 16), lambda i: (0, 0)),
        ],
        out_specs=[
            pl.BlockSpec((hb, D, 2 * D), lambda i: (i, 0, 0)),
            pl.BlockSpec((hb, T, 2 * D), lambda i: (i, 0, 0)),
        ],
        out_shape=[jax.ShapeDtypeStruct((H, D, 2 * D), f32), jax.ShapeDtypeStruct((H, T, 2 * D), f32)],
        compiler_params=pltpu.CompilerParams(vmem_limit_bytes=48 * 2**20),
    )(keys, values, queries, betas)

MESH = pl.DeviceIdType.MESH
HEADS = 16
NX, NL, NG, NY = 4, 4, 4, 4


def compose(late, early):
    joined = dot3(late[:, :D], early)
    return jnp.concatenate([joined[:, :D], joined[:, D:] + late[:, D:]], axis=1)


def advance(pair, state):
    return dot3(pair[:, :D], state) + pair[:, D:]


def scan_kernel(
    ab_ref, gain_ref, m_ref, gains_ref,
    both, chip, row_in, row_pre, row_tot, low_in, low_pre, low_tot,
    high_in, high_pre, high_tot, y_in, y_state, state, low_out, low_state,
    row_out, chip_state, after,
    local_sem, send, recv,
):
    seq, head = lax.axis_index("seq"), lax.axis_index("head")
    x, c = head // 2, head % 2
    y, g, l = seq // (NG * NL), (seq // NL) % NG, seq % NL
    oc = 1 - c

    def device(xx=None, cc=None, yy=None, gg=None, ll=None):
        xx, cc = x if xx is None else xx, c if cc is None else cc
        yy, gg, ll = y if yy is None else yy, g if gg is None else gg, l if ll is None else ll
        return {"seq": (yy * NG + gg) * NL + ll, "head": xx * 2 + cc}

    partner = device(cc=oc)

    def others(me, count):
        return [(me + k) % count for k in range(1, count)]

    def remote(src, dst, s, r, where):
        return pltpu.make_async_remote_copy(
            src_ref=src, dst_ref=dst, send_sem=send.at[s], recv_sem=recv.at[r],
            device_id=where, device_id_type=MESH,
        )

    peers = [partner]
    peers += [device(xx=v) for v in others(x, NX)]
    peers += [device(ll=v) for v in others(l, NL)]
    peers += [device(gg=v) for v in others(g, NG)]
    peers += [device(yy=v) for v in others(y, NY)]
    barrier = pltpu.get_barrier_semaphore()
    for peer in peers:
        pl.semaphore_signal(barrier, inc=1, device_id=peer, device_id_type=MESH)
    own = pltpu.make_async_copy(ab_ref.at[pl.ds(8 * c, 8)], both.at[c], local_sem)
    own.start()
    gains_ref[head] = gain_ref[...]
    pl.semaphore_wait(barrier, len(peers))

    pair_copies = []
    for i in range(8):
        copy = remote(ab_ref.at[8 * oc + i], both.at[c, i], i, i, partner)
        copy.start()
        pair_copies.append(copy)
    gain_copy = remote(gain_ref, gains_ref.at[head], 8, 8, partner)
    gain_copy.start()
    own.wait()

    def pair_recv(i):
        remote(ab_ref.at[i], both.at[oc, i], i, i, partner).wait_recv()

    row_copies = []
    for k in (1, 2, 3, 0):
        dest = (x + k) % NX
        for e in range(2):
            i = 2 * dest + e
            remote(ab_ref.at[i], both.at[oc, i], i, i, partner).wait_recv()
            joined = compose(both[1, i], both[0, i])
            if k == 0:
                row_in[x, e] = joined
            else:
                chip[i] = joined
        if k:
            copy = remote(chip.at[pl.ds(2 * dest, 2)], row_in.at[x], 9 + k, 9 + x, device(xx=dest))
            copy.start()
            row_copies.append(copy)
    remote(gain_ref, gains_ref.at[2 * x + oc], 8, 8, partner).wait_recv()
    gain_copies = []
    for k in (1, 2, 3):
        copy = remote(
            gains_ref.at[pl.ds(2 * x, 2)], gains_ref.at[pl.ds(2 * x, 2)], 13 + k, 13 + x,
            device(xx=(x + k) % NX),
        )
        copy.start()
        gain_copies.append(copy)

    for k in (1, 2, 3):
        origin = (x + k) % NX
        remote(chip.at[pl.ds(0, 2)], row_in.at[origin], 9 + k, 9 + origin, device(xx=origin)).wait_recv()
    for e in range(2):
        row_pre[0, e] = row_in[0, e]
    for s in (1, 2):
        for e in range(2):
            row_pre[s, e] = compose(row_in[s, e], row_pre[s - 1, e])
    for e in range(2):
        row_tot[e] = compose(row_in[3, e], row_pre[2, e])

    active = l % 2 == c
    for e in range(2):
        owner = 2 * e + c
        out = remote(row_tot.at[e], low_in.at[l], 17 + e, 17 + l, device(ll=owner))

        @pl.when(owner != l)
        def _():
            out.start()

        @pl.when(owner == l)
        def _():
            low_in[l] = row_tot[e]

    def high_copy(k, there, slot):
        return remote(high_tot, high_in.at[slot], 21 + k, 21 + slot, device(gg=there))

    def y_copy(k, there, slot):
        return remote(low_tot, y_in.at[slot], 25 + k, 25 + slot, device(yy=there))

    def low_copy(k, there, e):
        return remote(low_out.at[there], low_state.at[e], 29 + k, 29 + e, device(ll=there))

    @pl.when(active)
    def _():
        for k in (1, 2, 3):
            origin = (l + k) % NL
            remote(row_tot.at[0], low_in.at[origin], 17, 17 + origin, device(ll=origin)).wait_recv()
        low_pre[0] = low_in[0]
        for s in (1, 2):
            low_pre[s] = compose(low_in[s], low_pre[s - 1])
        total = compose(low_in[3], low_pre[2])
        high_tot[...] = total
        high_in[g] = total
        for k in (1, 2, 3):
            high_copy(k, (g + k) % NG, g).start()
        for k in (1, 2, 3):
            origin = (g + k) % NG
            high_copy(k, origin, origin).wait_recv()
        high_pre[0] = high_in[0]
        for s in (1, 2):
            high_pre[s] = compose(high_in[s], high_pre[s - 1])
        total = compose(high_in[3], high_pre[2])
        low_tot[...] = total
        y_in[y] = total
        for k in (1, 2, 3):
            y_copy(k, (y + k) % NY, y).start()
        for k in (1, 2, 3):
            origin = (y + k) % NY
            y_copy(k, origin, origin).wait_recv()
        y_state[0] = jnp.zeros((D, D), f32)
        y_state[1] = y_in[0, :, D:]
        for s in (1, 2):
            y_state[s + 1] = advance(y_in[s], y_state[s])
        state[...] = y_state[y]

        @pl.when(g > 0)
        def _():
            state[...] = advance(high_pre[g - 1], state[...])

        low_out[0] = state[...]
        for s in (0, 1, 2):
            low_out[s + 1] = advance(low_pre[s], state[...])
        for k in (1, 2, 3):
            low_copy(k, (l + k) % NL, l // 2).start()
        low_state[l // 2] = low_out[l]

    for e in range(2):
        owner = 2 * e + c

        @pl.when(owner != l)
        def _():
            low_copy(0, owner, e).wait_recv()

    for e in range(2):
        row_out[0, e] = low_state[e]
        for s in (0, 1, 2):
            row_out[s + 1, e] = advance(row_pre[s, e], low_state[e])
    state_copies = []
    for k in (1, 2, 3):
        dest = (x + k) % NX
        copy = remote(row_out.at[dest], chip_state.at[pl.ds(2 * x, 2)], 33 + k, 33 + x, device(xx=dest))
        copy.start()
        state_copies.append(copy)
    for e in range(2):
        chip_state[2 * x + e] = row_out[x, e]

    def back_copy(i):
        return remote(after.at[i], m_ref.at[8 * c + i], 37 + i, 37 + i, partner)

    for k in (0, 1, 2, 3):
        origin = (x + k) % NX
        if k:
            remote(
                row_out.at[origin], chip_state.at[pl.ds(2 * origin, 2)], 33 + k, 33 + origin, device(xx=origin)
            ).wait_recv()
        for e in range(2):
            i = 2 * origin + e
            begin = chip_state[i]
            end = advance(both[0, i], begin)

            @pl.when(c == 0)
            def _():
                m_ref[i] = begin
                after[i] = end

            @pl.when(c == 1)
            def _():
                m_ref[8 + i] = end
                after[i] = begin

            back_copy(i).start()
    for i in range(8):
        remote(after.at[i], m_ref.at[8 * oc + i], 37 + i, 37 + i, partner).wait_recv()
    for k in (1, 2, 3):
        origin = (x + k) % NX
        remote(
            gains_ref.at[pl.ds(2 * origin, 2)], gains_ref.at[pl.ds(2 * origin, 2)], 13 + k, 13 + origin,
            device(xx=origin),
        ).wait_recv()

    for copy in pair_copies + [gain_copy] + row_copies + gain_copies + state_copies:
        copy.wait_send()
    for e in range(2):
        @pl.when(2 * e + c != l)
        def _():
            remote(row_tot.at[e], low_in.at[l], 17 + e, 17 + l, device(ll=2 * e + c)).wait_send()

    @pl.when(active)
    def _():
        for k in (1, 2, 3):
            high_copy(k, (g + k) % NG, g).wait_send()
            y_copy(k, (y + k) % NY, y).wait_send()
            low_copy(k, (l + k) % NL, l // 2).wait_send()
    for i in range(8):
        back_copy(i).wait_send()


def scan_states(ab, gain):
    wide, square = (D, 2 * D), (D, D)
    vm = lambda *s: pltpu.VMEM(s, f32)
    return pl.pallas_call(
        scan_kernel,
        in_specs=[pl.BlockSpec(memory_space=pltpu.VMEM), pl.BlockSpec(memory_space=pltpu.VMEM)],
        out_specs=[pl.BlockSpec(memory_space=pltpu.VMEM), pl.BlockSpec(memory_space=pltpu.VMEM)],
        out_shape=[jax.ShapeDtypeStruct((HEADS, D, D), f32), jax.ShapeDtypeStruct((8, 8, D), f32)],
        scratch_shapes=[
            vm(2, 8, *wide), vm(8, *wide), vm(NX, 2, *wide), vm(NX, 2, *wide), vm(2, *wide),
            vm(NL, *wide), vm(NL, *wide), vm(*wide),
            vm(NG, *wide), vm(NG, *wide), vm(*wide), vm(NY, *wide), vm(NY, *square), vm(*square),
            vm(NL, *square), vm(2, *square),
            vm(NX, 2, *square), vm(8, *square), vm(8, *square),
            pltpu.SemaphoreType.DMA, pltpu.SemaphoreType.DMA((45,)), pltpu.SemaphoreType.DMA((45,)),
        ],
        compiler_params=pltpu.CompilerParams(
            collective_id=0, has_side_effects=True, vmem_limit_bytes=48 * 2**20
        ),
    )(ab, gain)


def output_kernel(qo_ref, m_ref, gains_ref, gate_ref, out_ref, rows):
    for h in range(HEADS):
        r = dot3(qo_ref[h, :, :D], m_ref[h]) + qo_ref[h, :, D:]
        scale = lax.rsqrt(jnp.mean(r * r, axis=-1, keepdims=True) + 1e-6)
        rows[h] = r * scale * gains_ref[h // 2, h % 2 : h % 2 + 1, :]
    gate = gate_ref[...].astype(f32)
    normed = jnp.swapaxes(rows[...], 0, 1)
    out_ref[...] = (normed * (gate / (1.0 + jnp.exp(-gate)))).astype(bf16)


def outputs(qo, m, gains, gate):
    whole = pl.BlockSpec(memory_space=pltpu.VMEM)
    return pl.pallas_call(
        output_kernel,
        in_specs=[whole] * 4,
        out_specs=whole,
        out_shape=jax.ShapeDtypeStruct((T, HEADS, D), bf16),
        scratch_shapes=[pltpu.VMEM((HEADS, T, D), f32)],
        compiler_params=pltpu.CompilerParams(vmem_limit_bytes=48 * 2**20),
    )(qo, m, gains, gate)


def local(queries, keys, values, betas, gate, gain):
    keys_h = jnp.transpose(keys, (1, 0, 2, 3)).reshape(HEADS, N, D)
    values_h = jnp.transpose(values, (1, 0, 2, 3)).reshape(HEADS, N, D)
    queries_h = jnp.transpose(queries, (1, 0, 2))
    betas_h = jnp.transpose(betas, (0, 2, 1)).reshape(N, HEADS).astype(f32)
    ab, qo = local_maps(keys_h, values_h, queries_h, betas_h)
    m, gains = scan_states(ab, jnp.pad(gain, ((0, 6), (0, 0))))
    return outputs(qo, m, gains, gate)


def solution(mesh):
    return jax.shard_map(
        local,
        mesh=mesh,
        in_specs=(
            P(("seq", "head"), None, None),
            P(("seq", "head"), None, None, None),
            P(("seq", "head"), None, None, None),
            P(("seq", "head"), None, None),
            P(("seq", "head"), None, None),
            P("head", None),
        ),
        out_specs=P(("seq", "head"), None, None),
        check_vma=False,
    )
```

```python
import functools
import jax, jax.numpy as jnp
from jax import lax
from jax.experimental import pallas as pl
from jax.experimental.pallas import tpu as pltpu
from jax.sharding import PartitionSpec as P
f32, bf16 = jnp.float32, jnp.bfloat16
D = 128
N = 256
T = 128
BASE = 16

def split(a):
    hi = a.astype(bf16)
    return hi, (a - hi.astype(f32)).astype(bf16)

def mm(a, b):
    return lax.dot_general(a, b, (((1,), (0,)), ((), ())), preferred_element_type=f32)

def mm_nt(a, b):
    return lax.dot_general(a, b, (((1,), (1,)), ((), ())), preferred_element_type=f32)

def mm_tn(a, b):
    return lax.dot_general(a, b, (((0,), (0,)), ((), ())), preferred_element_type=f32)

def dot3(a, b):
    ah, al = split(a)
    bh, bl = split(b)
    return dot3s(ah, al, bh, bl)

def dot3s(ah, al, bh, bl):
    if ah.shape[1] == 128:
        return mm(jnp.concatenate([ah, al], 1), jnp.concatenate([bh, bh], 0)) + mm(ah, bl)
    return mm(ah, bh) + (mm(al, bh) + mm(ah, bl))

def unit_lower_inverses(lows):
    n = len(lows)
    lane = lax.broadcasted_iota(jnp.int32, (BASE, 128), 1)
    row = lax.broadcasted_iota(jnp.int32, (BASE, 128), 0)
    blk = lane // BASE
    packed = []
    for low in lows:
        z = jnp.zeros((BASE, 128), f32)
        for b in range(128 // BASE):
            z = jnp.where(blk == b, low[BASE * b:BASE * (b + 1), :], z)
        packed.append(jnp.where(row > lane % BASE, z, 0.0))
    eye = jnp.where(row == lane % BASE, 1.0, 0.0).astype(f32)
    xs = [eye for _ in lows]
    for j in range(BASE - 1):
        idx = blk * BASE + j
        for i in range(n):
            lj = jnp.take_along_axis(packed[i], idx, axis=1, mode="promise_in_bounds")
            xs[i] = xs[i] - lj * xs[i][j:j + 1, :]
    fulls = []
    for x in xs:
        fulls.append(jnp.concatenate([jnp.where(blk == b, x, 0.0) for b in range(128 // BASE)], axis=0))
    m = BASE
    r2 = lax.broadcasted_iota(jnp.int32, (128, 128), 0)
    c2 = lax.broadcasted_iota(jnp.int32, (128, 128), 1)
    while m < 128:
        offmask = ((r2 // m) % 2 == 1) & (c2 // m == r2 // m - 1)
        out = []
        for i in range(n):
            x = fulls[i]
            odd = [x[m * (2 * b + 1):m * (2 * b + 2), :] for b in range(64 // m)]
            xo = jnp.concatenate(odd, 0) if len(odd) > 1 else odd[0]
            off = jnp.where(offmask, lows[i], 0.0)
            xh, xl = split(x)
            xoh, xol = split(xo)
            y = dot3s(xoh, xol, *split(off))
            z = xo - dot3s(*split(y), xh, xl)
            rows = []
            for b in range(64 // m):
                rows.append(x[m * 2 * b:m * (2 * b + 1), :])
                rows.append(z[m * b:m * (b + 1), :])
            out.append(jnp.concatenate(rows, 0))
        fulls = out
        m *= 2
    return fulls

MESH = pl.DeviceIdType.MESH
HEADS = 16
NX, NL, NG, NY = 4, 4, 4, 4
PAIR, ROW, LOW, HIGH, YS, HIGH_BACK, LOW_BACK, ROW_BACK, BACK, GAIN, GAIN_ROW, SEMS = (
    0, 8, 16, 24, 32, 40, 48, 56, 64, 72, 73, 77,
)


def local_maps(keys, values, queries, betas):
    r2 = lax.broadcasted_iota(jnp.int32, (128, 128), 0)
    c2 = lax.broadcasted_iota(jnp.int32, (128, 128), 1)
    vis = lax.broadcasted_iota(jnp.int32, (T, N), 1) <= 2 * lax.broadcasted_iota(jnp.int32, (T, N), 0) + 1
    eye = jnp.where(r2 == c2, 1.0, 0.0).astype(f32)
    lows, rest = [], []
    for k, v, beta in zip(keys, values, betas):
        kf = k.astype(f32)
        ssq = jnp.sum(kf * kf, axis=1, keepdims=True) + 1e-6
        p = beta / ssq
        bs = beta * lax.rsqrt(ssq)
        gram = mm_nt(k, k)
        l11 = jnp.where(r2 > c2, p[:128] * gram[:128, :128], 0.0)
        l22 = jnp.where(r2 > c2, p[128:] * gram[128:, 128:], 0.0)
        l21 = p[128:] * gram[128:, :128]
        rhs = jnp.concatenate([p * kf, bs * v.astype(f32)], axis=1)
        lows += [l11, l22]
        rest.append((l21, rhs))
    invs = unit_lower_inverses(lows)
    maps, outs = [], []
    for h, (k, q) in enumerate(zip(keys, queries)):
        l21, rhs = rest[h]
        t1, t2 = invs[2 * h], invs[2 * h + 1]
        y1 = dot3(t1, rhs[:128])
        y2 = dot3(t2, rhs[128:] - dot3(l21, y1))
        yh, yl = split(jnp.concatenate([y1, y2], 0))
        ky = mm_tn(k, yh) + mm_tn(k, yl)
        maps.append((eye - ky[:, :128], ky[:, 128:]))
        s = jnp.where(vis, mm_nt(q, k), 0.0)
        sh, sl = split(s)
        sy = dot3s(sh, sl, yh, yl)
        outs.append((q.astype(f32) - sy[:, :128], sy[:, 128:]))
    return maps, outs


def compose(late, early):
    joined = dot3(late[:, :D], early)
    return jnp.concatenate([joined[:, :D], joined[:, D:] + late[:, D:]], axis=1)


def advance(pair, state):
    return dot3(pair[:, :D], state) + pair[:, D:]


def states_kernel(
    k_ref, v_ref, q_ref, b_ref, gain_ref, qo_ref, m_ref, gains_ref,
    outbox, both, chip, row_in, row_pre, row_tot, low_in, low_pre, low_tot,
    high_in, high_pre, high_tot, y_in, y_state, high_out, high_state, low_out, low_state,
    row_out, chip_state, after, send, recv,
):
    seq, head = lax.axis_index("seq"), lax.axis_index("head")
    x, c = head // 2, head % 2
    y, g, l = seq // (NG * NL), (seq // NL) % NG, seq % NL
    oc = 1 - c

    def device(xx=None, cc=None, yy=None, gg=None, ll=None):
        xx, cc = x if xx is None else xx, c if cc is None else cc
        yy, gg, ll = y if yy is None else yy, g if gg is None else gg, l if ll is None else ll
        return {"seq": (yy * NG + gg) * NL + ll, "head": xx * 2 + cc}

    partner = device(cc=oc)

    def remote(src, dst, s, r, where):
        return pltpu.make_async_remote_copy(
            src_ref=src, dst_ref=dst, send_sem=send.at[s], recv_sem=recv.at[r],
            device_id=where, device_id_type=MESH,
        )

    peers = [partner]
    peers += [device(xx=(x + k) % NX) for k in (1, 2, 3)]
    peers += [device(ll=(l + k) % NL) for k in (1, 2, 3)]
    peers += [device(gg=(g + k) % NG) for k in (1, 2, 3)]
    peers += [device(yy=(y + k) % NY) for k in (1, 2, 3)]
    barrier = pltpu.get_barrier_semaphore()
    for peer in peers:
        pl.semaphore_signal(barrier, inc=1, device_id=peer, device_id_type=MESH)
    gains_ref[head] = gain_ref[...]
    pl.semaphore_wait(barrier, len(peers))

    def gain_copy():
        return remote(gain_ref, gains_ref.at[head], GAIN, GAIN, partner)

    def gain_row_copy(k, there, origin):
        rows = gains_ref.at[pl.ds(2 * origin, 2)]
        return remote(rows, rows, GAIN_ROW + k, GAIN_ROW + origin, device(xx=there))

    gain_copy().start()

    def pair_copy(i):
        return remote(outbox.at[i], both.at[c, i], PAIR + i, PAIR + i, partner)

    def pair_wait(i):
        remote(outbox.at[i], both.at[oc, i], PAIR + i, PAIR + i, partner).wait_recv()

    def row_copy(e, k, there, origin):
        return remote(
            chip.at[2 * there + e], row_in.at[e, origin], ROW + 4 * e + k, ROW + 4 * e + origin, device(xx=there)
        )

    def low_copy(e, there, origin):
        return remote(row_tot.at[e], low_in.at[e, origin], LOW + 4 * e, LOW + 4 * e + origin, device(ll=there))

    def high_copy(e, there, origin):
        return remote(low_tot.at[e], high_in.at[e, origin], HIGH + 4 * e, HIGH + 4 * e + origin, device(gg=there))

    def y_copy(e, k, there, origin):
        return remote(high_tot.at[e], y_in.at[e, origin], YS + 4 * e + k, YS + 4 * e + origin, device(yy=there))

    def high_back(e, there):
        return remote(
            high_out.at[e, there], high_state.at[e], HIGH_BACK + 4 * e + there, HIGH_BACK + 4 * e, device(gg=there)
        )

    def low_back(e, there):
        return remote(
            low_out.at[e, there], low_state.at[e], LOW_BACK + 4 * e + there, LOW_BACK + 4 * e, device(ll=there)
        )

    def row_back(e, k, there, origin):
        return remote(
            row_out.at[e, there], chip_state.at[2 * origin + e], ROW_BACK + 4 * e + k, ROW_BACK + 4 * e + origin,
            device(xx=there),
        )

    def back_copy(i):
        return remote(after.at[i], m_ref.at[8 * c + i], BACK + i, BACK + i, partner)

    def back_wait(i):
        remote(after.at[i], m_ref.at[8 * oc + i], BACK + i, BACK + i, partner).wait_recv()

    def joint(parts, e, pre, tot):
        first = compose(parts[e, 1], parts[e, 0])
        last = compose(parts[e, 3], parts[e, 2])
        tot[e] = compose(last, first)
        pre[e, 0] = first

    def third(parts, e, pre):
        pre[e, 1] = compose(parts[e, 2], pre[e, 0])

    def prefix(parts, pre, e, place):
        return parts[e, 0] if place == 1 else pre[e, place - 2]

    def join_chip(it):
        e, s = it // 4, it % 4
        there = (x + 1 + s) % NX
        i = 2 * there + e
        pair_wait(i)
        joined = compose(both[1, i], both[0, i])

        @pl.when(s < 3)
        def _():
            chip[i] = joined
            row_copy(e, 1 + s, there, x).start()

        @pl.when(s == 3)
        def _():
            row_in[e, x] = joined

    def up_row(e):
        own = 2 * e + c
        for k in (1, 2, 3):
            origin = (x + k) % NX
            row_copy(e, 0, origin, origin).wait_recv()
        joint(row_in, e, row_pre, row_tot)

        @pl.when(l != own)
        def _():
            low_copy(e, own, l).start()

        @pl.when(l == own)
        def _():
            low_in[e, l] = row_tot[e]

        third(row_in, e, row_pre)

    def up_low(e):
        own = 2 * e + c

        @pl.when(l == own)
        def _():
            for k in (1, 2, 3):
                origin = (l + k) % NL
                low_copy(e, origin, origin).wait_recv()
            joint(low_in, e, low_pre, low_tot)

            @pl.when(g != own)
            def _():
                high_copy(e, own, g).start()

            @pl.when(g == own)
            def _():
                high_in[e, g] = low_tot[e]

            third(low_in, e, low_pre)

    def up_high(e):
        own = 2 * e + c

        @pl.when((l == own) & (g == own))
        def _():
            for k in (1, 2, 3):
                origin = (g + k) % NG
                high_copy(e, origin, origin).wait_recv()
            joint(high_in, e, high_pre, high_tot)
            for k in (1, 2, 3):
                @pl.when(y + k < NY)
                def _():
                    y_copy(e, k, (y + k) % NY, y).start()
            third(high_in, e, high_pre)

    def down_high(e):
        own = 2 * e + c

        @pl.when((l == own) & (g == own))
        def _():
            y_state[e] = jnp.zeros((D, D), f32)
            for s in (0, 1, 2):
                @pl.when(y > s)
                def _():
                    y_copy(e, 0, s, s).wait_recv()
                    y_state[e] = advance(y_in[e, s], y_state[e])
            start = y_state[e]
            for place in range(NG):
                high_out[e, place] = start if place == 0 else advance(prefix(high_in, high_pre, e, place), start)

                @pl.when(g != place)
                def _():
                    high_back(e, place).start()

                @pl.when(g == place)
                def _():
                    high_state[e] = high_out[e, place]

    def down_low(e):
        own = 2 * e + c

        @pl.when(l == own)
        def _():
            @pl.when(g != own)
            def _():
                high_back(e, own).wait_recv()
            start = high_state[e]
            for place in range(NL):
                low_out[e, place] = start if place == 0 else advance(prefix(low_in, low_pre, e, place), start)

                @pl.when(l != place)
                def _():
                    low_back(e, place).start()

                @pl.when(l == place)
                def _():
                    low_state[e] = low_out[e, place]

    def down_row(e):
        own = 2 * e + c

        @pl.when(l != own)
        def _():
            low_back(e, own).wait_recv()
        start = low_state[e]
        for place in range(NX):
            row_out[e, place] = start if place == 0 else advance(prefix(row_in, row_pre, e, place), start)
        for k in (2, 1, 3):
            row_back(e, k, (x + k) % NX, x).start()
        chip_state[2 * x + e] = row_out[e, x]

    def down_chip(e):
        for k in (0, 1, 3, 2):
            origin = (x + k) % NX
            if k:
                row_back(e, 0, origin, origin).wait_recv()
            i = 2 * origin + e
            begin = chip_state[i]
            end = advance(both[0, i], begin)

            @pl.when(c == 0)
            def _():
                m_ref[i] = begin
                after[i] = end

            @pl.when(c == 1)
            def _():
                m_ref[8 + i] = end
                after[i] = begin

            back_copy(i).start()

    lane = lax.broadcasted_iota(jnp.int32, (N, HEADS), 1)

    def turn(it, carry):
        e, s = it // 4, it % 4
        i = 2 * ((x + 1 + s) % NX) + e
        here = (8 * oc + i, 8 * c + i)
        betas = [jnp.sum(jnp.where(lane == h, b_ref[...], 0.0), axis=1, keepdims=True) for h in here]
        maps, outs = local_maps(
            [k_ref[h] for h in here], [v_ref[h] for h in here], [q_ref[h] for h in here], betas
        )
        outbox[i, :, :D], outbox[i, :, D:] = maps[0]
        pair_copy(i).start()
        both[c, i, :, :D], both[c, i, :, D:] = maps[1]
        for h, (q_part, o_part) in zip(here, outs):
            qo_ref[h, :, :D] = q_part
            qo_ref[h, :, D:] = o_part

        @pl.when(it > 0)
        def _():
            join_chip(it - 1)

        @pl.when(it == 4)
        def _():
            up_row(0)

        @pl.when(it == 5)
        def _():
            up_low(0)

        @pl.when(it == 6)
        def _():
            up_high(0)

        @pl.when(it == 7)
        def _():
            down_high(0)

        return carry

    lax.fori_loop(0, 8, turn, 0)
    join_chip(7)
    remote(gain_ref, gains_ref.at[2 * x + oc], GAIN, GAIN, partner).wait_recv()
    for k in (1, 2, 3):
        gain_row_copy(k, (x + k) % NX, x).start()
    up_row(1)
    down_low(0)
    up_low(1)
    down_row(0)
    up_high(1)
    down_chip(0)
    down_high(1)
    down_low(1)
    down_row(1)
    down_chip(1)
    for i in range(8):
        back_wait(i)
    for k in (1, 2, 3):
        origin = (x + k) % NX
        gain_row_copy(k, origin, origin).wait_recv()

    gain_copy().wait_send()
    for k in (1, 2, 3):
        gain_row_copy(k, (x + k) % NX, x).wait_send()
    for i in range(8):
        pair_copy(i).wait_send()
        back_copy(i).wait_send()
    for e in range(2):
        own = 2 * e + c
        for k in (1, 2, 3):
            row_copy(e, k, (x + k) % NX, x).wait_send()
            row_back(e, k, (x + k) % NX, x).wait_send()

        @pl.when(l != own)
        def _():
            low_copy(e, own, l).wait_send()

        @pl.when(l == own)
        def _():
            @pl.when(g != own)
            def _():
                high_copy(e, own, g).wait_send()

            for place in range(NL):
                @pl.when(l != place)
                def _():
                    low_back(e, place).wait_send()

            @pl.when(g == own)
            def _():
                for k in (1, 2, 3):
                    @pl.when(y + k < NY)
                    def _():
                        y_copy(e, k, (y + k) % NY, y).wait_send()
                for place in range(NG):
                    @pl.when(g != place)
                    def _():
                        high_back(e, place).wait_send()


def states(keys, values, queries, betas, gain):
    wide, square = (D, 2 * D), (D, D)
    whole = pl.BlockSpec(memory_space=pltpu.VMEM)

    def vm(*shape):
        return pltpu.VMEM(shape, f32)

    return pl.pallas_call(
        states_kernel,
        in_specs=[whole] * 5,
        out_specs=[whole] * 3,
        out_shape=[
            jax.ShapeDtypeStruct((HEADS, T, 2 * D), f32),
            jax.ShapeDtypeStruct((HEADS, D, D), f32),
            jax.ShapeDtypeStruct((8, 8, D), f32),
        ],
        scratch_shapes=[
            vm(8, *wide), vm(2, 8, *wide), vm(8, *wide),
            vm(2, NX, *wide), vm(2, 2, *wide), vm(2, *wide),
            vm(2, NL, *wide), vm(2, 2, *wide), vm(2, *wide),
            vm(2, NG, *wide), vm(2, 2, *wide), vm(2, *wide),
            vm(2, NY, *wide), vm(2, *square),
            vm(2, NG, *square), vm(2, *square), vm(2, NL, *square), vm(2, *square),
            vm(2, NX, *square), vm(8, *square), vm(8, *square),
            pltpu.SemaphoreType.DMA((SEMS,)), pltpu.SemaphoreType.DMA((SEMS,)),
        ],
        compiler_params=pltpu.CompilerParams(
            collective_id=0, has_side_effects=True, vmem_limit_bytes=48 * 2**20
        ),
    )(keys, values, queries, betas, gain)


def output_kernel(qo_ref, m_ref, gains_ref, gate_ref, out_ref, rows):
    for h in range(HEADS):
        r = dot3(qo_ref[h, :, :D], m_ref[h]) + qo_ref[h, :, D:]
        scale = lax.rsqrt(jnp.mean(r * r, axis=-1, keepdims=True) + 1e-6)
        rows[h] = r * scale * gains_ref[h // 2, h % 2 : h % 2 + 1, :]
    gate = gate_ref[...].astype(f32)
    normed = jnp.swapaxes(rows[...], 0, 1)
    out_ref[...] = (normed * (gate / (1.0 + jnp.exp(-gate)))).astype(bf16)


def outputs(qo, m, gains, gate):
    whole = pl.BlockSpec(memory_space=pltpu.VMEM)
    return pl.pallas_call(
        output_kernel,
        in_specs=[whole] * 4,
        out_specs=whole,
        out_shape=jax.ShapeDtypeStruct((T, HEADS, D), bf16),
        scratch_shapes=[pltpu.VMEM((HEADS, T, D), f32)],
        compiler_params=pltpu.CompilerParams(vmem_limit_bytes=48 * 2**20),
    )(qo, m, gains, gate)


def local(queries, keys, values, betas, gate, gain):
    keys_h = jnp.transpose(keys, (1, 0, 2, 3)).reshape(HEADS, N, D)
    values_h = jnp.transpose(values, (1, 0, 2, 3)).reshape(HEADS, N, D)
    queries_h = jnp.transpose(queries, (1, 0, 2))
    betas_h = jnp.transpose(betas, (0, 2, 1)).reshape(N, HEADS).astype(f32)
    qo, m, gains = states(keys_h, values_h, queries_h, betas_h, jnp.pad(gain, ((0, 6), (0, 0))))
    return outputs(qo, m, gains, gate)


def solution(mesh):
    return jax.shard_map(
        local,
        mesh=mesh,
        in_specs=(
            P(("seq", "head"), None, None),
            P(("seq", "head"), None, None, None),
            P(("seq", "head"), None, None, None),
            P(("seq", "head"), None, None),
            P(("seq", "head"), None, None),
            P("head", None),
        ),
        out_specs=P(("seq", "head"), None, None),
        check_vma=False,
    )
```

```python
import functools
import jax, jax.numpy as jnp
from jax import lax
from jax.experimental import pallas as pl
from jax.experimental.pallas import tpu as pltpu
from jax.sharding import PartitionSpec as P
f32, bf16 = jnp.float32, jnp.bfloat16
D = 128
N = 256
T = 128
BASE = 16

def split(a):
    hi = a.astype(bf16)
    return hi, (a - hi.astype(f32)).astype(bf16)

def mm(a, b):
    return lax.dot_general(a, b, (((1,), (0,)), ((), ())), preferred_element_type=f32)

def mm_nt(a, b):
    return lax.dot_general(a, b, (((1,), (1,)), ((), ())), preferred_element_type=f32)

def mm_tn(a, b):
    return lax.dot_general(a, b, (((0,), (0,)), ((), ())), preferred_element_type=f32)

def dot3(a, b):
    ah, al = split(a)
    bh, bl = split(b)
    return dot3s(ah, al, bh, bl)

def dot3s(ah, al, bh, bl):
    if ah.shape[1] == 128:
        return mm(jnp.concatenate([ah, al], 1), jnp.concatenate([bh, bh], 0)) + mm(ah, bl)
    return mm(ah, bh) + (mm(al, bh) + mm(ah, bl))

def unit_lower_inverses(lows):
    n = len(lows)
    lane = lax.broadcasted_iota(jnp.int32, (BASE, 128), 1)
    row = lax.broadcasted_iota(jnp.int32, (BASE, 128), 0)
    blk = lane // BASE
    packed = []
    for low in lows:
        z = jnp.zeros((BASE, 128), f32)
        for b in range(128 // BASE):
            z = jnp.where(blk == b, low[BASE * b:BASE * (b + 1), :], z)
        packed.append(jnp.where(row > lane % BASE, z, 0.0))
    eye = jnp.where(row == lane % BASE, 1.0, 0.0).astype(f32)
    xs = [eye for _ in lows]
    for j in range(BASE - 1):
        idx = blk * BASE + j
        for i in range(n):
            lj = jnp.take_along_axis(packed[i], idx, axis=1, mode="promise_in_bounds")
            xs[i] = xs[i] - lj * xs[i][j:j + 1, :]
    fulls = []
    for x in xs:
        fulls.append(jnp.concatenate([jnp.where(blk == b, x, 0.0) for b in range(128 // BASE)], axis=0))
    m = BASE
    r2 = lax.broadcasted_iota(jnp.int32, (128, 128), 0)
    c2 = lax.broadcasted_iota(jnp.int32, (128, 128), 1)
    while m < 128:
        offmask = ((r2 // m) % 2 == 1) & (c2 // m == r2 // m - 1)
        xos = [jnp.concatenate([x[m * (2 * b + 1):m * (2 * b + 2), :] for b in range(64 // m)], 0) for x in fulls]
        offs = [split(jnp.where(offmask, low, 0.0)) for low in lows]
        xos_s = [split(xo) for xo in xos]
        xs_s = [split(x) for x in fulls]
        ys = [dot3s(*xo, *off) for xo, off in zip(xos_s, offs)]
        ys = [split(y) for y in ys]
        zs = [xo - dot3s(*y, *x) for xo, y, x in zip(xos, ys, xs_s)]
        out = []
        for x, z in zip(fulls, zs):
            rows = []
            for b in range(64 // m):
                rows.append(x[m * 2 * b:m * (2 * b + 1), :])
                rows.append(z[m * b:m * (b + 1), :])
            out.append(jnp.concatenate(rows, 0))
        fulls = out
        m *= 2
    return fulls

MESH = pl.DeviceIdType.MESH
HEADS = 16
NX, NL, NG, NY = 4, 4, 4, 4
PAIR, ROW, LOW, HIGH, YS, LOW_BACK, ROW_BACK, BACK, GAIN, GAIN_ROW, SEMS = 0, 8, 16, 24, 32, 40, 48, 56, 64, 65, 69


def local_solves(keys, values, betas):
    hs = range(len(keys))
    r2 = lax.broadcasted_iota(jnp.int32, (128, 128), 0)
    c2 = lax.broadcasted_iota(jnp.int32, (128, 128), 1)
    eye = jnp.where(r2 == c2, 1.0, 0.0).astype(f32)
    lows, crosses, rights = [], [], []
    for k, v, beta in zip(keys, values, betas):
        kf = k.astype(f32)
        ssq = jnp.sum(kf * kf, axis=1, keepdims=True) + 1e-6
        p = beta / ssq
        bs = beta * lax.rsqrt(ssq)
        gram = mm_nt(k, k)
        lows.append(jnp.where(r2 > c2, p[:128] * gram[:128, :128], 0.0))
        lows.append(jnp.where(r2 > c2, p[128:] * gram[128:, 128:], 0.0))
        crosses.append(p[128:] * gram[128:, :128])
        rights.append(jnp.concatenate([p * kf, bs * v.astype(f32)], axis=1))
    invs = unit_lower_inverses(lows)
    y1 = [dot3(invs[2 * h], rights[h][:128]) for h in hs]
    rest = [rights[h][128:] - dot3(crosses[h], y1[h]) for h in hs]
    y2 = [dot3(invs[2 * h + 1], rest[h]) for h in hs]
    ys = [split(jnp.concatenate([y1[h], y2[h]], 0)) for h in hs]
    kys = [mm_tn(keys[h], ys[h][0]) + mm_tn(keys[h], ys[h][1]) for h in hs]
    return ys, [(eye - ky[:, :D], ky[:, D:]) for ky in kys]


def local_outputs(queries, keys, ys):
    vis = lax.broadcasted_iota(jnp.int32, (T, N), 1) <= 2 * lax.broadcasted_iota(jnp.int32, (T, N), 0) + 1
    scores = [split(jnp.where(vis, mm_nt(q, k), 0.0)) for q, k in zip(queries, keys)]
    sys_ = [dot3s(*s, *y) for s, y in zip(scores, ys)]
    return [(q.astype(f32) - sy[:, :D], sy[:, D:]) for q, sy in zip(queries, sys_)]


def compose(late, early):
    joined = dot3(late[:, :D], early)
    return jnp.concatenate([joined[:, :D], joined[:, D:] + late[:, D:]], axis=1)


def advance(pair, state):
    return dot3(pair[:, :D], state) + pair[:, D:]


def states_kernel(
    k_ref, v_ref, q_ref, b_ref, gain_ref, qo_ref, m_ref, gains_ref,
    pool, chip, row_in, row_pre, row_tot, low_in, low_pre, low_tot,
    high_in, high_pre, high_tot, y_in, start, low_out, low_state,
    row_out, chip_state, after, send, recv,
):
    seq, head = lax.axis_index("seq"), lax.axis_index("head")
    x, c = head // 2, head % 2
    y, g, l = seq // (NG * NL), (seq // NL) % NG, seq % NL
    oc = 1 - c

    def meet(gg):
        return 2 - c + (((gg + 1) // 2) % 2) * (2 * c - 1)

    hub = meet(g)
    is_hub = l == hub

    def device(xx=None, cc=None, yy=None, gg=None, ll=None):
        xx, cc = x if xx is None else xx, c if cc is None else cc
        yy, gg, ll = y if yy is None else yy, g if gg is None else gg, l if ll is None else ll
        return {"seq": (yy * NG + gg) * NL + ll, "head": xx * 2 + cc}

    partner = device(cc=oc)

    def remote(src, dst, s, r, where):
        return pltpu.make_async_remote_copy(
            src_ref=src, dst_ref=dst, send_sem=send.at[s], recv_sem=recv.at[r],
            device_id=where, device_id_type=MESH,
        )

    barrier = pltpu.get_barrier_semaphore()

    def greet(peers):
        for peer in peers:
            pl.semaphore_signal(barrier, inc=1, device_id=peer, device_id_type=MESH)

    greet([partner] + [device(xx=(x + k) % NX) for k in (1, 2, 3)])

    @pl.when(is_hub)
    def _():
        greet([device(ll=(l + k) % NL) for k in (1, 2, 3)])
        greet([device(gg=(g + k) % NG, ll=meet((g + k) % NG)) for k in (1, 2, 3)])
        greet([device(yy=(y + k) % NY) for k in (1, 2, 3)])

    @pl.when(l != hub)
    def _():
        greet([device(ll=hub)])

    gains_ref[head] = gain_ref[...]

    @pl.when(is_hub)
    def _():
        pl.semaphore_wait(barrier, 13)

    @pl.when(l != hub)
    def _():
        pl.semaphore_wait(barrier, 5)

    def gain_copy():
        return remote(gain_ref, gains_ref.at[head], GAIN, GAIN, partner)

    def gain_row_copy(k, there, origin):
        rows = gains_ref.at[pl.ds(2 * origin, 2)]
        return remote(rows, rows, GAIN_ROW + k, GAIN_ROW + origin, device(xx=there))

    def pair_copy(i):
        return remote(pool.at[oc, i], pool.at[2, i], PAIR + i, PAIR + i, partner)

    def row_copy(e, k, there, origin):
        return remote(
            chip.at[2 * there + e], row_in.at[e, origin], ROW + 4 * e + k, ROW + 4 * e + origin, device(xx=there)
        )

    def low_copy(e, there, origin):
        return remote(row_tot.at[e], low_in.at[e, origin], LOW + 4 * e, LOW + 4 * e + origin, device(ll=there))

    def high_copy(e, k, there, origin):
        return remote(
            low_tot.at[e], high_in.at[e, origin], HIGH + 4 * e + k, HIGH + 4 * e + origin,
            device(gg=there, ll=meet(there)),
        )

    def y_copy(e, k, there, origin):
        return remote(high_tot.at[e], y_in.at[e, origin], YS + 4 * e + k, YS + 4 * e + origin, device(yy=there))

    def low_back(e, there):
        return remote(
            low_out.at[e, there], low_state.at[e], LOW_BACK + 4 * e + there, LOW_BACK + 4 * e, device(ll=there)
        )

    def row_back(e, k, there, origin):
        return remote(
            row_out.at[e, there], chip_state.at[2 * origin + e], ROW_BACK + 4 * e + k, ROW_BACK + 4 * e + origin,
            device(xx=there),
        )

    def back_copy(src, i):
        return remote(src.at[i], m_ref.at[8 * c + i], BACK + i, BACK + i, partner)

    def joint(parts, e, pre, tot):
        first = compose(parts[e, 1], parts[e, 0])
        last = compose(parts[e, 3], parts[e, 2])
        tot[e] = compose(last, first)
        pre[e, 0] = parts[e, 0]
        pre[e, 1] = first

    def third(parts, e, pre):
        pre[e, 2] = compose(parts[e, 2], pre[e, 1])

    def join_chip(e):
        for k in (2, 1, 3, 0):
            there = (x + k) % NX
            i = 2 * there + e
            pair_copy(i).wait_recv()
            joined = compose(pool[2 - c, i], pool[2 * c, i])
            if k:
                chip[i] = joined
                row_copy(e, k, there, x).start()
            else:
                row_in[e, x] = joined

    def up_row(e):
        for k in (1, 2, 3):
            origin = (x + k) % NX
            row_copy(e, 0, origin, origin).wait_recv()
        joint(row_in, e, row_pre, row_tot)

        @pl.when(l != hub)
        def _():
            low_copy(e, hub, l).start()

        @pl.when(is_hub)
        def _():
            low_in[e, l] = row_tot[e]

        third(row_in, e, row_pre)

    def up_low(e):
        @pl.when(is_hub)
        def _():
            for k in (1, 2, 3):
                origin = (l + k) % NL
                low_copy(e, origin, origin).wait_recv()
            joint(low_in, e, low_pre, low_tot)
            for k in (2, 1, 3):
                high_copy(e, k, (g + k) % NG, g).start()
            high_in[e, g] = low_tot[e]
            third(low_in, e, low_pre)

    def up_high(e):
        @pl.when(is_hub)
        def _():
            for k in (1, 2, 3):
                origin = (g + k) % NG
                high_copy(e, k, origin, origin).wait_recv()
            joint(high_in, e, high_pre, high_tot)
            for k in (2, 1, 3):
                @pl.when(y + k < NY)
                def _():
                    y_copy(e, k, (y + k) % NY, y).start()
            third(high_in, e, high_pre)

    def down_high(e):
        @pl.when(is_hub)
        def _():
            start[e] = jnp.zeros((D, D), f32)
            for s in (0, 1, 2):
                @pl.when(y > s)
                def _():
                    y_copy(e, 0, s, s).wait_recv()
                    start[e] = advance(y_in[e, s], start[e])

            @pl.when(g > 0)
            def _():
                start[e] = advance(high_pre[e, g - 1], start[e])

            begin = start[e]
            for place in range(NL):
                low_out[e, place] = begin if place == 0 else advance(low_pre[e, place - 1], begin)

                @pl.when(l != place)
                def _():
                    low_back(e, place).start()

                @pl.when(l == place)
                def _():
                    low_state[e] = low_out[e, place]

    def down_row(e):
        @pl.when(l != hub)
        def _():
            low_back(e, hub).wait_recv()
        begin = low_state[e]
        for place in range(NX):
            row_out[e, place] = begin if place == 0 else advance(row_pre[e, place - 1], begin)
        for k in (2, 1, 3):
            row_back(e, k, (x + k) % NX, x).start()
        chip_state[2 * x + e] = row_out[e, x]

    def down_chip(e):
        for k in (0, 1, 3, 2):
            origin = (x + k) % NX
            i = 2 * origin + e
            if k:
                row_back(e, 0, origin, origin).wait_recv()

            @pl.when(c == 1)
            def _():
                back_copy(chip_state, i).start()

            begin = chip_state[i]
            end = advance(pool[2 * c, i], begin)

            @pl.when(c == 0)
            def _():
                after[i] = end
                back_copy(after, i).start()
                m_ref[i] = begin

            @pl.when(c == 1)
            def _():
                m_ref[8 + i] = end

    gain_copy().start()
    lane = lax.broadcasted_iota(jnp.int32, (N, HEADS), 1)

    def turn(t, carry):
        e, half = t // 2, t % 2
        here = [2 * v + e for v in range(NX)]
        betas = [
            jnp.sum(jnp.where(lane == 8 * half + i, b_ref[...], 0.0), axis=1, keepdims=True) for i in here
        ]
        keys = [k_ref[8 * half + i] for i in here]
        ys, maps = local_solves(keys, [v_ref[8 * half + i] for i in here], betas)
        for i, (a_part, b_part) in zip(here, maps):
            pool[half, i, :, :D] = a_part
            pool[half, i, :, D:] = b_part

        @pl.when(half != c)
        def _():
            for i in here:
                pair_copy(i).start()

        outs = local_outputs([q_ref[8 * half + i] for i in here], keys, ys)
        for i, (q_part, o_part) in zip(here, outs):
            qo_ref[8 * half + i, :, :D] = q_part
            qo_ref[8 * half + i, :, D:] = o_part

        @pl.when(t == 1 + c)
        def _():
            join_chip(0)

        @pl.when((t == 2) & (c == 0))
        def _():
            up_row(0)

        return carry

    lax.fori_loop(0, 4, turn, 0)

    def on_core(which, step):
        @pl.when(c == which)
        def _():
            step()

    on_core(1, lambda: up_row(0))
    join_chip(1)
    remote(gain_ref, gains_ref.at[2 * x + oc], GAIN, GAIN, partner).wait_recv()
    for k in (1, 2, 3):
        gain_row_copy(k, (x + k) % NX, x).start()
    on_core(0, lambda: up_low(0))
    up_row(1)
    on_core(1, lambda: up_low(0))
    on_core(0, lambda: up_high(0))
    up_low(1)
    on_core(1, lambda: up_high(0))
    down_high(0)
    up_high(1)
    down_row(0)
    on_core(0, lambda: down_chip(0))
    down_high(1)
    on_core(1, lambda: down_chip(0))
    down_row(1)
    down_chip(1)
    for i in range(8):
        remote(after.at[i], m_ref.at[8 * oc + i], BACK + i, BACK + i, partner).wait_recv()
    for k in (1, 2, 3):
        origin = (x + k) % NX
        gain_row_copy(k, origin, origin).wait_recv()

    gain_copy().wait_send()
    for k in (1, 2, 3):
        gain_row_copy(k, (x + k) % NX, x).wait_send()
    for i in range(8):
        pair_copy(i).wait_send()
        back_copy(after, i).wait_send()
    for e in range(2):
        for k in (1, 2, 3):
            row_copy(e, k, (x + k) % NX, x).wait_send()
            row_back(e, k, (x + k) % NX, x).wait_send()

        @pl.when(l != hub)
        def _():
            low_copy(e, hub, l).wait_send()

        @pl.when(is_hub)
        def _():
            for place in range(NL):
                @pl.when(l != place)
                def _():
                    low_back(e, place).wait_send()
            for k in (1, 2, 3):
                high_copy(e, k, (g + k) % NG, g).wait_send()

                @pl.when(y + k < NY)
                def _():
                    y_copy(e, k, (y + k) % NY, y).wait_send()


def states(keys, values, queries, betas, gain):
    wide, square = (D, 2 * D), (D, D)
    whole = pl.BlockSpec(memory_space=pltpu.VMEM)

    def vm(*shape):
        return pltpu.VMEM(shape, f32)

    return pl.pallas_call(
        states_kernel,
        in_specs=[whole] * 5,
        out_specs=[whole] * 3,
        out_shape=[
            jax.ShapeDtypeStruct((HEADS, T, 2 * D), f32),
            jax.ShapeDtypeStruct((HEADS, D, D), f32),
            jax.ShapeDtypeStruct((8, 8, D), f32),
        ],
        scratch_shapes=[
            vm(3, 8, *wide), vm(8, *wide),
            vm(2, NX, *wide), vm(2, 3, *wide), vm(2, *wide),
            vm(2, NL, *wide), vm(2, 3, *wide), vm(2, *wide),
            vm(2, NG, *wide), vm(2, 3, *wide), vm(2, *wide),
            vm(2, NY, *wide), vm(2, *square), vm(2, NL, *square), vm(2, *square),
            vm(2, NX, *square), vm(8, *square), vm(8, *square),
            pltpu.SemaphoreType.DMA((SEMS,)), pltpu.SemaphoreType.DMA((SEMS,)),
        ],
        compiler_params=pltpu.CompilerParams(
            collective_id=0, has_side_effects=True, vmem_limit_bytes=48 * 2**20
        ),
    )(keys, values, queries, betas, gain)


def output_kernel(qo_ref, m_ref, gains_ref, gate_ref, out_ref, rows):
    for h in range(HEADS):
        r = dot3(qo_ref[h, :, :D], m_ref[h]) + qo_ref[h, :, D:]
        scale = lax.rsqrt(jnp.mean(r * r, axis=-1, keepdims=True) + 1e-6)
        rows[h] = r * scale * gains_ref[h // 2, h % 2 : h % 2 + 1, :]
    gate = gate_ref[...].astype(f32)
    normed = jnp.swapaxes(rows[...], 0, 1)
    out_ref[...] = (normed * (gate / (1.0 + jnp.exp(-gate)))).astype(bf16)


def outputs(qo, m, gains, gate):
    whole = pl.BlockSpec(memory_space=pltpu.VMEM)
    return pl.pallas_call(
        output_kernel,
        in_specs=[whole] * 4,
        out_specs=whole,
        out_shape=jax.ShapeDtypeStruct((T, HEADS, D), bf16),
        scratch_shapes=[pltpu.VMEM((HEADS, T, D), f32)],
        compiler_params=pltpu.CompilerParams(vmem_limit_bytes=48 * 2**20),
    )(qo, m, gains, gate)


def local(queries, keys, values, betas, gate, gain):
    keys_h = jnp.transpose(keys, (1, 0, 2, 3)).reshape(HEADS, N, D)
    values_h = jnp.transpose(values, (1, 0, 2, 3)).reshape(HEADS, N, D)
    queries_h = jnp.transpose(queries, (1, 0, 2))
    betas_h = jnp.transpose(betas, (0, 2, 1)).reshape(N, HEADS).astype(f32)
    qo, m, gains = states(keys_h, values_h, queries_h, betas_h, jnp.pad(gain, ((0, 6), (0, 0))))
    return outputs(qo, m, gains, gate)


def solution(mesh):
    return jax.shard_map(
        local,
        mesh=mesh,
        in_specs=(
            P(("seq", "head"), None, None),
            P(("seq", "head"), None, None, None),
            P(("seq", "head"), None, None, None),
            P(("seq", "head"), None, None),
            P(("seq", "head"), None, None),
            P("head", None),
        ),
        out_specs=P(("seq", "head"), None, None),
        check_vma=False,
    )
```

```python
import functools
import jax, jax.numpy as jnp
from jax import lax
from jax.experimental import pallas as pl
from jax.experimental.pallas import tpu as pltpu
from jax.sharding import PartitionSpec as P
f32, bf16 = jnp.float32, jnp.bfloat16
D = 128
N = 256
T = 128
BASE = 16

def split(a):
    hi = a.astype(bf16)
    return hi, (a - hi.astype(f32)).astype(bf16)

def mm(a, b):
    return lax.dot_general(a, b, (((1,), (0,)), ((), ())), preferred_element_type=f32)

def mm_nt(a, b):
    return lax.dot_general(a, b, (((1,), (1,)), ((), ())), preferred_element_type=f32)

def mm_tn(a, b):
    return lax.dot_general(a, b, (((0,), (0,)), ((), ())), preferred_element_type=f32)

def dot3(a, b):
    ah, al = split(a)
    bh, bl = split(b)
    return dot3s(ah, al, bh, bl)

def dot3s(ah, al, bh, bl):
    if ah.shape[1] == 128:
        return mm(jnp.concatenate([ah, al], 1), jnp.concatenate([bh, bh], 0)) + mm(ah, bl)
    return mm(ah, bh) + (mm(al, bh) + mm(ah, bl))

def unit_lower_inverses(lows):
    n = len(lows)
    lane = lax.broadcasted_iota(jnp.int32, (BASE, 128), 1)
    row = lax.broadcasted_iota(jnp.int32, (BASE, 128), 0)
    blk = lane // BASE
    packed = []
    for low in lows:
        z = jnp.zeros((BASE, 128), f32)
        for b in range(128 // BASE):
            z = jnp.where(blk == b, low[BASE * b:BASE * (b + 1), :], z)
        packed.append(jnp.where(row > lane % BASE, z, 0.0))
    eye = jnp.where(row == lane % BASE, 1.0, 0.0).astype(f32)
    xs = [eye for _ in lows]
    for j in range(BASE - 1):
        idx = blk * BASE + j
        for i in range(n):
            lj = jnp.take_along_axis(packed[i], idx, axis=1, mode="promise_in_bounds")
            xs[i] = xs[i] - lj * xs[i][j:j + 1, :]
    fulls = []
    for x in xs:
        fulls.append(jnp.concatenate([jnp.where(blk == b, x, 0.0) for b in range(128 // BASE)], axis=0))
    m = BASE
    r2 = lax.broadcasted_iota(jnp.int32, (128, 128), 0)
    c2 = lax.broadcasted_iota(jnp.int32, (128, 128), 1)
    while m < 128:
        offmask = ((r2 // m) % 2 == 1) & (c2 // m == r2 // m - 1)
        xos = [jnp.concatenate([x[m * (2 * b + 1):m * (2 * b + 2), :] for b in range(64 // m)], 0) for x in fulls]
        offs = [split(jnp.where(offmask, low, 0.0)) for low in lows]
        xos_s = [split(xo) for xo in xos]
        xs_s = [split(x) for x in fulls]
        ys = [dot3s(*xo, *off) for xo, off in zip(xos_s, offs)]
        ys = [split(y) for y in ys]
        zs = [xo - dot3s(*y, *x) for xo, y, x in zip(xos, ys, xs_s)]
        out = []
        for x, z in zip(fulls, zs):
            rows = []
            for b in range(64 // m):
                rows.append(x[m * 2 * b:m * (2 * b + 1), :])
                rows.append(z[m * b:m * (b + 1), :])
            out.append(jnp.concatenate(rows, 0))
        fulls = out
        m *= 2
    return fulls

MESH = pl.DeviceIdType.MESH
HEADS = 16
NX, NL, NG, NY = 4, 4, 4, 4
PAIR, ROW, LOW, HIGH, YS, LOW_BACK, ROW_BACK, BACK, GAIN, GAIN_ROW, SEMS = 0, 8, 16, 24, 32, 40, 48, 56, 64, 65, 69


def local_solves(keys, values, betas):
    hs = range(len(keys))
    r2 = lax.broadcasted_iota(jnp.int32, (128, 128), 0)
    c2 = lax.broadcasted_iota(jnp.int32, (128, 128), 1)
    eye = jnp.where(r2 == c2, 1.0, 0.0).astype(f32)
    lows, crosses, rights = [], [], []
    for k, v, beta in zip(keys, values, betas):
        kf = k.astype(f32)
        ssq = jnp.sum(kf * kf, axis=1, keepdims=True) + 1e-6
        p = beta / ssq
        bs = beta * lax.rsqrt(ssq)
        gram = mm_nt(k, k)
        lows.append(jnp.where(r2 > c2, p[:128] * gram[:128, :128], 0.0))
        lows.append(jnp.where(r2 > c2, p[128:] * gram[128:, 128:], 0.0))
        crosses.append(p[128:] * gram[128:, :128])
        rights.append(jnp.concatenate([p * kf, bs * v.astype(f32)], axis=1))
    invs = unit_lower_inverses(lows)
    y1 = [dot3(invs[2 * h], rights[h][:128]) for h in hs]
    rest = [rights[h][128:] - dot3(crosses[h], y1[h]) for h in hs]
    y2 = [dot3(invs[2 * h + 1], rest[h]) for h in hs]
    ys = [split(jnp.concatenate([y1[h], y2[h]], 0)) for h in hs]
    kys = [mm_tn(keys[h], ys[h][0]) + mm_tn(keys[h], ys[h][1]) for h in hs]
    return ys, [(eye - ky[:, :D], ky[:, D:]) for ky in kys]


def local_outputs(queries, keys, ys):
    vis = lax.broadcasted_iota(jnp.int32, (T, N), 1) <= 2 * lax.broadcasted_iota(jnp.int32, (T, N), 0) + 1
    scores = [split(jnp.where(vis, mm_nt(q, k), 0.0)) for q, k in zip(queries, keys)]
    sys_ = [dot3s(*s, *y) for s, y in zip(scores, ys)]
    return [(q.astype(f32) - sy[:, :D], sy[:, D:]) for q, sy in zip(queries, sys_)]


def compose(late, early):
    joined = dot3(late[:, :D], early)
    return jnp.concatenate([joined[:, :D], joined[:, D:] + late[:, D:]], axis=1)


def advance(pair, state):
    return dot3(pair[:, :D], state) + pair[:, D:]


def states_kernel(
    k_ref, v_ref, q_ref, b_ref, gain_ref, qo_ref, m_ref, gains_ref,
    pool, chip, row_in, row_pre, row_tot, low_in, low_pre, low_tot,
    high_in, high_pre, high_tot, y_in, start, low_out, low_state,
    row_out, chip_state, after, send, recv, near,
):
    seq, head = lax.axis_index("seq"), lax.axis_index("head")
    x, c = head // 2, head % 2
    y, g, l = seq // (NG * NL), (seq // NL) % NG, seq % NL
    oc = 1 - c

    def meet(gg):
        return 2 - c + (((gg + 1) // 2) % 2) * (2 * c - 1)

    hub = meet(g)
    is_hub = l == hub

    def device(xx=None, cc=None, yy=None, gg=None, ll=None):
        xx, cc = x if xx is None else xx, c if cc is None else cc
        yy, gg, ll = y if yy is None else yy, g if gg is None else gg, l if ll is None else ll
        return {"seq": (yy * NG + gg) * NL + ll, "head": xx * 2 + cc}

    partner = device(cc=oc)

    def remote(src, dst, s, r, where):
        return pltpu.make_async_remote_copy(
            src_ref=src, dst_ref=dst, send_sem=send.at[s], recv_sem=recv.at[r],
            device_id=where, device_id_type=MESH,
        )

    barrier = pltpu.get_barrier_semaphore()
    rows = [device(xx=(x + k) % NX) for k in (1, 2, 3)]

    def greet(peers):
        for peer in peers:
            pl.semaphore_signal(barrier, inc=1, device_id=peer, device_id_type=MESH)

    @pl.when(is_hub)
    def _():
        greet([device(ll=(l + k) % NL) for k in (1, 2, 3)])
        greet([device(xx=(x + k) % NX, cc=oc) for k in (0, 1, 2, 3)])
        greet([device(gg=(g + k) % NG, ll=meet((g + k) % NG)) for k in (1, 2, 3)])
        for k in (1, 2, 3):
            @pl.when(y >= k)
            def _():
                greet([device(yy=(y + NY - k) % NY)])

    @pl.when(l != hub)
    def _():
        greet(rows)

    @pl.when((l != hub) & (l != 3 - hub))
    def _():
        greet([partner])

    def near_met():
        @pl.when((l != hub) & (l != 3 - hub))
        def _():
            pl.semaphore_wait(barrier, 5)
            pl.semaphore_signal(near, inc=1, device_id=device(ll=hub), device_id_type=MESH)

        @pl.when(l == 3 - hub)
        def _():
            pl.semaphore_wait(barrier, 8)
            pl.semaphore_signal(near, inc=1, device_id=device(ll=hub), device_id_type=MESH)
            pl.semaphore_signal(near, inc=1, device_id=partner, device_id_type=MESH)

    gains_ref[head] = gain_ref[...]

    def gain_copy():
        return remote(gain_ref, gains_ref.at[head], GAIN, GAIN, partner)

    def gain_row_copy(k, there, origin):
        rows = gains_ref.at[pl.ds(2 * origin, 2)]
        return remote(rows, rows, GAIN_ROW + k, GAIN_ROW + origin, device(xx=there))

    def pair_copy(i):
        return remote(pool.at[oc, i], pool.at[2, i], PAIR + i, PAIR + i, partner)

    def row_copy(e, k, there, origin):
        return remote(
            chip.at[2 * there + e], row_in.at[e, origin], ROW + 4 * e + k, ROW + 4 * e + origin, device(xx=there)
        )

    def low_copy(e, there, origin):
        return remote(row_tot.at[e], low_in.at[e, origin], LOW + 4 * e, LOW + 4 * e + origin, device(ll=there))

    def high_copy(e, k, there, origin):
        return remote(
            low_tot.at[e], high_in.at[e, origin], HIGH + 4 * e + k, HIGH + 4 * e + origin,
            device(gg=there, ll=meet(there)),
        )

    def y_copy(e, k, there, origin):
        return remote(high_tot.at[e], y_in.at[e, origin], YS + 4 * e + k, YS + 4 * e + origin, device(yy=there))

    def low_back(e, there):
        return remote(
            low_out.at[e, there], low_state.at[e], LOW_BACK + 4 * e + there, LOW_BACK + 4 * e, device(ll=there)
        )

    def row_back(e, k, there, origin):
        return remote(
            row_out.at[e, there], chip_state.at[2 * origin + e], ROW_BACK + 4 * e + k, ROW_BACK + 4 * e + origin,
            device(xx=there),
        )

    def back_copy(src, i):
        return remote(src.at[i], m_ref.at[8 * c + i], BACK + i, BACK + i, partner)

    def joint(parts, e, pre, tot):
        first = compose(parts[e, 1], parts[e, 0])
        last = compose(parts[e, 3], parts[e, 2])
        tot[e] = compose(last, first)
        pre[e, 0] = parts[e, 0]
        pre[e, 1] = first

    def third(parts, e, pre):
        pre[e, 2] = compose(parts[e, 2], pre[e, 1])

    def join_chip(e):
        for k in (2, 1, 3, 0):
            there = (x + k) % NX
            i = 2 * there + e
            pair_copy(i).wait_recv()
            joined = compose(pool[2 - c, i], pool[2 * c, i])
            if k:
                chip[i] = joined
                row_copy(e, k, there, x).start()
            else:
                row_in[e, x] = joined

    def up_row(e):
        for k in (1, 2, 3):
            origin = (x + k) % NX
            row_copy(e, 0, origin, origin).wait_recv()
        joint(row_in, e, row_pre, row_tot)

        @pl.when(l != hub)
        def _():
            low_copy(e, hub, l).start()

        @pl.when(is_hub)
        def _():
            low_in[e, l] = row_tot[e]

        third(row_in, e, row_pre)

    def up_low(e):
        @pl.when(is_hub)
        def _():
            for k in (1, 2, 3):
                origin = (l + k) % NL
                low_copy(e, origin, origin).wait_recv()
            joint(low_in, e, low_pre, low_tot)
            if e == 0:
                pl.semaphore_wait(barrier, 6 - y)
            for k in (2, 1, 3):
                high_copy(e, k, (g + k) % NG, g).start()
            high_in[e, g] = low_tot[e]
            third(low_in, e, low_pre)

    def up_high(e):
        @pl.when(is_hub)
        def _():
            for k in (1, 2, 3):
                origin = (g + k) % NG
                high_copy(e, k, origin, origin).wait_recv()
            joint(high_in, e, high_pre, high_tot)
            for k in (2, 1, 3):
                @pl.when(y + k < NY)
                def _():
                    y_copy(e, k, (y + k) % NY, y).start()
            third(high_in, e, high_pre)

    def down_high(e):
        @pl.when(is_hub)
        def _():
            start[e] = jnp.zeros((D, D), f32)
            for s in (0, 1, 2):
                @pl.when(y > s)
                def _():
                    y_copy(e, 0, s, s).wait_recv()
                    start[e] = advance(y_in[e, s], start[e])

            @pl.when(g > 0)
            def _():
                start[e] = advance(high_pre[e, g - 1], start[e])

            begin = start[e]
            for place in range(NL):
                low_out[e, place] = begin if place == 0 else advance(low_pre[e, place - 1], begin)

                @pl.when(l != place)
                def _():
                    low_back(e, place).start()

                @pl.when(l == place)
                def _():
                    low_state[e] = low_out[e, place]

    def down_row(e):
        @pl.when(l != hub)
        def _():
            low_back(e, hub).wait_recv()
        begin = low_state[e]
        for place in range(NX):
            row_out[e, place] = begin if place == 0 else advance(row_pre[e, place - 1], begin)
        for k in (2, 1, 3):
            row_back(e, k, (x + k) % NX, x).start()
        chip_state[2 * x + e] = row_out[e, x]

    def down_chip(e):
        for k in (0, 1, 3, 2):
            origin = (x + k) % NX
            i = 2 * origin + e
            if k:
                row_back(e, 0, origin, origin).wait_recv()

            @pl.when(c == 1)
            def _():
                back_copy(chip_state, i).start()

            begin = chip_state[i]
            end = advance(pool[2 * c, i], begin)

            @pl.when(c == 0)
            def _():
                after[i] = end
                back_copy(after, i).start()
                m_ref[i] = begin

            @pl.when(c == 1)
            def _():
                m_ref[8 + i] = end

    lane = lax.broadcasted_iota(jnp.int32, (N, HEADS), 1)

    def turn(t, carry):
        e, half = t // 2, t % 2
        here = [2 * v + e for v in range(NX)]
        betas = [
            jnp.sum(jnp.where(lane == 8 * half + i, b_ref[...], 0.0), axis=1, keepdims=True) for i in here
        ]
        keys = [k_ref[8 * half + i] for i in here]
        ys, maps = local_solves(keys, [v_ref[8 * half + i] for i in here], betas)
        for i, (a_part, b_part) in zip(here, maps):
            pool[half, i, :, :D] = a_part
            pool[half, i, :, D:] = b_part

        @pl.when(t == 0)
        def _():
            near_met()

        @pl.when((t == 1) & is_hub)
        def _():
            pl.semaphore_wait(near, 4)

        @pl.when((t == 1) & is_hub & (c == 1))
        def _():
            for v in range(NX):
                pair_copy(2 * v).start()

        @pl.when((half != c) & ((t > 0) | (l != hub)))
        def _():
            for i in here:
                pair_copy(i).start()

        @pl.when(t == 1)
        def _():
            gain_copy().start()

        outs = local_outputs([q_ref[8 * half + i] for i in here], keys, ys)
        for i, (q_part, o_part) in zip(here, outs):
            qo_ref[8 * half + i, :, :D] = q_part
            qo_ref[8 * half + i, :, D:] = o_part

        @pl.when(t == 1 + c)
        def _():
            join_chip(0)

        @pl.when((t == 2) & (c == 0))
        def _():
            up_row(0)

        return carry

    lax.fori_loop(0, 4, turn, 0)

    def on_core(which, step):
        @pl.when(c == which)
        def _():
            step()

    on_core(1, lambda: up_row(0))
    join_chip(1)
    remote(gain_ref, gains_ref.at[2 * x + oc], GAIN, GAIN, partner).wait_recv()
    for k in (1, 2, 3):
        gain_row_copy(k, (x + k) % NX, x).start()
    on_core(0, lambda: up_low(0))
    up_row(1)
    on_core(1, lambda: up_low(0))
    on_core(0, lambda: up_high(0))
    up_low(1)
    on_core(1, lambda: up_high(0))
    down_high(0)
    up_high(1)
    down_row(0)
    on_core(0, lambda: down_chip(0))
    down_high(1)
    on_core(1, lambda: down_chip(0))
    down_row(1)
    down_chip(1)
    for i in range(8):
        remote(after.at[i], m_ref.at[8 * oc + i], BACK + i, BACK + i, partner).wait_recv()
    for k in (1, 2, 3):
        origin = (x + k) % NX
        gain_row_copy(k, origin, origin).wait_recv()

    gain_copy().wait_send()
    for k in (1, 2, 3):
        gain_row_copy(k, (x + k) % NX, x).wait_send()
    for i in range(8):
        pair_copy(i).wait_send()
        back_copy(after, i).wait_send()
    for e in range(2):
        for k in (1, 2, 3):
            row_copy(e, k, (x + k) % NX, x).wait_send()
            row_back(e, k, (x + k) % NX, x).wait_send()

        @pl.when(l != hub)
        def _():
            low_copy(e, hub, l).wait_send()

        @pl.when(is_hub)
        def _():
            for place in range(NL):
                @pl.when(l != place)
                def _():
                    low_back(e, place).wait_send()
            for k in (1, 2, 3):
                high_copy(e, k, (g + k) % NG, g).wait_send()

                @pl.when(y + k < NY)
                def _():
                    y_copy(e, k, (y + k) % NY, y).wait_send()


def states(keys, values, queries, betas, gain):
    wide, square = (D, 2 * D), (D, D)
    whole = pl.BlockSpec(memory_space=pltpu.VMEM)

    def vm(*shape):
        return pltpu.VMEM(shape, f32)

    return pl.pallas_call(
        states_kernel,
        in_specs=[whole] * 5,
        out_specs=[whole] * 3,
        out_shape=[
            jax.ShapeDtypeStruct((HEADS, T, 2 * D), f32),
            jax.ShapeDtypeStruct((HEADS, D, D), f32),
            jax.ShapeDtypeStruct((8, 2, D), f32),
        ],
        scratch_shapes=[
            vm(3, 8, *wide), vm(8, *wide),
            vm(2, NX, *wide), vm(2, 3, *wide), vm(2, *wide),
            vm(2, NL, *wide), vm(2, 3, *wide), vm(2, *wide),
            vm(2, NG, *wide), vm(2, 3, *wide), vm(2, *wide),
            vm(2, NY, *wide), vm(2, *square), vm(2, NL, *square), vm(2, *square),
            vm(2, NX, *square), vm(8, *square), vm(8, *square),
            pltpu.SemaphoreType.DMA((SEMS,)), pltpu.SemaphoreType.DMA((SEMS,)), pltpu.SemaphoreType.REGULAR,
        ],
        compiler_params=pltpu.CompilerParams(
            collective_id=0, has_side_effects=True, vmem_limit_bytes=48 * 2**20
        ),
    )(keys, values, queries, betas, gain)


def by_head_kernel(k_ref, v_ref, q_ref, ko_ref, vo_ref, qo_ref, held, sem, q_sem):
    fetch = pltpu.make_async_copy(q_ref, held, q_sem)
    fetch.start()
    copies = [
        pltpu.make_async_copy(src.at[:, h], dst.at[h], sem.at[n, h])
        for h in range(HEADS)
        for n, (src, dst) in enumerate(((k_ref, ko_ref), (v_ref, vo_ref)))
    ]
    for copy in copies:
        copy.start()
    fetch.wait()
    qo_ref[...] = jnp.swapaxes(held[...].astype(f32), 0, 1).astype(bf16)
    for copy in copies:
        copy.wait()


def by_head(keys, values, queries):
    whole, away = pl.BlockSpec(memory_space=pltpu.VMEM), pl.BlockSpec(memory_space=pl.ANY)
    pairs = jax.ShapeDtypeStruct((HEADS, T, 2, D), bf16)
    k, v, q = pl.pallas_call(
        by_head_kernel,
        in_specs=[away] * 3,
        out_specs=[whole] * 3,
        out_shape=[pairs, pairs, jax.ShapeDtypeStruct((HEADS, T, D), bf16)],
        scratch_shapes=[
            pltpu.VMEM((T, HEADS, D), bf16), pltpu.SemaphoreType.DMA((2, HEADS)), pltpu.SemaphoreType.DMA,
        ],
        compiler_params=pltpu.CompilerParams(vmem_limit_bytes=50 * 2**20),
    )(keys, values, queries)
    return k.reshape(HEADS, N, D), v.reshape(HEADS, N, D), q


def output_kernel(qo_ref, m_ref, gains_ref, gate_ref, out_ref, rows):
    for h in range(HEADS):
        r = dot3(qo_ref[h, :, :D], m_ref[h]) + qo_ref[h, :, D:]
        scale = lax.rsqrt(jnp.mean(r * r, axis=-1, keepdims=True) + 1e-6)
        rows[h] = r * scale * gains_ref[h // 2, h % 2 : h % 2 + 1, :]
    gate = gate_ref[...].astype(f32)
    normed = jnp.swapaxes(rows[...], 0, 1)
    out_ref[...] = (normed * (gate / (1.0 + jnp.exp(-gate)))).astype(bf16)


def outputs(qo, m, gains, gate):
    whole = pl.BlockSpec(memory_space=pltpu.VMEM)
    return pl.pallas_call(
        output_kernel,
        in_specs=[whole] * 4,
        out_specs=whole,
        out_shape=jax.ShapeDtypeStruct((T, HEADS, D), bf16),
        scratch_shapes=[pltpu.VMEM((HEADS, T, D), f32)],
        compiler_params=pltpu.CompilerParams(vmem_limit_bytes=48 * 2**20),
    )(qo, m, gains, gate)


def local(queries, keys, values, betas, gate, gain):
    keys_h, values_h, queries_h = by_head(keys, values, queries)
    betas_h = jnp.transpose(betas, (0, 2, 1)).reshape(N, HEADS).astype(f32)
    qo, m, gains = states(keys_h, values_h, queries_h, betas_h, gain)
    return outputs(qo, m, gains, gate)


def solution(mesh):
    return jax.shard_map(
        local,
        mesh=mesh,
        in_specs=(
            P(("seq", "head"), None, None),
            P(("seq", "head"), None, None, None),
            P(("seq", "head"), None, None, None),
            P(("seq", "head"), None, None),
            P(("seq", "head"), None, None),
            P("head", None),
        ),
        out_specs=P(("seq", "head"), None, None),
        check_vma=False,
    )
```

```python
import functools
import jax, jax.numpy as jnp
from jax import lax
from jax.experimental import pallas as pl
from jax.experimental.pallas import tpu as pltpu
from jax.sharding import PartitionSpec as P
f32, bf16 = jnp.float32, jnp.bfloat16
D = 128
N = 256
T = 128
BASE = 16

def split(a):
    hi = a.astype(bf16)
    return hi, (a - hi.astype(f32)).astype(bf16)

def mm(a, b):
    return lax.dot_general(a, b, (((1,), (0,)), ((), ())), preferred_element_type=f32)

def mm_nt(a, b):
    return lax.dot_general(a, b, (((1,), (1,)), ((), ())), preferred_element_type=f32)

def mm_tn(a, b):
    return lax.dot_general(a, b, (((0,), (0,)), ((), ())), preferred_element_type=f32)

def dot3(a, b):
    ah, al = split(a)
    bh, bl = split(b)
    return dot3s(ah, al, bh, bl)

def dot3s(ah, al, bh, bl):
    if ah.shape[1] == 128:
        return mm(jnp.concatenate([ah, al], 1), jnp.concatenate([bh, bh], 0)) + mm(ah, bl)
    return mm(ah, bh) + (mm(al, bh) + mm(ah, bl))

def unit_lower_inverses(lows):
    n = len(lows)
    lane = lax.broadcasted_iota(jnp.int32, (BASE, 128), 1)
    row = lax.broadcasted_iota(jnp.int32, (BASE, 128), 0)
    blk = lane // BASE
    half = BASE // 2
    upper, lower = [], []
    for low in lows:
        z = jnp.zeros((BASE, 128), f32)
        for b in range(128 // BASE):
            z = jnp.where(blk == b, low[BASE * b:BASE * (b + 1), :], z)
        z = jnp.where(row > lane % BASE, z, 0.0)
        upper.append(z[:half])
        lower.append(z[half:])
    eye = jnp.where(row == lane % BASE, 1.0, 0.0).astype(f32)
    tops, ends = [eye[:half] for _ in lows], [eye[half:] for _ in lows]
    blk = blk[:half]
    for j in range(BASE - 1):
        idx = blk * BASE + j
        for i in range(n):
            pivot = tops[i][j:j + 1, :] if j < half else ends[i][j - half:j - half + 1, :]
            ends[i] = ends[i] - jnp.take_along_axis(lower[i], idx, axis=1, mode="promise_in_bounds") * pivot
            if j < half - 1:
                tops[i] = tops[i] - jnp.take_along_axis(upper[i], idx, axis=1, mode="promise_in_bounds") * pivot
    xs = [jnp.concatenate([top, end], 0) for top, end in zip(tops, ends)]
    blk = lane // BASE
    fulls = []
    for x in xs:
        fulls.append(jnp.concatenate([jnp.where(blk == b, x, 0.0) for b in range(128 // BASE)], axis=0))
    m = BASE
    r2 = lax.broadcasted_iota(jnp.int32, (128, 128), 0)
    c2 = lax.broadcasted_iota(jnp.int32, (128, 128), 1)
    while m < 128:
        offmask = ((r2 // m) % 2 == 1) & (c2 // m == r2 // m - 1)
        xos = [jnp.concatenate([x[m * (2 * b + 1):m * (2 * b + 2), :] for b in range(64 // m)], 0) for x in fulls]
        offs = [split(jnp.where(offmask, low, 0.0)) for low in lows]
        xos_s = [split(xo) for xo in xos]
        xs_s = [split(x) for x in fulls]
        ys = [dot3s(*xo, *off) for xo, off in zip(xos_s, offs)]
        ys = [split(y) for y in ys]
        zs = [xo - dot3s(*y, *x) for xo, y, x in zip(xos, ys, xs_s)]
        out = []
        for x, z in zip(fulls, zs):
            rows = []
            for b in range(64 // m):
                rows.append(x[m * 2 * b:m * (2 * b + 1), :])
                rows.append(z[m * b:m * (b + 1), :])
            out.append(jnp.concatenate(rows, 0))
        fulls = out
        m *= 2
    return fulls

MESH = pl.DeviceIdType.MESH
HEADS = 16
NX, NL, NG, NY = 4, 4, 4, 4
PAIR, ROW, LOW, HIGH, YS, LOW_BACK, ROW_BACK, BACK, GAIN, GAIN_ROW, SEMS = 0, 8, 16, 24, 32, 40, 48, 56, 64, 65, 69


def local_solves(keys, values, betas):
    hs = range(len(keys))
    r2 = lax.broadcasted_iota(jnp.int32, (128, 128), 0)
    c2 = lax.broadcasted_iota(jnp.int32, (128, 128), 1)
    eye = jnp.where(r2 == c2, 1.0, 0.0).astype(f32)
    lows, crosses, rights = [], [], []
    for k, v, beta in zip(keys, values, betas):
        kf = k.astype(f32)
        ssq = jnp.sum(kf * kf, axis=1, keepdims=True) + 1e-6
        p = beta / ssq
        bs = beta * lax.rsqrt(ssq)
        gram = mm_nt(k, k)
        lows.append(jnp.where(r2 > c2, p[:128] * gram[:128, :128], 0.0))
        lows.append(jnp.where(r2 > c2, p[128:] * gram[128:, 128:], 0.0))
        crosses.append(p[128:] * gram[128:, :128])
        rights.append(jnp.concatenate([p * kf, bs * v.astype(f32)], axis=1))
    invs = unit_lower_inverses(lows)
    y1 = [dot3(invs[2 * h], rights[h][:128]) for h in hs]
    rest = [rights[h][128:] - dot3(crosses[h], y1[h]) for h in hs]
    y2 = [dot3(invs[2 * h + 1], rest[h]) for h in hs]
    ys = [split(jnp.concatenate([y1[h], y2[h]], 0)) for h in hs]
    kys = [mm_tn(keys[h], ys[h][0]) + mm_tn(keys[h], ys[h][1]) for h in hs]
    return ys, [(eye - ky[:, :D], ky[:, D:]) for ky in kys]


def local_outputs(queries, keys, ys):
    vis = lax.broadcasted_iota(jnp.int32, (T, N), 1) <= 2 * lax.broadcasted_iota(jnp.int32, (T, N), 0) + 1
    scores = [split(jnp.where(vis, mm_nt(q, k), 0.0)) for q, k in zip(queries, keys)]
    sys_ = [dot3s(*s, *y) for s, y in zip(scores, ys)]
    return [(q.astype(f32) - sy[:, :D], sy[:, D:]) for q, sy in zip(queries, sys_)]


def compose(late, early):
    joined = dot3(late[:, :D], early)
    return jnp.concatenate([joined[:, :D], joined[:, D:] + late[:, D:]], axis=1)


def advance(pair, state):
    return dot3(pair[:, :D], state) + pair[:, D:]


def states_kernel(
    k_ref, v_ref, q_ref, b_ref, gain_ref, qo_ref, m_ref, gains_ref,
    pool, chip, row_in, row_pre, row_tot, low_in, low_pre, low_tot,
    high_in, high_tot, y_in, start, low_out, low_state,
    row_out, chip_state, after, y_high, y_low, send, recv, near,
):
    seq, head = lax.axis_index("seq"), lax.axis_index("head")
    x, c = head // 2, head % 2
    y, g, l = seq // (NG * NL), (seq // NL) % NG, seq % NL
    oc = 1 - c

    def meet(gg):
        return 2 - c + (((gg + 1) // 2) % 2) * (2 * c - 1)

    hub = meet(g)
    is_hub = l == hub

    def device(xx=None, cc=None, yy=None, gg=None, ll=None):
        xx, cc = x if xx is None else xx, c if cc is None else cc
        yy, gg, ll = y if yy is None else yy, g if gg is None else gg, l if ll is None else ll
        return {"seq": (yy * NG + gg) * NL + ll, "head": xx * 2 + cc}

    partner = device(cc=oc)

    def remote(src, dst, s, r, where):
        return pltpu.make_async_remote_copy(
            src_ref=src, dst_ref=dst, send_sem=send.at[s], recv_sem=recv.at[r],
            device_id=where, device_id_type=MESH,
        )

    barrier = pltpu.get_barrier_semaphore()
    rows = [device(xx=(x + k) % NX) for k in (1, 2, 3)]

    def greet(peers):
        for peer in peers:
            pl.semaphore_signal(barrier, inc=1, device_id=peer, device_id_type=MESH)

    @pl.when(is_hub)
    def _():
        greet([device(ll=(l + k) % NL) for k in (1, 2, 3)])
        greet([device(xx=(x + k) % NX, cc=oc) for k in (0, 1, 2, 3)])
        greet([device(gg=(g + k) % NG, ll=meet((g + k) % NG)) for k in (1, 2, 3)])
        for k in (1, 2, 3):
            @pl.when(y >= k)
            def _():
                greet([device(yy=(y + NY - k) % NY)])

    @pl.when(l != hub)
    def _():
        greet(rows)

    @pl.when((l != hub) & (l != 3 - hub))
    def _():
        greet([partner])

    def near_met():
        @pl.when((l != hub) & (l != 3 - hub))
        def _():
            pl.semaphore_wait(barrier, 5)
            pl.semaphore_signal(near, inc=1, device_id=device(ll=hub), device_id_type=MESH)

        @pl.when(l == 3 - hub)
        def _():
            pl.semaphore_wait(barrier, 8)
            pl.semaphore_signal(near, inc=1, device_id=device(ll=hub), device_id_type=MESH)
            pl.semaphore_signal(near, inc=1, device_id=partner, device_id_type=MESH)

    gains_ref[head] = gain_ref[...]

    def gain_copy():
        return remote(gain_ref, gains_ref.at[head], GAIN, GAIN, partner)

    def gain_row_copy(k, there, origin):
        rows = gains_ref.at[pl.ds(2 * origin, 2)]
        return remote(rows, rows, GAIN_ROW + k, GAIN_ROW + origin, device(xx=there))

    def pair_copy(i):
        return remote(pool.at[oc, i], pool.at[2, i], PAIR + i, PAIR + i, partner)

    def row_copy(e, k, there, origin):
        return remote(
            chip.at[2 * there + e], row_in.at[e, origin], ROW + 4 * e + k, ROW + 4 * e + origin, device(xx=there)
        )

    def low_copy(e, there, origin):
        return remote(row_tot.at[e], low_in.at[e, origin], LOW + 4 * e, LOW + 4 * e + origin, device(ll=there))

    def high_copy(e, k, there, origin):
        return remote(
            low_tot.at[e], high_in.at[e, origin], HIGH + 4 * e + k, HIGH + 4 * e + origin,
            device(gg=there, ll=meet(there)),
        )

    def y_copy(e, k, there, origin):
        return remote(high_tot.at[e], y_in.at[e, origin], YS + 4 * e + k, YS + 4 * e + origin, device(yy=there))

    def y_copy_first(e, k, there):
        part = pl.ds(D, D)
        return remote(
            high_tot.at[e, :, part], y_in.at[e, 0, :, part], YS + 4 * e + k, YS + 4 * e, device(yy=there)
        )

    def low_back(e, there):
        return remote(
            low_out.at[e, there], low_state.at[e], LOW_BACK + 4 * e + there, LOW_BACK + 4 * e, device(ll=there)
        )

    def row_back(e, k, there, origin):
        return remote(
            row_out.at[e, there], chip_state.at[2 * origin + e], ROW_BACK + 4 * e + k, ROW_BACK + 4 * e + origin,
            device(xx=there),
        )

    def back_copy(src, i):
        return remote(src.at[i], m_ref.at[8 * c + i], BACK + i, BACK + i, partner)

    def joint(parts, e, pre, tot):
        first = compose(parts[e, 1], parts[e, 0])
        last = compose(parts[e, 3], parts[e, 2])
        tot[e] = compose(last, first)
        pre[e, 0] = parts[e, 0]
        pre[e, 1] = first

    def third(parts, e, pre):
        pre[e, 2] = compose(parts[e, 2], pre[e, 1])

    def join_chip(e):
        for k in (2, 1, 3, 0):
            there = (x + k) % NX
            i = 2 * there + e
            pair_copy(i).wait_recv()
            joined = compose(pool[2 - c, i], pool[2 * c, i])
            if k:
                chip[i] = joined
                row_copy(e, k, there, x).start()
            else:
                row_in[e, x] = joined

    def up_row(e):
        for k in (1, 2, 3):
            origin = (x + k) % NX
            row_copy(e, 0, origin, origin).wait_recv()
        joint(row_in, e, row_pre, row_tot)

        @pl.when(l != hub)
        def _():
            low_copy(e, hub, l).start()

        @pl.when(is_hub)
        def _():
            low_in[e, l] = row_tot[e]

        third(row_in, e, row_pre)

    def up_low(e):
        @pl.when(is_hub)
        def _():
            for k in (1, 2, 3):
                origin = (l + k) % NL
                low_copy(e, origin, origin).wait_recv()
            joint(low_in, e, low_pre, low_tot)
            if e == 0:
                pl.semaphore_wait(barrier, 6 - y)
            for later in (True, False):
                for k in (1, 2, 3):
                    @pl.when((g + k < NG) == later)
                    def _():
                        high_copy(e, k, (g + k) % NG, g).start()
            high_in[e, g] = low_tot[e]
            third(low_in, e, low_pre)

    def high_wait(e, s):
        high_copy(e, 0, s, s).wait_recv()

    def through_hubs(e):
        @pl.when(is_hub)
        def _():
            for s in (0, 1, 2):
                @pl.when(g > s)
                def _():
                    high_wait(e, s)
                    high_tot[e] = high_in[e, 0] if s == 0 else compose(high_in[e, s], high_tot[e])

            start[e] = jnp.zeros((D, D), f32)

            @pl.when(y > 0)
            def _():
                y_copy_first(e, 0, 0).wait_recv()
                start[e] = y_in[e, 0, :, D:]

            for s in (1, 2):
                @pl.when(y > s)
                def _():
                    y_copy(e, 0, s, s).wait_recv()
                    start[e] = advance(y_in[e, s], start[e])

            @pl.when(g > 0)
            def _():
                start[e] = advance(high_tot[e], start[e])

            begin = start[e]
            for place in range(NL):
                low_out[e, place] = begin if place == 0 else advance(low_pre[e, place - 1], begin)

                @pl.when(l != place)
                def _():
                    low_back(e, place).start()

                @pl.when(l == place)
                def _():
                    low_state[e] = low_out[e, place]

            for s in range(NG):
                @pl.when(s > g)
                def _():
                    high_wait(e, s)

                @pl.when((s >= g) & (y < NY - 1))
                def _():
                    high_tot[e] = high_in[e, 0] if s == 0 else compose(high_in[e, s], high_tot[e])

            for k in (1, 2, 3):
                @pl.when(y == 0)
                def _():
                    y_copy_first(e, k, k).start()

                @pl.when((y > 0) & (y + k < NY))
                def _():
                    y_copy(e, k, (y + k) % NY, y).start()

    def down_row(e):
        @pl.when(l != hub)
        def _():
            low_back(e, hub).wait_recv()
        begin = low_state[e]
        for place in range(NX):
            row_out[e, place] = begin if place == 0 else advance(row_pre[e, place - 1], begin)
        for k in (2, 1, 3):
            row_back(e, k, (x + k) % NX, x).start()
        chip_state[2 * x + e] = row_out[e, x]

    def down_chip(e):
        for k in (0, 1, 3, 2):
            origin = (x + k) % NX
            i = 2 * origin + e
            if k:
                row_back(e, 0, origin, origin).wait_recv()

            @pl.when(c == 1)
            def _():
                back_copy(chip_state, i).start()

            begin = chip_state[i]
            end = advance(pool[2 * c, i], begin)

            @pl.when(c == 0)
            def _():
                after[i] = end
                back_copy(after, i).start()
                m_ref[i] = begin

            @pl.when(c == 1)
            def _():
                m_ref[8 + i] = end

    lane = lax.broadcasted_iota(jnp.int32, (N, HEADS), 1)

    def turn(t, carry):
        e, half = t // 2, t % 2
        here = [2 * v + e for v in range(NX)]
        betas = [
            jnp.sum(jnp.where(lane == 8 * half + i, b_ref[...], 0.0), axis=1, keepdims=True) for i in here
        ]
        keys = [k_ref[8 * half + i] for i in here]
        ys, maps = local_solves(keys, [v_ref[8 * half + i] for i in here], betas)
        for i, (a_part, b_part), (hi, lo) in zip(here, maps, ys):
            pool[half, i, :, :D] = a_part
            pool[half, i, :, D:] = b_part
            y_high[8 * half + i] = hi
            y_low[8 * half + i] = lo

        @pl.when(t == 0)
        def _():
            near_met()

        @pl.when((t == 1) & is_hub)
        def _():
            pl.semaphore_wait(near, 4)

        @pl.when((t == 1) & is_hub & (c == 1))
        def _():
            for v in range(NX):
                pair_copy(2 * v).start()

        @pl.when((half != c) & ((t > 0) | (l != hub)))
        def _():
            for i in here:
                pair_copy(i).start()

        @pl.when(t == 1)
        def _():
            gain_copy().start()

        @pl.when(t == 1 + c)
        def _():
            join_chip(0)

        @pl.when((t == 2) & (c == 0))
        def _():
            up_row(0)

        return carry

    lax.fori_loop(0, 4, turn, 0)

    def local_out(first):
        here = [first + 2 * v for v in range(NX)]
        outs = local_outputs(
            [q_ref[h] for h in here], [k_ref[h] for h in here], [(y_high[h], y_low[h]) for h in here]
        )
        for h, (q_part, o_part) in zip(here, outs):
            qo_ref[h, :, :D] = q_part
            qo_ref[h, :, D:] = o_part

    def on_core(which, step):
        @pl.when(c == which)
        def _():
            step()

    on_core(1, lambda: up_row(0))
    join_chip(1)
    remote(gain_ref, gains_ref.at[2 * x + oc], GAIN, GAIN, partner).wait_recv()
    for k in (1, 2, 3):
        gain_row_copy(k, (x + k) % NX, x).start()
    local_out(0)
    on_core(0, lambda: up_low(0))
    up_row(1)
    on_core(1, lambda: up_low(0))
    local_out(1)
    up_low(1)
    local_out(8)
    through_hubs(0)
    local_out(9)
    down_row(0)
    on_core(0, lambda: down_chip(0))
    through_hubs(1)
    on_core(1, lambda: down_chip(0))
    down_row(1)
    down_chip(1)
    for i in range(8):
        remote(after.at[i], m_ref.at[8 * oc + i], BACK + i, BACK + i, partner).wait_recv()
    for k in (1, 2, 3):
        origin = (x + k) % NX
        gain_row_copy(k, origin, origin).wait_recv()

    gain_copy().wait_send()
    for k in (1, 2, 3):
        gain_row_copy(k, (x + k) % NX, x).wait_send()
    for i in range(8):
        pair_copy(i).wait_send()
        back_copy(after, i).wait_send()
    for e in range(2):
        for k in (1, 2, 3):
            row_copy(e, k, (x + k) % NX, x).wait_send()
            row_back(e, k, (x + k) % NX, x).wait_send()

        @pl.when(l != hub)
        def _():
            low_copy(e, hub, l).wait_send()

        @pl.when(is_hub)
        def _():
            for place in range(NL):
                @pl.when(l != place)
                def _():
                    low_back(e, place).wait_send()
            for k in (1, 2, 3):
                high_copy(e, k, (g + k) % NG, g).wait_send()

                @pl.when(y == 0)
                def _():
                    y_copy_first(e, k, k).wait_send()

                @pl.when((y > 0) & (y + k < NY))
                def _():
                    y_copy(e, k, (y + k) % NY, y).wait_send()


def states(keys, values, queries, betas, gain):
    wide, square = (D, 2 * D), (D, D)
    whole = pl.BlockSpec(memory_space=pltpu.VMEM)

    def vm(*shape):
        return pltpu.VMEM(shape, f32)

    return pl.pallas_call(
        states_kernel,
        in_specs=[whole] * 5,
        out_specs=[whole] * 3,
        out_shape=[
            jax.ShapeDtypeStruct((HEADS, T, 2 * D), f32),
            jax.ShapeDtypeStruct((HEADS, D, D), f32),
            jax.ShapeDtypeStruct((8, 2, D), f32),
        ],
        scratch_shapes=[
            vm(3, 8, *wide), vm(8, *wide),
            vm(2, NX, *wide), vm(2, 3, *wide), vm(2, *wide),
            vm(2, NL, *wide), vm(2, 3, *wide), vm(2, *wide),
            vm(2, NG, *wide), vm(2, *wide),
            vm(2, NY, *wide), vm(2, *square), vm(2, NL, *square), vm(2, *square),
            vm(2, NX, *square), vm(8, *square), vm(8, *square),
            pltpu.VMEM((HEADS, N, 2 * D), bf16), pltpu.VMEM((HEADS, N, 2 * D), bf16),
            pltpu.SemaphoreType.DMA((SEMS,)), pltpu.SemaphoreType.DMA((SEMS,)), pltpu.SemaphoreType.REGULAR,
        ],
        compiler_params=pltpu.CompilerParams(
            collective_id=0, has_side_effects=True, vmem_limit_bytes=48 * 2**20
        ),
    )(keys, values, queries, betas, gain)


def by_head_kernel(k_ref, v_ref, q_ref, ko_ref, vo_ref, qo_ref, held, sem, q_sem):
    fetch = pltpu.make_async_copy(q_ref, held, q_sem)
    fetch.start()
    copies = [
        pltpu.make_async_copy(src.at[:, h], dst.at[h], sem.at[n, h])
        for h in range(HEADS)
        for n, (src, dst) in enumerate(((k_ref, ko_ref), (v_ref, vo_ref)))
    ]
    for copy in copies:
        copy.start()
    fetch.wait()
    qo_ref[...] = jnp.swapaxes(held[...].astype(f32), 0, 1).astype(bf16)
    for copy in copies:
        copy.wait()


def by_head(keys, values, queries):
    whole, away = pl.BlockSpec(memory_space=pltpu.VMEM), pl.BlockSpec(memory_space=pl.ANY)
    pairs = jax.ShapeDtypeStruct((HEADS, T, 2, D), bf16)
    k, v, q = pl.pallas_call(
        by_head_kernel,
        in_specs=[away] * 3,
        out_specs=[whole] * 3,
        out_shape=[pairs, pairs, jax.ShapeDtypeStruct((HEADS, T, D), bf16)],
        scratch_shapes=[
            pltpu.VMEM((T, HEADS, D), bf16), pltpu.SemaphoreType.DMA((2, HEADS)), pltpu.SemaphoreType.DMA,
        ],
        compiler_params=pltpu.CompilerParams(vmem_limit_bytes=50 * 2**20),
    )(keys, values, queries)
    return k.reshape(HEADS, N, D), v.reshape(HEADS, N, D), q


def output_kernel(qo_ref, m_ref, gains_ref, gate_ref, out_ref, rows):
    for h in range(HEADS):
        r = dot3(qo_ref[h, :, :D], m_ref[h]) + qo_ref[h, :, D:]
        scale = lax.rsqrt(jnp.mean(r * r, axis=-1, keepdims=True) + 1e-6)
        rows[h] = r * scale * gains_ref[h // 2, h % 2 : h % 2 + 1, :]
    gate = gate_ref[...].astype(f32)
    normed = jnp.swapaxes(rows[...], 0, 1)
    out_ref[...] = (normed * (gate / (1.0 + jnp.exp(-gate)))).astype(bf16)


def outputs(qo, m, gains, gate):
    whole = pl.BlockSpec(memory_space=pltpu.VMEM)
    return pl.pallas_call(
        output_kernel,
        in_specs=[whole] * 4,
        out_specs=whole,
        out_shape=jax.ShapeDtypeStruct((T, HEADS, D), bf16),
        scratch_shapes=[pltpu.VMEM((HEADS, T, D), f32)],
        compiler_params=pltpu.CompilerParams(vmem_limit_bytes=48 * 2**20),
    )(qo, m, gains, gate)


def local(queries, keys, values, betas, gate, gain):
    keys_h, values_h, queries_h = by_head(keys, values, queries)
    betas_h = jnp.transpose(betas, (0, 2, 1)).reshape(N, HEADS).astype(f32)
    qo, m, gains = states(keys_h, values_h, queries_h, betas_h, gain)
    return outputs(qo, m, gains, gate)


def solution(mesh):
    return jax.shard_map(
        local,
        mesh=mesh,
        in_specs=(
            P(("seq", "head"), None, None),
            P(("seq", "head"), None, None, None),
            P(("seq", "head"), None, None, None),
            P(("seq", "head"), None, None),
            P(("seq", "head"), None, None),
            P("head", None),
        ),
        out_specs=P(("seq", "head"), None, None),
        check_vma=False,
    )
```

```python
import functools
import jax, jax.numpy as jnp
from jax import lax
from jax.experimental import pallas as pl
from jax.experimental.pallas import tpu as pltpu
from jax.sharding import PartitionSpec as P
f32, bf16 = jnp.float32, jnp.bfloat16
D = 128
N = 256
T = 128
BASE = 16

def split(a):
    hi = a.astype(bf16)
    return hi, (a - hi.astype(f32)).astype(bf16)

def mm(a, b):
    return lax.dot_general(a, b, (((1,), (0,)), ((), ())), preferred_element_type=f32)

def mm_nt(a, b):
    return lax.dot_general(a, b, (((1,), (1,)), ((), ())), preferred_element_type=f32)

def mm_tn(a, b):
    return lax.dot_general(a, b, (((0,), (0,)), ((), ())), preferred_element_type=f32)

def dot3(a, b):
    ah, al = split(a)
    bh, bl = split(b)
    return dot3s(ah, al, bh, bl)

def dot3s(ah, al, bh, bl):
    if ah.shape[1] == 128:
        return mm(jnp.concatenate([ah, al], 1), jnp.concatenate([bh, bh], 0)) + mm(ah, bl)
    return mm(ah, bh) + (mm(al, bh) + mm(ah, bl))

def unit_lower_inverses(lows):
    n = len(lows)
    lane = lax.broadcasted_iota(jnp.int32, (BASE, 128), 1)
    row = lax.broadcasted_iota(jnp.int32, (BASE, 128), 0)
    blk = lane // BASE
    half = BASE // 2
    upper, lower = [], []
    for low in lows:
        z = jnp.zeros((BASE, 128), f32)
        for b in range(128 // BASE):
            z = jnp.where(blk == b, low[BASE * b:BASE * (b + 1), :], z)
        z = jnp.where(row > lane % BASE, z, 0.0)
        upper.append(z[:half])
        lower.append(z[half:])
    eye = jnp.where(row == lane % BASE, 1.0, 0.0).astype(f32)
    tops, ends = [eye[:half] for _ in lows], [eye[half:] for _ in lows]
    blk = blk[:half]
    for j in range(BASE - 1):
        idx = blk * BASE + j
        for i in range(n):
            pivot = tops[i][j:j + 1, :] if j < half else ends[i][j - half:j - half + 1, :]
            ends[i] = ends[i] - jnp.take_along_axis(lower[i], idx, axis=1, mode="promise_in_bounds") * pivot
            if j < half - 1:
                tops[i] = tops[i] - jnp.take_along_axis(upper[i], idx, axis=1, mode="promise_in_bounds") * pivot
    xs = [jnp.concatenate([top, end], 0) for top, end in zip(tops, ends)]
    blk = lane // BASE
    fulls = []
    for x in xs:
        fulls.append(jnp.concatenate([jnp.where(blk == b, x, 0.0) for b in range(128 // BASE)], axis=0))
    m = BASE
    r2 = lax.broadcasted_iota(jnp.int32, (128, 128), 0)
    c2 = lax.broadcasted_iota(jnp.int32, (128, 128), 1)
    while m < 128:
        offmask = ((r2 // m) % 2 == 1) & (c2 // m == r2 // m - 1)
        xos = [jnp.concatenate([x[m * (2 * b + 1):m * (2 * b + 2), :] for b in range(64 // m)], 0) for x in fulls]
        offs = [split(jnp.where(offmask, low, 0.0)) for low in lows]
        xos_s = [split(xo) for xo in xos]
        xs_s = [split(x) for x in fulls]
        ys = [dot3s(*xo, *off) for xo, off in zip(xos_s, offs)]
        ys = [split(y) for y in ys]
        zs = [xo - dot3s(*y, *x) for xo, y, x in zip(xos, ys, xs_s)]
        out = []
        for x, z in zip(fulls, zs):
            rows = []
            for b in range(64 // m):
                rows.append(x[m * 2 * b:m * (2 * b + 1), :])
                rows.append(z[m * b:m * (b + 1), :])
            out.append(jnp.concatenate(rows, 0))
        fulls = out
        m *= 2
    return fulls

MESH = pl.DeviceIdType.MESH
HEADS = 16
NX, NL, NG, NY = 4, 4, 4, 4
PAIR, ROW, LOW, HIGH, YS, LOW_BACK, ROW_BACK, BACK, GAIN, GAIN_ROW, SEMS = 0, 8, 16, 24, 32, 40, 48, 56, 64, 65, 69


def local_solves(keys, values, betas):
    hs = range(len(keys))
    r2 = lax.broadcasted_iota(jnp.int32, (128, 128), 0)
    c2 = lax.broadcasted_iota(jnp.int32, (128, 128), 1)
    eye = jnp.where(r2 == c2, 1.0, 0.0).astype(f32)
    lows, crosses, rights = [], [], []
    for k, v, beta in zip(keys, values, betas):
        kf = k.astype(f32)
        ssq = jnp.sum(kf * kf, axis=1, keepdims=True) + 1e-6
        p = beta / ssq
        bs = beta * lax.rsqrt(ssq)
        gram = mm_nt(k, k)
        lows.append(jnp.where(r2 > c2, p[:128] * gram[:128, :128], 0.0))
        lows.append(jnp.where(r2 > c2, p[128:] * gram[128:, 128:], 0.0))
        crosses.append(p[128:] * gram[128:, :128])
        rights.append(jnp.concatenate([p * kf, bs * v.astype(f32)], axis=1))
    invs = unit_lower_inverses(lows)
    y1 = [dot3(invs[2 * h], rights[h][:128]) for h in hs]
    rest = [rights[h][128:] - dot3(crosses[h], y1[h]) for h in hs]
    y2 = [dot3(invs[2 * h + 1], rest[h]) for h in hs]
    ys = [split(jnp.concatenate([y1[h], y2[h]], 0)) for h in hs]
    kys = [mm_tn(keys[h], ys[h][0]) + mm_tn(keys[h], ys[h][1]) for h in hs]
    return ys, [(eye - ky[:, :D], ky[:, D:]) for ky in kys]


def local_outputs(queries, keys, ys):
    vis = lax.broadcasted_iota(jnp.int32, (T, N), 1) <= 2 * lax.broadcasted_iota(jnp.int32, (T, N), 0) + 1
    scores = [split(jnp.where(vis, mm_nt(q, k), 0.0)) for q, k in zip(queries, keys)]
    sys_ = [dot3s(*s, *y) for s, y in zip(scores, ys)]
    return [(q.astype(f32) - sy[:, :D], sy[:, D:]) for q, sy in zip(queries, sys_)]


def compose(late, early):
    joined = dot3(late[:, :D], early)
    return jnp.concatenate([joined[:, :D], joined[:, D:] + late[:, D:]], axis=1)


def advance(pair, state):
    return dot3(pair[:, :D], state) + pair[:, D:]


def states_kernel(
    k_ref, v_ref, q_ref, b_ref, gain_ref, qo_ref, m_ref, gains_ref,
    pool, chip, row_in, row_pre, row_tot, low_in, low_pre, low_tot,
    high_in, high_tot, y_in, start, low_out, low_state,
    row_out, chip_state, after, y_high, y_low, send, recv, near,
):
    seq, head = lax.axis_index("seq"), lax.axis_index("head")
    x, c = head // 2, head % 2
    y, g, l = seq // (NG * NL), (seq // NL) % NG, seq % NL
    oc = 1 - c

    def meet(gg):
        return 2 - c + (((gg + 1) // 2) % 2) * (2 * c - 1)

    hub = meet(g)
    is_hub = l == hub

    def device(xx=None, cc=None, yy=None, gg=None, ll=None):
        xx, cc = x if xx is None else xx, c if cc is None else cc
        yy, gg, ll = y if yy is None else yy, g if gg is None else gg, l if ll is None else ll
        return {"seq": (yy * NG + gg) * NL + ll, "head": xx * 2 + cc}

    partner = device(cc=oc)

    def remote(src, dst, s, r, where):
        return pltpu.make_async_remote_copy(
            src_ref=src, dst_ref=dst, send_sem=send.at[s], recv_sem=recv.at[r],
            device_id=where, device_id_type=MESH,
        )

    barrier = pltpu.get_barrier_semaphore()
    rows = [device(xx=(x + k) % NX) for k in (1, 2, 3)]

    def greet(peers):
        for peer in peers:
            pl.semaphore_signal(barrier, inc=1, device_id=peer, device_id_type=MESH)

    @pl.when(is_hub)
    def _():
        greet([device(ll=(l + k) % NL) for k in (1, 2, 3)])
        greet([device(xx=(x + k) % NX, cc=oc) for k in (0, 1, 2, 3)])
        greet([device(gg=(g + k) % NG, ll=meet((g + k) % NG)) for k in (1, 2, 3)])
        for k in (1, 2, 3):
            @pl.when(y >= k)
            def _():
                greet([device(yy=(y + NY - k) % NY)])

    @pl.when(l != hub)
    def _():
        greet(rows)

    @pl.when((l != hub) & (l != 3 - hub))
    def _():
        greet([partner])

    def near_met():
        @pl.when((l != hub) & (l != 3 - hub))
        def _():
            pl.semaphore_wait(barrier, 5)
            pl.semaphore_signal(near, inc=1, device_id=device(ll=hub), device_id_type=MESH)

        @pl.when(l == 3 - hub)
        def _():
            pl.semaphore_wait(barrier, 8)
            pl.semaphore_signal(near, inc=1, device_id=device(ll=hub), device_id_type=MESH)
            pl.semaphore_signal(near, inc=1, device_id=partner, device_id_type=MESH)

    gains_ref[head] = gain_ref[...]

    def gain_copy():
        return remote(gain_ref, gains_ref.at[head], GAIN, GAIN, partner)

    def gain_row_copy(k, there, origin):
        rows = gains_ref.at[pl.ds(2 * origin, 2)]
        return remote(rows, rows, GAIN_ROW + k, GAIN_ROW + origin, device(xx=there))

    def pair_copy(i):
        return remote(pool.at[oc, i], pool.at[2, i], PAIR + i, PAIR + i, partner)

    def row_copy(e, k, there, origin):
        return remote(
            chip.at[2 * there + e], row_in.at[e, origin], ROW + 4 * e + k, ROW + 4 * e + origin, device(xx=there)
        )

    def low_copy(e, there, origin):
        return remote(row_tot.at[e], low_in.at[e, origin], LOW + 4 * e, LOW + 4 * e + origin, device(ll=there))

    def high_copy(e, k, there, origin):
        return remote(
            low_tot.at[e], high_in.at[e, origin], HIGH + 4 * e + k, HIGH + 4 * e + origin,
            device(gg=there, ll=meet(there)),
        )

    def y_copy(e, k, there, origin):
        return remote(high_tot.at[e], y_in.at[e, origin], YS + 4 * e + k, YS + 4 * e + origin, device(yy=there))

    def y_copy_first(e, k, there):
        part = pl.ds(D, D)
        return remote(
            high_tot.at[e, :, part], y_in.at[e, 0, :, part], YS + 4 * e + k, YS + 4 * e, device(yy=there)
        )

    def low_back(e, there):
        return remote(
            low_out.at[e, there], low_state.at[e], LOW_BACK + 4 * e + there, LOW_BACK + 4 * e, device(ll=there)
        )

    def row_back(e, k, there, origin):
        return remote(
            row_out.at[e, there], chip_state.at[2 * origin + e], ROW_BACK + 4 * e + k, ROW_BACK + 4 * e + origin,
            device(xx=there),
        )

    def back_copy(src, i):
        return remote(src.at[i], m_ref.at[8 * c + i], BACK + i, BACK + i, partner)

    def joint(parts, e, pre, tot):
        first = compose(parts[e, 1], parts[e, 0])
        last = compose(parts[e, 3], parts[e, 2])
        tot[e] = compose(last, first)
        pre[e, 0] = parts[e, 0]
        pre[e, 1] = first

    def third(parts, e, pre):
        pre[e, 2] = compose(parts[e, 2], pre[e, 1])

    def join_chip(e):
        for k in (2, 1, 3, 0):
            there = (x + k) % NX
            i = 2 * there + e
            pair_copy(i).wait_recv()
            joined = compose(pool[2 - c, i], pool[2 * c, i])
            if k:
                chip[i] = joined
                row_copy(e, k, there, x).start()
            else:
                row_in[e, x] = joined

    def up_row(e):
        for k in (1, 2, 3):
            origin = (x + k) % NX
            row_copy(e, 0, origin, origin).wait_recv()
        joint(row_in, e, row_pre, row_tot)

        @pl.when(l != hub)
        def _():
            low_copy(e, hub, l).start()

        @pl.when(is_hub)
        def _():
            low_in[e, l] = row_tot[e]

        third(row_in, e, row_pre)

    def up_low(e):
        @pl.when(is_hub)
        def _():
            for k in (1, 2, 3):
                origin = (l + k) % NL
                low_copy(e, origin, origin).wait_recv()
            joint(low_in, e, low_pre, low_tot)

            @pl.when(e == 0)
            def _():
                pl.semaphore_wait(barrier, 6 - y)

            for later in (True, False):
                for k in (1, 2, 3):
                    @pl.when((g + k < NG) == later)
                    def _():
                        high_copy(e, k, (g + k) % NG, g).start()
            high_in[e, g] = low_tot[e]
            third(low_in, e, low_pre)

    def high_wait(e, s):
        high_copy(e, 0, s, s).wait_recv()

    def through_hubs(e):
        @pl.when(is_hub)
        def _():
            for s in (0, 1, 2):
                @pl.when(g > s)
                def _():
                    high_wait(e, s)
                    high_tot[e] = high_in[e, 0] if s == 0 else compose(high_in[e, s], high_tot[e])

            start[e] = jnp.zeros((D, D), f32)

            @pl.when(y > 0)
            def _():
                y_copy_first(e, 0, 0).wait_recv()
                start[e] = y_in[e, 0, :, D:]

            for s in (1, 2):
                @pl.when(y > s)
                def _():
                    y_copy(e, 0, s, s).wait_recv()
                    start[e] = advance(y_in[e, s], start[e])

            @pl.when(g > 0)
            def _():
                start[e] = advance(high_tot[e], start[e])

            begin = start[e]
            for place in range(NL):
                low_out[e, place] = begin if place == 0 else advance(low_pre[e, place - 1], begin)

                @pl.when(l != place)
                def _():
                    low_back(e, place).start()

                @pl.when(l == place)
                def _():
                    low_state[e] = low_out[e, place]

            for s in range(NG):
                @pl.when(s > g)
                def _():
                    high_wait(e, s)

                @pl.when((s >= g) & (y < NY - 1))
                def _():
                    high_tot[e] = high_in[e, 0] if s == 0 else compose(high_in[e, s], high_tot[e])

            for k in (1, 2, 3):
                @pl.when(y == 0)
                def _():
                    y_copy_first(e, k, k).start()

                @pl.when((y > 0) & (y + k < NY))
                def _():
                    y_copy(e, k, (y + k) % NY, y).start()

    def down_row(e):
        @pl.when(l != hub)
        def _():
            low_back(e, hub).wait_recv()
        begin = low_state[e]
        for place in range(NX):
            row_out[e, place] = begin if place == 0 else advance(row_pre[e, place - 1], begin)
        for k in (2, 1, 3):
            row_back(e, k, (x + k) % NX, x).start()
        chip_state[2 * x + e] = row_out[e, x]

    def down_chip(e):
        for k in (0, 1, 3, 2):
            origin = (x + k) % NX
            i = 2 * origin + e
            if k:
                row_back(e, 0, origin, origin).wait_recv()

            @pl.when(c == 1)
            def _():
                back_copy(chip_state, i).start()

            begin = chip_state[i]
            end = advance(pool[2 * c, i], begin)

            @pl.when(c == 0)
            def _():
                after[i] = end
                back_copy(after, i).start()
                m_ref[i] = begin

            @pl.when(c == 1)
            def _():
                m_ref[8 + i] = end

    lane = lax.broadcasted_iota(jnp.int32, (N, HEADS), 1)

    def turn(t):
        e, half = t // 2, t % 2
        here = [2 * v + e for v in range(NX)]
        betas = [
            jnp.sum(jnp.where(lane == 8 * half + i, b_ref[...], 0.0), axis=1, keepdims=True) for i in here
        ]
        keys = [k_ref[8 * half + i] for i in here]
        ys, maps = local_solves(keys, [v_ref[8 * half + i] for i in here], betas)
        for i, (a_part, b_part), (hi, lo) in zip(here, maps, ys):
            pool[half, i, :, :D] = a_part
            pool[half, i, :, D:] = b_part
            y_high[8 * half + i] = hi
            y_low[8 * half + i] = lo

        @pl.when(t == 0)
        def _():
            near_met()

        @pl.when((t == 1) & is_hub)
        def _():
            pl.semaphore_wait(near, 4)

        @pl.when((t == 1) & is_hub & (c == 1))
        def _():
            for v in range(NX):
                pair_copy(2 * v).start()

        @pl.when((half != c) & ((t > 0) | (l != hub)))
        def _():
            for i in here:
                pair_copy(i).start()

        @pl.when(t == 1)
        def _():
            gain_copy().start()

    def local_out(first):
        here = [first + 2 * v for v in range(NX)]
        outs = local_outputs(
            [q_ref[h] for h in here], [k_ref[h] for h in here], [(y_high[h], y_low[h]) for h in here]
        )
        for h, (q_part, o_part) in zip(here, outs):
            qo_ref[h, :, :D] = q_part
            qo_ref[h, :, D:] = o_part

    def slot(it, carry):
        @pl.when(it < 4)
        def _():
            turn(it)

        @pl.when(it == 4)
        def _():
            remote(gain_ref, gains_ref.at[2 * x + oc], GAIN, GAIN, partner).wait_recv()
            for k in (1, 2, 3):
                gain_row_copy(k, (x + k) % NX, x).start()

        @pl.when((it == 1 + c) | (it == 3 + c))
        def _():
            join_chip((it - 1 - c) // 2)

        @pl.when((it == 2 + c) | (it == 4))
        def _():
            up_row(it // 4)

        @pl.when((it == 3 + c) | (it == 5))
        def _():
            up_low(it // 5)

        @pl.when((it == 5) | (it == 6))
        def _():
            through_hubs(it - 5)
            down_row(it - 5)

        @pl.when(it > 6)
        def _():
            down_chip(it - 7)

        @pl.when((it > 3) & (it < 8))
        def _():
            local_out(8 * ((it - 4) // 2) + (it - 4) % 2)

        return carry

    lax.fori_loop(0, 9, slot, 0)
    for i in range(8):
        remote(after.at[i], m_ref.at[8 * oc + i], BACK + i, BACK + i, partner).wait_recv()
    for k in (1, 2, 3):
        origin = (x + k) % NX
        gain_row_copy(k, origin, origin).wait_recv()

    gain_copy().wait_send()
    for k in (1, 2, 3):
        gain_row_copy(k, (x + k) % NX, x).wait_send()
    for i in range(8):
        pair_copy(i).wait_send()
        back_copy(after, i).wait_send()
    for e in range(2):
        for k in (1, 2, 3):
            row_copy(e, k, (x + k) % NX, x).wait_send()
            row_back(e, k, (x + k) % NX, x).wait_send()

        @pl.when(l != hub)
        def _():
            low_copy(e, hub, l).wait_send()

        @pl.when(is_hub)
        def _():
            for place in range(NL):
                @pl.when(l != place)
                def _():
                    low_back(e, place).wait_send()
            for k in (1, 2, 3):
                high_copy(e, k, (g + k) % NG, g).wait_send()

                @pl.when(y == 0)
                def _():
                    y_copy_first(e, k, k).wait_send()

                @pl.when((y > 0) & (y + k < NY))
                def _():
                    y_copy(e, k, (y + k) % NY, y).wait_send()


def states(keys, values, queries, betas, gain):
    wide, square = (D, 2 * D), (D, D)
    whole = pl.BlockSpec(memory_space=pltpu.VMEM)

    def vm(*shape):
        return pltpu.VMEM(shape, f32)

    return pl.pallas_call(
        states_kernel,
        in_specs=[whole] * 5,
        out_specs=[whole] * 3,
        out_shape=[
            jax.ShapeDtypeStruct((HEADS, T, 2 * D), f32),
            jax.ShapeDtypeStruct((HEADS, D, D), f32),
            jax.ShapeDtypeStruct((8, 2, D), f32),
        ],
        scratch_shapes=[
            vm(3, 8, *wide), vm(8, *wide),
            vm(2, NX, *wide), vm(2, 3, *wide), vm(2, *wide),
            vm(2, NL, *wide), vm(2, 3, *wide), vm(2, *wide),
            vm(2, NG, *wide), vm(2, *wide),
            vm(2, NY, *wide), vm(2, *square), vm(2, NL, *square), vm(2, *square),
            vm(2, NX, *square), vm(8, *square), vm(8, *square),
            pltpu.VMEM((HEADS, N, 2 * D), bf16), pltpu.VMEM((HEADS, N, 2 * D), bf16),
            pltpu.SemaphoreType.DMA((SEMS,)), pltpu.SemaphoreType.DMA((SEMS,)), pltpu.SemaphoreType.REGULAR,
        ],
        compiler_params=pltpu.CompilerParams(
            collective_id=0, has_side_effects=True, vmem_limit_bytes=48 * 2**20
        ),
    )(keys, values, queries, betas, gain)


def by_head_kernel(k_ref, v_ref, q_ref, ko_ref, vo_ref, qo_ref, held, sem, q_sem):
    fetch = pltpu.make_async_copy(q_ref, held, q_sem)
    fetch.start()
    copies = [
        pltpu.make_async_copy(src.at[:, h], dst.at[h], sem.at[n, h])
        for h in range(HEADS)
        for n, (src, dst) in enumerate(((k_ref, ko_ref), (v_ref, vo_ref)))
    ]
    for copy in copies:
        copy.start()
    fetch.wait()
    qo_ref[...] = jnp.swapaxes(held[...].astype(f32), 0, 1).astype(bf16)
    for copy in copies:
        copy.wait()


def by_head(keys, values, queries):
    whole, away = pl.BlockSpec(memory_space=pltpu.VMEM), pl.BlockSpec(memory_space=pl.ANY)
    pairs = jax.ShapeDtypeStruct((HEADS, T, 2, D), bf16)
    k, v, q = pl.pallas_call(
        by_head_kernel,
        in_specs=[away] * 3,
        out_specs=[whole] * 3,
        out_shape=[pairs, pairs, jax.ShapeDtypeStruct((HEADS, T, D), bf16)],
        scratch_shapes=[
            pltpu.VMEM((T, HEADS, D), bf16), pltpu.SemaphoreType.DMA((2, HEADS)), pltpu.SemaphoreType.DMA,
        ],
        compiler_params=pltpu.CompilerParams(vmem_limit_bytes=50 * 2**20),
    )(keys, values, queries)
    return k.reshape(HEADS, N, D), v.reshape(HEADS, N, D), q


def output_kernel(qo_ref, m_ref, gains_ref, gate_ref, out_ref, rows):
    for h in range(HEADS):
        r = dot3(qo_ref[h, :, :D], m_ref[h]) + qo_ref[h, :, D:]
        scale = lax.rsqrt(jnp.mean(r * r, axis=-1, keepdims=True) + 1e-6)
        rows[h] = r * scale * gains_ref[h // 2, h % 2 : h % 2 + 1, :]
    gate = gate_ref[...].astype(f32)
    normed = jnp.swapaxes(rows[...], 0, 1)
    out_ref[...] = (normed * (gate / (1.0 + jnp.exp(-gate)))).astype(bf16)


def outputs(qo, m, gains, gate):
    whole = pl.BlockSpec(memory_space=pltpu.VMEM)
    return pl.pallas_call(
        output_kernel,
        in_specs=[whole] * 4,
        out_specs=whole,
        out_shape=jax.ShapeDtypeStruct((T, HEADS, D), bf16),
        scratch_shapes=[pltpu.VMEM((HEADS, T, D), f32)],
        compiler_params=pltpu.CompilerParams(vmem_limit_bytes=48 * 2**20),
    )(qo, m, gains, gate)


def local(queries, keys, values, betas, gate, gain):
    keys_h, values_h, queries_h = by_head(keys, values, queries)
    betas_h = jnp.transpose(betas, (0, 2, 1)).reshape(N, HEADS).astype(f32)
    qo, m, gains = states(keys_h, values_h, queries_h, betas_h, gain)
    return outputs(qo, m, gains, gate)


def solution(mesh):
    return jax.shard_map(
        local,
        mesh=mesh,
        in_specs=(
            P(("seq", "head"), None, None),
            P(("seq", "head"), None, None, None),
            P(("seq", "head"), None, None, None),
            P(("seq", "head"), None, None),
            P(("seq", "head"), None, None),
            P("head", None),
        ),
        out_specs=P(("seq", "head"), None, None),
        check_vma=False,
    )
```

```python
import functools
import jax, jax.numpy as jnp
from jax import lax
from jax.experimental import pallas as pl
from jax.experimental.pallas import tpu as pltpu
from jax.sharding import PartitionSpec as P
f32, bf16 = jnp.float32, jnp.bfloat16
D = 128
N = 256
T = 128
BASE = 16

def split(a):
    hi = a.astype(bf16)
    return hi, (a - hi.astype(f32)).astype(bf16)

def mm(a, b):
    return lax.dot_general(a, b, (((1,), (0,)), ((), ())), preferred_element_type=f32)

def mm_nt(a, b):
    return lax.dot_general(a, b, (((1,), (1,)), ((), ())), preferred_element_type=f32)

def mm_tn(a, b):
    return lax.dot_general(a, b, (((0,), (0,)), ((), ())), preferred_element_type=f32)

def dot3(a, b):
    ah, al = split(a)
    bh, bl = split(b)
    return dot3s(ah, al, bh, bl)

def dot3s(ah, al, bh, bl):
    if ah.shape[1] == 128:
        return mm(jnp.concatenate([ah, al], 1), jnp.concatenate([bh, bh], 0)) + mm(ah, bl)
    return mm(ah, bh) + (mm(al, bh) + mm(ah, bl))

def unit_lower_inverses(lows):
    n = len(lows)
    lane = lax.broadcasted_iota(jnp.int32, (BASE, 128), 1)
    row = lax.broadcasted_iota(jnp.int32, (BASE, 128), 0)
    blk = lane // BASE
    half = BASE // 2
    upper, lower = [], []
    for low in lows:
        z = jnp.zeros((BASE, 128), f32)
        for b in range(128 // BASE):
            z = jnp.where(blk == b, low[BASE * b:BASE * (b + 1), :], z)
        z = jnp.where(row > lane % BASE, z, 0.0)
        upper.append(z[:half])
        lower.append(z[half:])
    eye = jnp.where(row == lane % BASE, 1.0, 0.0).astype(f32)
    tops, ends = [eye[:half] for _ in lows], [eye[half:] for _ in lows]
    blk = blk[:half]
    for j in range(BASE - 1):
        idx = blk * BASE + j
        for i in range(n):
            pivot = tops[i][j:j + 1, :] if j < half else ends[i][j - half:j - half + 1, :]
            ends[i] = ends[i] - jnp.take_along_axis(lower[i], idx, axis=1, mode="promise_in_bounds") * pivot
            if j < half - 1:
                tops[i] = tops[i] - jnp.take_along_axis(upper[i], idx, axis=1, mode="promise_in_bounds") * pivot
    xs = [jnp.concatenate([top, end], 0) for top, end in zip(tops, ends)]
    blk = lane // BASE
    fulls = []
    for x in xs:
        fulls.append(jnp.concatenate([jnp.where(blk == b, x, 0.0) for b in range(128 // BASE)], axis=0))
    m = BASE
    r2 = lax.broadcasted_iota(jnp.int32, (128, 128), 0)
    c2 = lax.broadcasted_iota(jnp.int32, (128, 128), 1)
    while m < 128:
        offmask = ((r2 // m) % 2 == 1) & (c2 // m == r2 // m - 1)
        xos = [jnp.concatenate([x[m * (2 * b + 1):m * (2 * b + 2), :] for b in range(64 // m)], 0) for x in fulls]
        offs = [split(jnp.where(offmask, low, 0.0)) for low in lows]
        xos_s = [split(xo) for xo in xos]
        xs_s = [split(x) for x in fulls]
        ys = [dot3s(*xo, *off) for xo, off in zip(xos_s, offs)]
        ys = [split(y) for y in ys]
        zs = [xo - dot3s(*y, *x) for xo, y, x in zip(xos, ys, xs_s)]
        out = []
        for x, z in zip(fulls, zs):
            rows = []
            for b in range(64 // m):
                rows.append(x[m * 2 * b:m * (2 * b + 1), :])
                rows.append(z[m * b:m * (b + 1), :])
            out.append(jnp.concatenate(rows, 0))
        fulls = out
        m *= 2
    return fulls

MESH = pl.DeviceIdType.MESH
HEADS = 16
NX, NL, NG, NY = 4, 4, 4, 4
PAIR, ROW, LOW, HIGH, YS, LOW_BACK, ROW_BACK, BACK, GAIN, GAIN_ROW, SEMS = 0, 8, 16, 24, 32, 40, 48, 56, 64, 65, 69


def local_solves(keys, values, betas):
    hs = range(len(keys))
    r2 = lax.broadcasted_iota(jnp.int32, (128, 128), 0)
    c2 = lax.broadcasted_iota(jnp.int32, (128, 128), 1)
    eye = jnp.where(r2 == c2, 1.0, 0.0).astype(f32)
    lows, crosses, rights = [], [], []
    for k, v, beta in zip(keys, values, betas):
        kf = k.astype(f32)
        ssq = jnp.sum(kf * kf, axis=1, keepdims=True) + 1e-6
        p = beta / ssq
        bs = beta * lax.rsqrt(ssq)
        gram = mm_nt(k, k)
        lows.append(jnp.where(r2 > c2, p[:128] * gram[:128, :128], 0.0))
        lows.append(jnp.where(r2 > c2, p[128:] * gram[128:, 128:], 0.0))
        crosses.append(p[128:] * gram[128:, :128])
        rights.append(jnp.concatenate([p * kf, bs * v.astype(f32)], axis=1))
    invs = unit_lower_inverses(lows)
    y1 = [dot3(invs[2 * h], rights[h][:128]) for h in hs]
    rest = [rights[h][128:] - dot3(crosses[h], y1[h]) for h in hs]
    y2 = [dot3(invs[2 * h + 1], rest[h]) for h in hs]
    ys = [split(jnp.concatenate([y1[h], y2[h]], 0)) for h in hs]
    kys = [mm_tn(keys[h], ys[h][0]) + mm_tn(keys[h], ys[h][1]) for h in hs]
    return ys, [(eye - ky[:, :D], ky[:, D:]) for ky in kys]


def local_outputs(queries, keys, ys):
    vis = lax.broadcasted_iota(jnp.int32, (T, N), 1) <= 2 * lax.broadcasted_iota(jnp.int32, (T, N), 0) + 1
    scores = [split(jnp.where(vis, mm_nt(q, k), 0.0)) for q, k in zip(queries, keys)]
    sys_ = [dot3s(*s, *y) for s, y in zip(scores, ys)]
    return [(q.astype(f32) - sy[:, :D], sy[:, D:]) for q, sy in zip(queries, sys_)]


def compose(late, early):
    joined = dot3(late[:, :D], early)
    return jnp.concatenate([joined[:, :D], joined[:, D:] + late[:, D:]], axis=1)


def advance(pair, state):
    return dot3(pair[:, :D], state) + pair[:, D:]


def states_kernel(
    k_ref, v_ref, q_ref, b_ref, gain_ref, qo_ref, m_ref, gains_ref,
    pool, chip, row_in, row_pre, row_tot, low_in, low_pre, low_tot,
    high_in, high_tot, y_in, row_end, start, low_out, low_state,
    row_out, chip_state, after, y_high, y_low, send, recv, near,
):
    seq, head = lax.axis_index("seq"), lax.axis_index("head")
    x, c = head // 2, head % 2
    y, g, l = seq // (NG * NL), (seq // NL) % NG, seq % NL
    oc = 1 - c

    def meet(gg):
        return 2 - c + (((gg + 1) // 2) % 2) * (2 * c - 1)

    hub = meet(g)
    is_hub = l == hub

    def device(xx=None, cc=None, yy=None, gg=None, ll=None):
        xx, cc = x if xx is None else xx, c if cc is None else cc
        yy, gg, ll = y if yy is None else yy, g if gg is None else gg, l if ll is None else ll
        return {"seq": (yy * NG + gg) * NL + ll, "head": xx * 2 + cc}

    partner = device(cc=oc)

    def remote(src, dst, s, r, where):
        return pltpu.make_async_remote_copy(
            src_ref=src, dst_ref=dst, send_sem=send.at[s], recv_sem=recv.at[r],
            device_id=where, device_id_type=MESH,
        )

    barrier = pltpu.get_barrier_semaphore()
    rows = [device(xx=(x + k) % NX) for k in (1, 2, 3)]

    def greet(peers):
        for peer in peers:
            pl.semaphore_signal(barrier, inc=1, device_id=peer, device_id_type=MESH)

    @pl.when(is_hub)
    def _():
        greet([device(ll=(l + k) % NL) for k in (1, 2, 3)])
        greet([device(xx=(x + k) % NX, cc=oc) for k in (0, 1, 2, 3)])
        greet([device(gg=(g + k) % NG, ll=meet((g + k) % NG)) for k in (1, 2, 3)])

        @pl.when(y > 0)
        def _():
            greet([device(yy=(y + NY - 1) % NY)])

    @pl.when(l != hub)
    def _():
        greet(rows)

    @pl.when((l != hub) & (l != 3 - hub))
    def _():
        greet([partner])

    def near_met():
        @pl.when((l != hub) & (l != 3 - hub))
        def _():
            pl.semaphore_wait(barrier, 5)
            pl.semaphore_signal(near, inc=1, device_id=device(ll=hub), device_id_type=MESH)

        @pl.when(l == 3 - hub)
        def _():
            pl.semaphore_wait(barrier, 8)
            pl.semaphore_signal(near, inc=1, device_id=device(ll=hub), device_id_type=MESH)
            pl.semaphore_signal(near, inc=1, device_id=partner, device_id_type=MESH)

    gains_ref[head] = gain_ref[...]

    def gain_copy():
        return remote(gain_ref, gains_ref.at[head], GAIN, GAIN, partner)

    def gain_row_copy(k, there, origin):
        rows = gains_ref.at[pl.ds(2 * origin, 2)]
        return remote(rows, rows, GAIN_ROW + k, GAIN_ROW + origin, device(xx=there))

    def pair_copy(i):
        return remote(pool.at[oc, i], pool.at[2, i], PAIR + i, PAIR + i, partner)

    def row_copy(e, k, there, origin):
        return remote(
            chip.at[2 * there + e], row_in.at[e, origin], ROW + 4 * e + k, ROW + 4 * e + origin, device(xx=there)
        )

    def low_copy(e, there, origin):
        return remote(row_tot.at[e], low_in.at[e, origin], LOW + 4 * e, LOW + 4 * e + origin, device(ll=there))

    def high_copy(e, k, there, origin):
        return remote(
            low_tot.at[e], high_in.at[e, origin], HIGH + 4 * e + k, HIGH + 4 * e + origin,
            device(gg=there, ll=meet(there)),
        )

    def y_copy(e, there):
        return remote(row_end.at[e], y_in.at[e], YS + e, YS + e, device(yy=there))

    def low_back(e, there):
        return remote(
            low_out.at[e, there], low_state.at[e], LOW_BACK + 4 * e + there, LOW_BACK + 4 * e, device(ll=there)
        )

    def row_back(e, k, there, origin):
        return remote(
            row_out.at[e, there], chip_state.at[2 * origin + e], ROW_BACK + 4 * e + k, ROW_BACK + 4 * e + origin,
            device(xx=there),
        )

    def back_copy(src, i):
        return remote(src.at[i], m_ref.at[8 * c + i], BACK + i, BACK + i, partner)

    def joint(parts, e, pre, tot):
        first = compose(parts[e, 1], parts[e, 0])
        last = compose(parts[e, 3], parts[e, 2])
        tot[e] = compose(last, first)
        pre[e, 0] = parts[e, 0]
        pre[e, 1] = first

    def third(parts, e, pre):
        pre[e, 2] = compose(parts[e, 2], pre[e, 1])

    def join_chip(e):
        for k in (2, 1, 3, 0):
            there = (x + k) % NX
            i = 2 * there + e
            pair_copy(i).wait_recv()
            joined = compose(pool[2 - c, i], pool[2 * c, i])
            if k:
                chip[i] = joined
                row_copy(e, k, there, x).start()
            else:
                row_in[e, x] = joined

    def up_row(e):
        for k in (1, 2, 3):
            origin = (x + k) % NX
            row_copy(e, 0, origin, origin).wait_recv()
        joint(row_in, e, row_pre, row_tot)

        @pl.when(l != hub)
        def _():
            low_copy(e, hub, l).start()

        @pl.when(is_hub)
        def _():
            low_in[e, l] = row_tot[e]

        third(row_in, e, row_pre)

    def up_low(e):
        @pl.when(is_hub)
        def _():
            for k in (1, 2, 3):
                origin = (l + k) % NL
                low_copy(e, origin, origin).wait_recv()
            joint(low_in, e, low_pre, low_tot)

            @pl.when(e == 0)
            def _():
                pl.semaphore_wait(barrier, 4 - y // (NY - 1))

            for later in (True, False):
                for k in (1, 2, 3):
                    @pl.when((g + k < NG) == later)
                    def _():
                        high_copy(e, k, (g + k) % NG, g).start()
            high_in[e, g] = low_tot[e]
            third(low_in, e, low_pre)

    def high_wait(e, s):
        high_copy(e, 0, s, s).wait_recv()

    def through_hubs(e):
        @pl.when(is_hub)
        def _():
            for s in (0, 1, 2):
                @pl.when(g > s)
                def _():
                    high_wait(e, s)
                    high_tot[e] = high_in[e, 0] if s == 0 else compose(high_in[e, s], high_tot[e])

            start[e] = jnp.zeros((D, D), f32)

            @pl.when(y > 0)
            def _():
                y_copy(e, (y + NY - 1) % NY).wait_recv()
                start[e] = y_in[e]

            @pl.when(g > 0)
            def _():
                start[e] = advance(high_tot[e], start[e])

            begin = start[e]
            for place in range(NL):
                low_out[e, place] = begin if place == 0 else advance(low_pre[e, place - 1], begin)

                @pl.when(l != place)
                def _():
                    low_back(e, place).start()

                @pl.when(l == place)
                def _():
                    low_state[e] = low_out[e, place]

            row_end[e] = begin
            for s in range(NG):
                @pl.when(s > g)
                def _():
                    high_wait(e, s)

                @pl.when((s >= g) & (y < NY - 1))
                def _():
                    row_end[e] = advance(high_in[e, s], row_end[e])

            @pl.when(y < NY - 1)
            def _():
                y_copy(e, (y + 1) % NY).start()

    def down_row(e):
        @pl.when(l != hub)
        def _():
            low_back(e, hub).wait_recv()
        begin = low_state[e]
        for place in range(NX):
            row_out[e, place] = begin if place == 0 else advance(row_pre[e, place - 1], begin)
        for k in (2, 1, 3):
            row_back(e, k, (x + k) % NX, x).start()
        chip_state[2 * x + e] = row_out[e, x]

    def down_chip(e):
        for k in (0, 1, 3, 2):
            origin = (x + k) % NX
            i = 2 * origin + e
            if k:
                row_back(e, 0, origin, origin).wait_recv()

            @pl.when(c == 1)
            def _():
                back_copy(chip_state, i).start()

            begin = chip_state[i]
            end = advance(pool[2 * c, i], begin)

            @pl.when(c == 0)
            def _():
                after[i] = end
                back_copy(after, i).start()
                m_ref[i] = begin

            @pl.when(c == 1)
            def _():
                m_ref[8 + i] = end

    lane = lax.broadcasted_iota(jnp.int32, (N, HEADS), 1)

    def turn(t):
        e, half = t // 2, t % 2
        here = [2 * v + e for v in range(NX)]
        betas = [
            jnp.sum(jnp.where(lane == 8 * half + i, b_ref[...], 0.0), axis=1, keepdims=True) for i in here
        ]
        keys = [k_ref[8 * half + i] for i in here]
        ys, maps = local_solves(keys, [v_ref[8 * half + i] for i in here], betas)
        for i, (a_part, b_part), (hi, lo) in zip(here, maps, ys):
            pool[half, i, :, :D] = a_part
            pool[half, i, :, D:] = b_part
            y_high[8 * half + i] = hi
            y_low[8 * half + i] = lo

        @pl.when(t == 0)
        def _():
            near_met()

        @pl.when((t == 1) & is_hub)
        def _():
            pl.semaphore_wait(near, 4)

        @pl.when((t == 1) & is_hub & (c == 1))
        def _():
            for v in range(NX):
                pair_copy(2 * v).start()

        @pl.when((half != c) & ((t > 0) | (l != hub)))
        def _():
            for i in here:
                pair_copy(i).start()

        @pl.when(t == 1)
        def _():
            gain_copy().start()

    def local_out(first):
        here = [first + 2 * v for v in range(NX)]
        outs = local_outputs(
            [q_ref[h] for h in here], [k_ref[h] for h in here], [(y_high[h], y_low[h]) for h in here]
        )
        for h, (q_part, o_part) in zip(here, outs):
            qo_ref[h, :, :D] = q_part
            qo_ref[h, :, D:] = o_part

    def slot(it, carry):
        @pl.when(it < 4)
        def _():
            turn(it)

        @pl.when(it == 4)
        def _():
            remote(gain_ref, gains_ref.at[2 * x + oc], GAIN, GAIN, partner).wait_recv()
            for k in (1, 2, 3):
                gain_row_copy(k, (x + k) % NX, x).start()

        @pl.when((it == 1 + c) | (it == 3 + c))
        def _():
            join_chip((it - 1 - c) // 2)

        @pl.when((it == 2 + c) | (it == 4))
        def _():
            up_row(it // 4)

        @pl.when((it == 3 + c) | (it == 5))
        def _():
            up_low(it // 5)

        @pl.when((it == 5) | (it == 6))
        def _():
            through_hubs(it - 5)
            down_row(it - 5)

        @pl.when(it > 6)
        def _():
            down_chip(it - 7)

        @pl.when((it > 3) & (it < 8))
        def _():
            local_out(8 * ((it - 4) // 2) + (it - 4) % 2)

        return carry

    lax.fori_loop(0, 9, slot, 0)
    for i in range(8):
        remote(after.at[i], m_ref.at[8 * oc + i], BACK + i, BACK + i, partner).wait_recv()
    for k in (1, 2, 3):
        origin = (x + k) % NX
        gain_row_copy(k, origin, origin).wait_recv()

    gain_copy().wait_send()
    for k in (1, 2, 3):
        gain_row_copy(k, (x + k) % NX, x).wait_send()
    for i in range(8):
        pair_copy(i).wait_send()
        back_copy(after, i).wait_send()
    for e in range(2):
        for k in (1, 2, 3):
            row_copy(e, k, (x + k) % NX, x).wait_send()
            row_back(e, k, (x + k) % NX, x).wait_send()

        @pl.when(l != hub)
        def _():
            low_copy(e, hub, l).wait_send()

        @pl.when(is_hub)
        def _():
            for place in range(NL):
                @pl.when(l != place)
                def _():
                    low_back(e, place).wait_send()
            for k in (1, 2, 3):
                high_copy(e, k, (g + k) % NG, g).wait_send()

            @pl.when(y < NY - 1)
            def _():
                y_copy(e, (y + 1) % NY).wait_send()


def states(keys, values, queries, betas, gain):
    wide, square = (D, 2 * D), (D, D)
    whole = pl.BlockSpec(memory_space=pltpu.VMEM)

    def vm(*shape):
        return pltpu.VMEM(shape, f32)

    return pl.pallas_call(
        states_kernel,
        in_specs=[whole] * 5,
        out_specs=[whole] * 3,
        out_shape=[
            jax.ShapeDtypeStruct((HEADS, T, 2 * D), f32),
            jax.ShapeDtypeStruct((HEADS, D, D), f32),
            jax.ShapeDtypeStruct((8, 2, D), f32),
        ],
        scratch_shapes=[
            vm(3, 8, *wide), vm(8, *wide),
            vm(2, NX, *wide), vm(2, 3, *wide), vm(2, *wide),
            vm(2, NL, *wide), vm(2, 3, *wide), vm(2, *wide),
            vm(2, NG, *wide), vm(2, *wide),
            vm(2, *square), vm(2, *square), vm(2, *square), vm(2, NL, *square), vm(2, *square),
            vm(2, NX, *square), vm(8, *square), vm(8, *square),
            pltpu.VMEM((HEADS, N, 2 * D), bf16), pltpu.VMEM((HEADS, N, 2 * D), bf16),
            pltpu.SemaphoreType.DMA((SEMS,)), pltpu.SemaphoreType.DMA((SEMS,)), pltpu.SemaphoreType.REGULAR,
        ],
        compiler_params=pltpu.CompilerParams(
            collective_id=0, has_side_effects=True, vmem_limit_bytes=48 * 2**20
        ),
    )(keys, values, queries, betas, gain)


def by_head_kernel(k_ref, v_ref, q_ref, ko_ref, vo_ref, qo_ref, held, sem, q_sem):
    fetch = pltpu.make_async_copy(q_ref, held, q_sem)
    fetch.start()
    copies = [
        pltpu.make_async_copy(src.at[:, h], dst.at[h], sem.at[n, h])
        for h in range(HEADS)
        for n, (src, dst) in enumerate(((k_ref, ko_ref), (v_ref, vo_ref)))
    ]
    for copy in copies:
        copy.start()
    fetch.wait()
    qo_ref[...] = jnp.swapaxes(held[...].astype(f32), 0, 1).astype(bf16)
    for copy in copies:
        copy.wait()


def by_head(keys, values, queries):
    whole, away = pl.BlockSpec(memory_space=pltpu.VMEM), pl.BlockSpec(memory_space=pl.ANY)
    pairs = jax.ShapeDtypeStruct((HEADS, T, 2, D), bf16)
    k, v, q = pl.pallas_call(
        by_head_kernel,
        in_specs=[away] * 3,
        out_specs=[whole] * 3,
        out_shape=[pairs, pairs, jax.ShapeDtypeStruct((HEADS, T, D), bf16)],
        scratch_shapes=[
            pltpu.VMEM((T, HEADS, D), bf16), pltpu.SemaphoreType.DMA((2, HEADS)), pltpu.SemaphoreType.DMA,
        ],
        compiler_params=pltpu.CompilerParams(vmem_limit_bytes=50 * 2**20),
    )(keys, values, queries)
    return k.reshape(HEADS, N, D), v.reshape(HEADS, N, D), q


def output_kernel(qo_ref, m_ref, gains_ref, gate_ref, out_ref, rows):
    for h in range(HEADS):
        r = dot3(qo_ref[h, :, :D], m_ref[h]) + qo_ref[h, :, D:]
        scale = lax.rsqrt(jnp.mean(r * r, axis=-1, keepdims=True) + 1e-6)
        rows[h] = r * scale * gains_ref[h // 2, h % 2 : h % 2 + 1, :]
    gate = gate_ref[...].astype(f32)
    normed = jnp.swapaxes(rows[...], 0, 1)
    out_ref[...] = (normed * (gate / (1.0 + jnp.exp(-gate)))).astype(bf16)


def outputs(qo, m, gains, gate):
    whole = pl.BlockSpec(memory_space=pltpu.VMEM)
    return pl.pallas_call(
        output_kernel,
        in_specs=[whole] * 4,
        out_specs=whole,
        out_shape=jax.ShapeDtypeStruct((T, HEADS, D), bf16),
        scratch_shapes=[pltpu.VMEM((HEADS, T, D), f32)],
        compiler_params=pltpu.CompilerParams(vmem_limit_bytes=48 * 2**20),
    )(qo, m, gains, gate)


def local(queries, keys, values, betas, gate, gain):
    keys_h, values_h, queries_h = by_head(keys, values, queries)
    betas_h = jnp.transpose(betas, (0, 2, 1)).reshape(N, HEADS).astype(f32)
    qo, m, gains = states(keys_h, values_h, queries_h, betas_h, gain)
    return outputs(qo, m, gains, gate)


def solution(mesh):
    return jax.shard_map(
        local,
        mesh=mesh,
        in_specs=(
            P(("seq", "head"), None, None),
            P(("seq", "head"), None, None, None),
            P(("seq", "head"), None, None, None),
            P(("seq", "head"), None, None),
            P(("seq", "head"), None, None),
            P("head", None),
        ),
        out_specs=P(("seq", "head"), None, None),
        check_vma=False,
    )
```

```python
import functools
import jax, jax.numpy as jnp
from jax import lax
from jax.experimental import pallas as pl
from jax.experimental.pallas import tpu as pltpu
from jax.sharding import PartitionSpec as P
f32, bf16 = jnp.float32, jnp.bfloat16
D = 128
N = 256
T = 128
BASE = 16

def split(a):
    hi = a.astype(bf16)
    return hi, (a - hi.astype(f32)).astype(bf16)

def mm(a, b):
    return lax.dot_general(a, b, (((1,), (0,)), ((), ())), preferred_element_type=f32)

def mm_nt(a, b):
    return lax.dot_general(a, b, (((1,), (1,)), ((), ())), preferred_element_type=f32)

def mm_tn(a, b):
    return lax.dot_general(a, b, (((0,), (0,)), ((), ())), preferred_element_type=f32)

def dot3(a, b):
    ah, al = split(a)
    bh, bl = split(b)
    return dot3s(ah, al, bh, bl)

def dot3s(ah, al, bh, bl):
    if ah.shape[1] == 128:
        return mm(jnp.concatenate([ah, al], 1), jnp.concatenate([bh, bh], 0)) + mm(ah, bl)
    return mm(ah, bh) + (mm(al, bh) + mm(ah, bl))

def unit_lower_inverses(lows):
    n = len(lows)
    lane = lax.broadcasted_iota(jnp.int32, (BASE, 128), 1)
    row = lax.broadcasted_iota(jnp.int32, (BASE, 128), 0)
    blk = lane // BASE
    half = BASE // 2
    upper, lower = [], []
    for low in lows:
        z = jnp.zeros((BASE, 128), f32)
        for b in range(128 // BASE):
            z = jnp.where(blk == b, low[BASE * b:BASE * (b + 1), :], z)
        z = jnp.where(row > lane % BASE, z, 0.0)
        upper.append(z[:half])
        lower.append(z[half:])
    eye = jnp.where(row == lane % BASE, 1.0, 0.0).astype(f32)
    tops, ends = [eye[:half] for _ in lows], [eye[half:] for _ in lows]
    blk = blk[:half]
    for j in range(BASE - 1):
        idx = blk * BASE + j
        for i in range(n):
            pivot = tops[i][j:j + 1, :] if j < half else ends[i][j - half:j - half + 1, :]
            ends[i] = ends[i] - jnp.take_along_axis(lower[i], idx, axis=1, mode="promise_in_bounds") * pivot
            if j < half - 1:
                tops[i] = tops[i] - jnp.take_along_axis(upper[i], idx, axis=1, mode="promise_in_bounds") * pivot
    xs = [jnp.concatenate([top, end], 0) for top, end in zip(tops, ends)]
    blk = lane // BASE
    fulls = []
    for x in xs:
        fulls.append(jnp.concatenate([jnp.where(blk == b, x, 0.0) for b in range(128 // BASE)], axis=0))
    m = BASE
    r2 = lax.broadcasted_iota(jnp.int32, (128, 128), 0)
    c2 = lax.broadcasted_iota(jnp.int32, (128, 128), 1)
    while m < 128:
        offmask = ((r2 // m) % 2 == 1) & (c2 // m == r2 // m - 1)
        xos = [jnp.concatenate([x[m * (2 * b + 1):m * (2 * b + 2), :] for b in range(64 // m)], 0) for x in fulls]
        offs = [split(jnp.where(offmask, low, 0.0)) for low in lows]
        xos_s = [split(xo) for xo in xos]
        xs_s = [split(x) for x in fulls]
        ys = [dot3s(*xo, *off) for xo, off in zip(xos_s, offs)]
        ys = [split(y) for y in ys]
        zs = [xo - dot3s(*y, *x) for xo, y, x in zip(xos, ys, xs_s)]
        out = []
        for x, z in zip(fulls, zs):
            rows = []
            for b in range(64 // m):
                rows.append(x[m * 2 * b:m * (2 * b + 1), :])
                rows.append(z[m * b:m * (b + 1), :])
            out.append(jnp.concatenate(rows, 0))
        fulls = out
        m *= 2
    return fulls

MESH = pl.DeviceIdType.MESH
HEADS = 16
NX, NL, NG, NY = 4, 4, 4, 4
PAIR, ROW, LOW, HIGH, YS, LOW_BACK, ROW_BACK, BACK, GAIN, GAIN_ROW, SEMS = 0, 8, 16, 24, 32, 40, 48, 56, 64, 65, 69


def local_solves(keys, values, betas):
    hs = range(len(keys))
    r2 = lax.broadcasted_iota(jnp.int32, (128, 128), 0)
    c2 = lax.broadcasted_iota(jnp.int32, (128, 128), 1)
    eye = jnp.where(r2 == c2, 1.0, 0.0).astype(f32)
    lows, crosses, rights = [], [], []
    for k, v, beta in zip(keys, values, betas):
        kf = k.astype(f32)
        ssq = jnp.sum(kf * kf, axis=1, keepdims=True) + 1e-6
        p = beta / ssq
        bs = beta * lax.rsqrt(ssq)
        gram = mm_nt(k, k)
        lows.append(jnp.where(r2 > c2, p[:128] * gram[:128, :128], 0.0))
        lows.append(jnp.where(r2 > c2, p[128:] * gram[128:, 128:], 0.0))
        crosses.append(p[128:] * gram[128:, :128])
        rights.append(jnp.concatenate([p * kf, bs * v.astype(f32)], axis=1))
    invs = unit_lower_inverses(lows)
    y1 = [dot3(invs[2 * h], rights[h][:128]) for h in hs]
    rest = [rights[h][128:] - dot3(crosses[h], y1[h]) for h in hs]
    y2 = [dot3(invs[2 * h + 1], rest[h]) for h in hs]
    ys = [split(jnp.concatenate([y1[h], y2[h]], 0)) for h in hs]
    kys = [mm_tn(keys[h], ys[h][0]) + mm_tn(keys[h], ys[h][1]) for h in hs]
    return ys, [(eye - ky[:, :D], ky[:, D:]) for ky in kys]


def local_outputs(queries, keys, ys):
    vis = lax.broadcasted_iota(jnp.int32, (T, N), 1) <= 2 * lax.broadcasted_iota(jnp.int32, (T, N), 0) + 1
    scores = [split(jnp.where(vis, mm_nt(q, k), 0.0)) for q, k in zip(queries, keys)]
    sys_ = [dot3s(*s, *y) for s, y in zip(scores, ys)]
    return [(q.astype(f32) - sy[:, :D], sy[:, D:]) for q, sy in zip(queries, sys_)]


def compose(late, early):
    joined = dot3(late[:, :D], early)
    return jnp.concatenate([joined[:, :D], joined[:, D:] + late[:, D:]], axis=1)


def advance(pair, state):
    return dot3(pair[:, :D], state) + pair[:, D:]


def states_kernel(
    k_ref, v_ref, q_ref, b_ref, gain_ref, qo_ref, m_ref, gains_ref,
    pool, chip, row_in, row_pre, row_tot, low_in, low_pre, low_tot,
    high_in, high_pre, high_tot, y_in, start, low_out, low_state,
    row_out, chip_state, after, y_high, y_low, send, recv, near,
):
    seq, head = lax.axis_index("seq"), lax.axis_index("head")
    x, c = head // 2, head % 2
    y, g, l = seq // (NG * NL), (seq // NL) % NG, seq % NL
    oc = 1 - c

    def meet(gg):
        return 2 - c + (((gg + 1) // 2) % 2) * (2 * c - 1)

    hub = meet(g)
    is_hub = l == hub

    def device(xx=None, cc=None, yy=None, gg=None, ll=None):
        xx, cc = x if xx is None else xx, c if cc is None else cc
        yy, gg, ll = y if yy is None else yy, g if gg is None else gg, l if ll is None else ll
        return {"seq": (yy * NG + gg) * NL + ll, "head": xx * 2 + cc}

    partner = device(cc=oc)

    def remote(src, dst, s, r, where):
        return pltpu.make_async_remote_copy(
            src_ref=src, dst_ref=dst, send_sem=send.at[s], recv_sem=recv.at[r],
            device_id=where, device_id_type=MESH,
        )

    barrier = pltpu.get_barrier_semaphore()
    rows = [device(xx=(x + k) % NX) for k in (1, 2, 3)]

    def greet(peers):
        for peer in peers:
            pl.semaphore_signal(barrier, inc=1, device_id=peer, device_id_type=MESH)

    @pl.when(is_hub)
    def _():
        greet([device(ll=(l + k) % NL) for k in (1, 2, 3)])
        greet([device(xx=(x + k) % NX, cc=oc) for k in (0, 1, 2, 3)])
        greet([device(gg=(g + k) % NG, ll=meet((g + k) % NG)) for k in (1, 2, 3)])
        for k in (1, 2, 3):
            @pl.when(y >= k)
            def _():
                greet([device(yy=(y + NY - k) % NY)])

    @pl.when(l != hub)
    def _():
        greet(rows)

    @pl.when((l != hub) & (l != 3 - hub))
    def _():
        greet([partner])

    def near_met():
        @pl.when((l != hub) & (l != 3 - hub))
        def _():
            pl.semaphore_wait(barrier, 5)
            pl.semaphore_signal(near, inc=1, device_id=device(ll=hub), device_id_type=MESH)

        @pl.when(l == 3 - hub)
        def _():
            pl.semaphore_wait(barrier, 8)
            pl.semaphore_signal(near, inc=1, device_id=device(ll=hub), device_id_type=MESH)
            pl.semaphore_signal(near, inc=1, device_id=partner, device_id_type=MESH)

    gains_ref[head] = gain_ref[...]

    def gain_copy():
        return remote(gain_ref, gains_ref.at[head], GAIN, GAIN, partner)

    def gain_row_copy(k, there, origin):
        rows = gains_ref.at[pl.ds(2 * origin, 2)]
        return remote(rows, rows, GAIN_ROW + k, GAIN_ROW + origin, device(xx=there))

    def pair_copy(i):
        return remote(pool.at[oc, i], pool.at[2, i], PAIR + i, PAIR + i, partner)

    def row_copy(e, k, there, origin):
        return remote(
            chip.at[2 * there + e], row_in.at[e, origin], ROW + 4 * e + k, ROW + 4 * e + origin, device(xx=there)
        )

    def low_copy(e, there, origin):
        return remote(row_tot.at[e], low_in.at[e, origin], LOW + 4 * e, LOW + 4 * e + origin, device(ll=there))

    def high_copy(e, k, there, origin):
        return remote(
            low_tot.at[e], high_in.at[e, origin], HIGH + 4 * e + k, HIGH + 4 * e + origin,
            device(gg=there, ll=meet(there)),
        )

    def y_copy(e, k, there, origin):
        return remote(high_tot.at[e], y_in.at[e, origin], YS + 4 * e + k, YS + 4 * e + origin, device(yy=there))

    def y_copy_first(e, k, there):
        part = pl.ds(D, D)
        return remote(
            high_tot.at[e, :, part], y_in.at[e, 0, :, part], YS + 4 * e + k, YS + 4 * e, device(yy=there)
        )

    def low_back(e, there):
        return remote(
            low_out.at[e, there], low_state.at[e], LOW_BACK + 4 * e + there, LOW_BACK + 4 * e, device(ll=there)
        )

    def row_back(e, k, there, origin):
        return remote(
            row_out.at[e, there], chip_state.at[2 * origin + e], ROW_BACK + 4 * e + k, ROW_BACK + 4 * e + origin,
            device(xx=there),
        )

    def back_copy(src, i):
        return remote(src.at[i], m_ref.at[8 * c + i], BACK + i, BACK + i, partner)

    def joint(parts, e, pre, tot):
        first = compose(parts[e, 1], parts[e, 0])
        last = compose(parts[e, 3], parts[e, 2])
        tot[e] = compose(last, first)
        pre[e, 0] = parts[e, 0]
        pre[e, 1] = first

    def third(parts, e, pre):
        pre[e, 2] = compose(parts[e, 2], pre[e, 1])

    def join_chip(e):
        for k in (2, 1, 3, 0):
            there = (x + k) % NX
            i = 2 * there + e
            pair_copy(i).wait_recv()
            joined = compose(pool[2 - c, i], pool[2 * c, i])
            if k:
                chip[i] = joined
                row_copy(e, k, there, x).start()
            else:
                row_in[e, x] = joined

    def up_row(e):
        for k in (1, 2, 3):
            origin = (x + k) % NX
            row_copy(e, 0, origin, origin).wait_recv()
        joint(row_in, e, row_pre, row_tot)

        @pl.when(l != hub)
        def _():
            low_copy(e, hub, l).start()

        @pl.when(is_hub)
        def _():
            low_in[e, l] = row_tot[e]

        third(row_in, e, row_pre)

    def up_low(e):
        @pl.when(is_hub)
        def _():
            for k in (1, 2, 3):
                origin = (l + k) % NL
                low_copy(e, origin, origin).wait_recv()
            joint(low_in, e, low_pre, low_tot)

            @pl.when(e == 0)
            def _():
                pl.semaphore_wait(barrier, 6 - y)

            for later in (True, False):
                for k in (1, 2, 3):
                    @pl.when((g + k < NG) == later)
                    def _():
                        high_copy(e, k, (g + k) % NG, g).start()
            high_in[e, g] = low_tot[e]
            third(low_in, e, low_pre)

    def high_wait(e, s):
        high_copy(e, 0, s, s).wait_recv()

    def through_hubs(e):
        @pl.when(is_hub)
        def _():
            for k in (1, 2, 3):
                high_wait(e, (g + k) % NG)
            joint(high_in, e, high_pre, high_tot)
            for k in (1, 2, 3):
                @pl.when(y == 0)
                def _():
                    y_copy_first(e, k, k).start()

                @pl.when((y > 0) & (y + k < NY))
                def _():
                    y_copy(e, k, (y + k) % NY, y).start()

            third(high_in, e, high_pre)
            start[e] = jnp.zeros((D, D), f32)

            @pl.when(y > 0)
            def _():
                y_copy_first(e, 0, 0).wait_recv()
                start[e] = y_in[e, 0, :, D:]

            for s in (1, 2):
                @pl.when(y > s)
                def _():
                    y_copy(e, 0, s, s).wait_recv()
                    start[e] = advance(y_in[e, s], start[e])

            @pl.when(g > 0)
            def _():
                start[e] = advance(high_pre[e, g - 1], start[e])

            begin = start[e]
            for place in range(NL):
                low_out[e, place] = begin if place == 0 else advance(low_pre[e, place - 1], begin)

                @pl.when(l != place)
                def _():
                    low_back(e, place).start()

                @pl.when(l == place)
                def _():
                    low_state[e] = low_out[e, place]

    def down_row(e):
        @pl.when(l != hub)
        def _():
            low_back(e, hub).wait_recv()
        begin = low_state[e]
        for place in range(NX):
            row_out[e, place] = begin if place == 0 else advance(row_pre[e, place - 1], begin)
        for k in (2, 1, 3):
            row_back(e, k, (x + k) % NX, x).start()
        chip_state[2 * x + e] = row_out[e, x]

    def down_chip(e):
        for k in (0, 1, 3, 2):
            origin = (x + k) % NX
            i = 2 * origin + e
            if k:
                row_back(e, 0, origin, origin).wait_recv()

            @pl.when(c == 1)
            def _():
                back_copy(chip_state, i).start()

            begin = chip_state[i]
            end = advance(pool[2 * c, i], begin)

            @pl.when(c == 0)
            def _():
                after[i] = end
                back_copy(after, i).start()
                m_ref[i] = begin

            @pl.when(c == 1)
            def _():
                m_ref[8 + i] = end

    lane = lax.broadcasted_iota(jnp.int32, (N, HEADS), 1)

    def turn(t):
        e, half = t // 2, t % 2
        here = [2 * v + e for v in range(NX)]
        betas = [
            jnp.sum(jnp.where(lane == 8 * half + i, b_ref[...], 0.0), axis=1, keepdims=True) for i in here
        ]
        keys = [k_ref[8 * half + i] for i in here]
        ys, maps = local_solves(keys, [v_ref[8 * half + i] for i in here], betas)
        for i, (a_part, b_part), (hi, lo) in zip(here, maps, ys):
            pool[half, i, :, :D] = a_part
            pool[half, i, :, D:] = b_part
            y_high[8 * half + i] = hi
            y_low[8 * half + i] = lo

        @pl.when(t == 0)
        def _():
            near_met()

        @pl.when((t == 1) & is_hub)
        def _():
            pl.semaphore_wait(near, 4)

        @pl.when((t == 1) & is_hub & (c == 1))
        def _():
            for v in range(NX):
                pair_copy(2 * v).start()

        @pl.when((half != c) & ((t > 0) | (l != hub)))
        def _():
            for i in here:
                pair_copy(i).start()

        @pl.when(t == 1)
        def _():
            gain_copy().start()

    def local_out(first):
        here = [first + 2 * v for v in range(NX)]
        outs = local_outputs(
            [q_ref[h] for h in here], [k_ref[h] for h in here], [(y_high[h], y_low[h]) for h in here]
        )
        for h, (q_part, o_part) in zip(here, outs):
            qo_ref[h, :, :D] = q_part
            qo_ref[h, :, D:] = o_part

    def slot(it, carry):
        @pl.when(it < 4)
        def _():
            turn(it)

        @pl.when(it == 4)
        def _():
            remote(gain_ref, gains_ref.at[2 * x + oc], GAIN, GAIN, partner).wait_recv()
            for k in (1, 2, 3):
                gain_row_copy(k, (x + k) % NX, x).start()

        @pl.when((it == 1 + c) | (it == 3 + c))
        def _():
            join_chip((it - 1 - c) // 2)

        @pl.when((it == 2 + c) | (it == 4))
        def _():
            up_row(it // 4)

        @pl.when((it == 3 + c) | (it == 5))
        def _():
            up_low(it // 5)

        @pl.when((it == 5) | (it == 6))
        def _():
            through_hubs(it - 5)
            down_row(it - 5)

        @pl.when(it > 6)
        def _():
            down_chip(it - 7)

        @pl.when((it > 3) & (it < 8))
        def _():
            local_out(8 * ((it - 4) // 2) + (it - 4) % 2)

        return carry

    lax.fori_loop(0, 9, slot, 0)
    for i in range(8):
        remote(after.at[i], m_ref.at[8 * oc + i], BACK + i, BACK + i, partner).wait_recv()
    for k in (1, 2, 3):
        origin = (x + k) % NX
        gain_row_copy(k, origin, origin).wait_recv()

    gain_copy().wait_send()
    for k in (1, 2, 3):
        gain_row_copy(k, (x + k) % NX, x).wait_send()
    for i in range(8):
        pair_copy(i).wait_send()
        back_copy(after, i).wait_send()
    for e in range(2):
        for k in (1, 2, 3):
            row_copy(e, k, (x + k) % NX, x).wait_send()
            row_back(e, k, (x + k) % NX, x).wait_send()

        @pl.when(l != hub)
        def _():
            low_copy(e, hub, l).wait_send()

        @pl.when(is_hub)
        def _():
            for place in range(NL):
                @pl.when(l != place)
                def _():
                    low_back(e, place).wait_send()
            for k in (1, 2, 3):
                high_copy(e, k, (g + k) % NG, g).wait_send()

                @pl.when(y == 0)
                def _():
                    y_copy_first(e, k, k).wait_send()

                @pl.when((y > 0) & (y + k < NY))
                def _():
                    y_copy(e, k, (y + k) % NY, y).wait_send()


def states(keys, values, queries, betas, gain):
    wide, square = (D, 2 * D), (D, D)
    whole = pl.BlockSpec(memory_space=pltpu.VMEM)

    def vm(*shape):
        return pltpu.VMEM(shape, f32)

    return pl.pallas_call(
        states_kernel,
        in_specs=[whole] * 5,
        out_specs=[whole] * 3,
        out_shape=[
            jax.ShapeDtypeStruct((HEADS, T, 2 * D), f32),
            jax.ShapeDtypeStruct((HEADS, D, D), f32),
            jax.ShapeDtypeStruct((8, 2, D), f32),
        ],
        scratch_shapes=[
            vm(3, 8, *wide), vm(8, *wide),
            vm(2, NX, *wide), vm(2, 3, *wide), vm(2, *wide),
            vm(2, NL, *wide), vm(2, 3, *wide), vm(2, *wide),
            vm(2, NG, *wide), vm(2, 3, *wide), vm(2, *wide),
            vm(2, NY, *wide), vm(2, *square), vm(2, NL, *square), vm(2, *square),
            vm(2, NX, *square), vm(8, *square), vm(8, *square),
            pltpu.VMEM((HEADS, N, 2 * D), bf16), pltpu.VMEM((HEADS, N, 2 * D), bf16),
            pltpu.SemaphoreType.DMA((SEMS,)), pltpu.SemaphoreType.DMA((SEMS,)), pltpu.SemaphoreType.REGULAR,
        ],
        compiler_params=pltpu.CompilerParams(
            collective_id=0, has_side_effects=True, vmem_limit_bytes=48 * 2**20
        ),
    )(keys, values, queries, betas, gain)


def by_head_kernel(k_ref, v_ref, q_ref, ko_ref, vo_ref, qo_ref, held, sem, q_sem):
    fetch = pltpu.make_async_copy(q_ref, held, q_sem)
    fetch.start()
    copies = [
        pltpu.make_async_copy(src.at[:, h], dst.at[h], sem.at[n, h])
        for h in range(HEADS)
        for n, (src, dst) in enumerate(((k_ref, ko_ref), (v_ref, vo_ref)))
    ]
    for copy in copies:
        copy.start()
    fetch.wait()
    qo_ref[...] = jnp.swapaxes(held[...].astype(f32), 0, 1).astype(bf16)
    for copy in copies:
        copy.wait()


def by_head(keys, values, queries):
    whole, away = pl.BlockSpec(memory_space=pltpu.VMEM), pl.BlockSpec(memory_space=pl.ANY)
    pairs = jax.ShapeDtypeStruct((HEADS, T, 2, D), bf16)
    k, v, q = pl.pallas_call(
        by_head_kernel,
        in_specs=[away] * 3,
        out_specs=[whole] * 3,
        out_shape=[pairs, pairs, jax.ShapeDtypeStruct((HEADS, T, D), bf16)],
        scratch_shapes=[
            pltpu.VMEM((T, HEADS, D), bf16), pltpu.SemaphoreType.DMA((2, HEADS)), pltpu.SemaphoreType.DMA,
        ],
        compiler_params=pltpu.CompilerParams(vmem_limit_bytes=50 * 2**20),
    )(keys, values, queries)
    return k.reshape(HEADS, N, D), v.reshape(HEADS, N, D), q


def output_kernel(qo_ref, m_ref, gains_ref, gate_ref, out_ref, rows):
    for h in range(HEADS):
        r = dot3(qo_ref[h, :, :D], m_ref[h]) + qo_ref[h, :, D:]
        scale = lax.rsqrt(jnp.mean(r * r, axis=-1, keepdims=True) + 1e-6)
        rows[h] = r * scale * gains_ref[h // 2, h % 2 : h % 2 + 1, :]
    gate = gate_ref[...].astype(f32)
    normed = jnp.swapaxes(rows[...], 0, 1)
    out_ref[...] = (normed * (gate / (1.0 + jnp.exp(-gate)))).astype(bf16)


def outputs(qo, m, gains, gate):
    whole = pl.BlockSpec(memory_space=pltpu.VMEM)
    return pl.pallas_call(
        output_kernel,
        in_specs=[whole] * 4,
        out_specs=whole,
        out_shape=jax.ShapeDtypeStruct((T, HEADS, D), bf16),
        scratch_shapes=[pltpu.VMEM((HEADS, T, D), f32)],
        compiler_params=pltpu.CompilerParams(vmem_limit_bytes=48 * 2**20),
    )(qo, m, gains, gate)


def local(queries, keys, values, betas, gate, gain):
    keys_h, values_h, queries_h = by_head(keys, values, queries)
    betas_h = jnp.transpose(betas, (0, 2, 1)).reshape(N, HEADS).astype(f32)
    qo, m, gains = states(keys_h, values_h, queries_h, betas_h, gain)
    return outputs(qo, m, gains, gate)


def solution(mesh):
    return jax.shard_map(
        local,
        mesh=mesh,
        in_specs=(
            P(("seq", "head"), None, None),
            P(("seq", "head"), None, None, None),
            P(("seq", "head"), None, None, None),
            P(("seq", "head"), None, None),
            P(("seq", "head"), None, None),
            P("head", None),
        ),
        out_specs=P(("seq", "head"), None, None),
        check_vma=False,
    )
```

```python
import functools
import jax, jax.numpy as jnp
from jax import lax
from jax.experimental import pallas as pl
from jax.experimental.pallas import tpu as pltpu
from jax.sharding import PartitionSpec as P
f32, bf16 = jnp.float32, jnp.bfloat16
D = 128
N = 256
T = 128
BASE = 16

def split(a):
    hi = a.astype(bf16)
    return hi, (a - hi.astype(f32)).astype(bf16)

def mm(a, b):
    return lax.dot_general(a, b, (((1,), (0,)), ((), ())), preferred_element_type=f32)

def mm_nt(a, b):
    return lax.dot_general(a, b, (((1,), (1,)), ((), ())), preferred_element_type=f32)

def mm_tn(a, b):
    return lax.dot_general(a, b, (((0,), (0,)), ((), ())), preferred_element_type=f32)

def dot3(a, b):
    ah, al = split(a)
    bh, bl = split(b)
    return dot3s(ah, al, bh, bl)

def dot3s(ah, al, bh, bl):
    if ah.shape[1] == 128:
        return mm(jnp.concatenate([ah, al], 1), jnp.concatenate([bh, bh], 0)) + mm(ah, bl)
    return mm(ah, bh) + (mm(al, bh) + mm(ah, bl))

def unit_lower_inverses(lows):
    n = len(lows)
    lane = lax.broadcasted_iota(jnp.int32, (BASE, 128), 1)
    row = lax.broadcasted_iota(jnp.int32, (BASE, 128), 0)
    blk = lane // BASE
    half = BASE // 2
    upper, lower = [], []
    for low in lows:
        z = jnp.zeros((BASE, 128), f32)
        for b in range(128 // BASE):
            z = jnp.where(blk == b, low[BASE * b:BASE * (b + 1), :], z)
        z = jnp.where(row > lane % BASE, z, 0.0)
        upper.append(z[:half])
        lower.append(z[half:])
    eye = jnp.where(row == lane % BASE, 1.0, 0.0).astype(f32)
    tops, ends = [eye[:half] for _ in lows], [eye[half:] for _ in lows]
    blk = blk[:half]
    for j in range(BASE - 1):
        idx = blk * BASE + j
        for i in range(n):
            pivot = tops[i][j:j + 1, :] if j < half else ends[i][j - half:j - half + 1, :]
            ends[i] = ends[i] - jnp.take_along_axis(lower[i], idx, axis=1, mode="promise_in_bounds") * pivot
            if j < half - 1:
                tops[i] = tops[i] - jnp.take_along_axis(upper[i], idx, axis=1, mode="promise_in_bounds") * pivot
    xs = [jnp.concatenate([top, end], 0) for top, end in zip(tops, ends)]
    blk = lane // BASE
    fulls = []
    for x in xs:
        fulls.append(jnp.concatenate([jnp.where(blk == b, x, 0.0) for b in range(128 // BASE)], axis=0))
    m = BASE
    r2 = lax.broadcasted_iota(jnp.int32, (128, 128), 0)
    c2 = lax.broadcasted_iota(jnp.int32, (128, 128), 1)
    while m < 128:
        offmask = ((r2 // m) % 2 == 1) & (c2 // m == r2 // m - 1)
        xos = [jnp.concatenate([x[m * (2 * b + 1):m * (2 * b + 2), :] for b in range(64 // m)], 0) for x in fulls]
        offs = [split(jnp.where(offmask, low, 0.0)) for low in lows]
        xos_s = [split(xo) for xo in xos]
        xs_s = [split(x) for x in fulls]
        ys = [dot3s(*xo, *off) for xo, off in zip(xos_s, offs)]
        ys = [split(y) for y in ys]
        zs = [xo - dot3s(*y, *x) for xo, y, x in zip(xos, ys, xs_s)]
        out = []
        for x, z in zip(fulls, zs):
            rows = []
            for b in range(64 // m):
                rows.append(x[m * 2 * b:m * (2 * b + 1), :])
                rows.append(z[m * b:m * (b + 1), :])
            out.append(jnp.concatenate(rows, 0))
        fulls = out
        m *= 2
    return fulls

MESH = pl.DeviceIdType.MESH
HEADS = 16
NX, NL, NG, NY = 4, 4, 4, 4
PAIR, ROW, LOW, HIGH, YS, LOW_BACK, ROW_BACK, BACK, GAIN, GAIN_ROW, SEMS = 0, 8, 16, 24, 32, 40, 48, 56, 64, 65, 69


def local_solves(keys, values, betas):
    hs = range(len(keys))
    r2 = lax.broadcasted_iota(jnp.int32, (128, 128), 0)
    c2 = lax.broadcasted_iota(jnp.int32, (128, 128), 1)
    eye = jnp.where(r2 == c2, 1.0, 0.0).astype(f32)
    lows, crosses, rights = [], [], []
    for k, v, beta in zip(keys, values, betas):
        kf = k.astype(f32)
        ssq = jnp.sum(kf * kf, axis=1, keepdims=True) + 1e-6
        p = beta / ssq
        bs = beta * lax.rsqrt(ssq)
        gram = mm_nt(k, k)
        lows.append(jnp.where(r2 > c2, p[:128] * gram[:128, :128], 0.0))
        lows.append(jnp.where(r2 > c2, p[128:] * gram[128:, 128:], 0.0))
        crosses.append(p[128:] * gram[128:, :128])
        rights.append(jnp.concatenate([p * kf, bs * v.astype(f32)], axis=1))
    invs = unit_lower_inverses(lows)
    y1 = [dot3(invs[2 * h], rights[h][:128]) for h in hs]
    rest = [rights[h][128:] - dot3(crosses[h], y1[h]) for h in hs]
    y2 = [dot3(invs[2 * h + 1], rest[h]) for h in hs]
    ys = [split(jnp.concatenate([y1[h], y2[h]], 0)) for h in hs]
    kys = [mm_tn(keys[h], ys[h][0]) + mm_tn(keys[h], ys[h][1]) for h in hs]
    return ys, [(eye - ky[:, :D], ky[:, D:]) for ky in kys]


def local_outputs(queries, keys, ys):
    vis = lax.broadcasted_iota(jnp.int32, (T, N), 1) <= 2 * lax.broadcasted_iota(jnp.int32, (T, N), 0) + 1
    scores = [split(jnp.where(vis, mm_nt(q, k), 0.0)) for q, k in zip(queries, keys)]
    sys_ = [dot3s(*s, *y) for s, y in zip(scores, ys)]
    return [(q.astype(f32) - sy[:, :D], sy[:, D:]) for q, sy in zip(queries, sys_)]


def compose(late, early):
    joined = dot3(late[:, :D], early)
    return jnp.concatenate([joined[:, :D], joined[:, D:] + late[:, D:]], axis=1)


def advance(pair, state):
    return dot3(pair[:, :D], state) + pair[:, D:]


def states_kernel(
    k_ref, v_ref, q_ref, b_ref, gain_ref, qo_ref, m_ref, gains_ref,
    pool, chip, row_in, row_pre, row_tot, low_in, low_pre, low_tot,
    high_in, high_pre, high_tot, y_in, start, low_out, low_state,
    row_out, chip_state, after, y_high, y_low, send, recv,
):
    seq, head = lax.axis_index("seq"), lax.axis_index("head")
    x, c = head // 2, head % 2
    y, g, l = seq // (NG * NL), (seq // NL) % NG, seq % NL
    oc = 1 - c

    def meet(gg):
        return 2 - c + (((gg + 1) // 2) % 2) * (2 * c - 1)

    hub = meet(g)
    is_hub = l == hub

    def device(xx=None, cc=None, yy=None, gg=None, ll=None):
        xx, cc = x if xx is None else xx, c if cc is None else cc
        yy, gg, ll = y if yy is None else yy, g if gg is None else gg, l if ll is None else ll
        return {"seq": (yy * NG + gg) * NL + ll, "head": xx * 2 + cc}

    partner = device(cc=oc)

    def remote(src, dst, s, r, where):
        return pltpu.make_async_remote_copy(
            src_ref=src, dst_ref=dst, send_sem=send.at[s], recv_sem=recv.at[r],
            device_id=where, device_id_type=MESH,
        )

    barrier = pltpu.get_barrier_semaphore()

    def greet(peers):
        for peer in peers:
            pl.semaphore_signal(barrier, inc=1, device_id=peer, device_id_type=MESH)

    greet([partner] + [device(xx=(x + k) % NX) for k in (1, 2, 3)])

    @pl.when(is_hub)
    def _():
        greet([device(ll=(l + k) % NL) for k in (1, 2, 3)])
        greet([device(gg=(g + k) % NG, ll=meet((g + k) % NG)) for k in (1, 2, 3)])
        greet([device(yy=(y + k) % NY) for k in (1, 2, 3)])

    @pl.when(l != hub)
    def _():
        greet([device(ll=hub)])

    def peers_met():
        @pl.when(is_hub)
        def _():
            pl.semaphore_wait(barrier, 13)

        @pl.when(l != hub)
        def _():
            pl.semaphore_wait(barrier, 5)

    gains_ref[head] = gain_ref[...]

    def gain_copy():
        return remote(gain_ref, gains_ref.at[head], GAIN, GAIN, partner)

    def gain_row_copy(k, there, origin):
        rows = gains_ref.at[pl.ds(2 * origin, 2)]
        return remote(rows, rows, GAIN_ROW + k, GAIN_ROW + origin, device(xx=there))

    def pair_copy(i):
        return remote(pool.at[oc, i], pool.at[2, i], PAIR + i, PAIR + i, partner)

    def row_copy(e, k, there, origin):
        return remote(
            chip.at[2 * there + e], row_in.at[e, origin], ROW + 4 * e + k, ROW + 4 * e + origin, device(xx=there)
        )

    def low_copy(e, there, origin):
        return remote(row_tot.at[e], low_in.at[e, origin], LOW + 4 * e, LOW + 4 * e + origin, device(ll=there))

    def high_copy(e, k, there, origin):
        return remote(
            low_tot.at[e], high_in.at[e, origin], HIGH + 4 * e + k, HIGH + 4 * e + origin,
            device(gg=there, ll=meet(there)),
        )

    def y_copy(e, k, there, origin):
        return remote(high_tot.at[e], y_in.at[e, origin], YS + 4 * e + k, YS + 4 * e + origin, device(yy=there))

    def y_copy_first(e, k, there):
        part = pl.ds(D, D)
        return remote(
            high_tot.at[e, :, part], y_in.at[e, 0, :, part], YS + 4 * e + k, YS + 4 * e, device(yy=there)
        )

    def low_back(e, there):
        return remote(
            low_out.at[e, there], low_state.at[e], LOW_BACK + 4 * e + there, LOW_BACK + 4 * e, device(ll=there)
        )

    def row_back(e, k, there, origin):
        return remote(
            row_out.at[e, there], chip_state.at[2 * origin + e], ROW_BACK + 4 * e + k, ROW_BACK + 4 * e + origin,
            device(xx=there),
        )

    def back_copy(src, i):
        return remote(src.at[i], m_ref.at[8 * c + i], BACK + i, BACK + i, partner)

    def joint(parts, e, pre, tot):
        first = compose(parts[e, 1], parts[e, 0])
        last = compose(parts[e, 3], parts[e, 2])
        tot[e] = compose(last, first)
        pre[e, 0] = parts[e, 0]
        pre[e, 1] = first

    def third(parts, e, pre):
        pre[e, 2] = compose(parts[e, 2], pre[e, 1])

    def join_chip(e):
        for k in (2, 1, 3, 0):
            there = (x + k) % NX
            i = 2 * there + e
            pair_copy(i).wait_recv()
            joined = compose(pool[2 - c, i], pool[2 * c, i])
            if k:
                chip[i] = joined
                row_copy(e, k, there, x).start()
            else:
                row_in[e, x] = joined

    def up_row(e):
        for k in (1, 2, 3):
            origin = (x + k) % NX
            row_copy(e, 0, origin, origin).wait_recv()
        joint(row_in, e, row_pre, row_tot)

        @pl.when(l != hub)
        def _():
            low_copy(e, hub, l).start()

        @pl.when(is_hub)
        def _():
            low_in[e, l] = row_tot[e]

        third(row_in, e, row_pre)

    def up_low(e):
        @pl.when(is_hub)
        def _():
            for k in (1, 2, 3):
                origin = (l + k) % NL
                low_copy(e, origin, origin).wait_recv()
            joint(low_in, e, low_pre, low_tot)

            for k in (2, 1, 3):
                high_copy(e, k, (g + k) % NG, g).start()
            high_in[e, g] = low_tot[e]
            third(low_in, e, low_pre)

    def high_wait(e, s):
        high_copy(e, 0, s, s).wait_recv()

    def up_high(e):
        @pl.when(is_hub)
        def _():
            for k in (1, 2, 3):
                high_wait(e, (g + k) % NG)
            joint(high_in, e, high_pre, high_tot)
            for k in (1, 2, 3):
                @pl.when(y == 0)
                def _():
                    y_copy_first(e, k, k).start()

                @pl.when((y > 0) & (y + k < NY))
                def _():
                    y_copy(e, k, (y + k) % NY, y).start()

            third(high_in, e, high_pre)

    def down_high(e):
        @pl.when(is_hub)
        def _():
            start[e] = jnp.zeros((D, D), f32)

            @pl.when(y > 0)
            def _():
                y_copy_first(e, 0, 0).wait_recv()
                start[e] = y_in[e, 0, :, D:]

            for s in (1, 2):
                @pl.when(y > s)
                def _():
                    y_copy(e, 0, s, s).wait_recv()
                    start[e] = advance(y_in[e, s], start[e])

            @pl.when(g > 0)
            def _():
                start[e] = advance(high_pre[e, g - 1], start[e])

            begin = start[e]
            for place in range(NL):
                low_out[e, place] = begin if place == 0 else advance(low_pre[e, place - 1], begin)

                @pl.when(l != place)
                def _():
                    low_back(e, place).start()

                @pl.when(l == place)
                def _():
                    low_state[e] = low_out[e, place]

    def down_row(e):
        @pl.when(l != hub)
        def _():
            low_back(e, hub).wait_recv()
        begin = low_state[e]
        for place in range(NX):
            row_out[e, place] = begin if place == 0 else advance(row_pre[e, place - 1], begin)
        for k in (2, 1, 3):
            row_back(e, k, (x + k) % NX, x).start()
        chip_state[2 * x + e] = row_out[e, x]

    def down_chip(e):
        for k in (0, 1, 3, 2):
            origin = (x + k) % NX
            i = 2 * origin + e
            if k:
                row_back(e, 0, origin, origin).wait_recv()

            @pl.when(c == 1)
            def _():
                back_copy(chip_state, i).start()

            begin = chip_state[i]
            end = advance(pool[2 * c, i], begin)

            @pl.when(c == 0)
            def _():
                after[i] = end
                back_copy(after, i).start()
                m_ref[i] = begin

            @pl.when(c == 1)
            def _():
                m_ref[8 + i] = end

    lane = lax.broadcasted_iota(jnp.int32, (N, HEADS), 1)

    def turn(t):
        e, half = t // 2, t % 2
        here = [2 * v + e for v in range(NX)]
        betas = [
            jnp.sum(jnp.where(lane == 8 * half + i, b_ref[...], 0.0), axis=1, keepdims=True) for i in here
        ]
        keys = [k_ref[8 * half + i] for i in here]
        ys, maps = local_solves(keys, [v_ref[8 * half + i] for i in here], betas)
        for i, (a_part, b_part), (hi, lo) in zip(here, maps, ys):
            pool[half, i, :, :D] = a_part
            pool[half, i, :, D:] = b_part
            y_high[8 * half + i] = hi
            y_low[8 * half + i] = lo

        @pl.when(t == 0)
        def _():
            peers_met()

        @pl.when(half != c)
        def _():
            for i in here:
                pair_copy(i).start()

        @pl.when(t == 1)
        def _():
            gain_copy().start()

    def local_out(first):
        here = [first + 2 * v for v in range(NX)]
        outs = local_outputs(
            [q_ref[h] for h in here], [k_ref[h] for h in here], [(y_high[h], y_low[h]) for h in here]
        )
        for h, (q_part, o_part) in zip(here, outs):
            qo_ref[h, :, :D] = q_part
            qo_ref[h, :, D:] = o_part

    def slot(it, carry):
        @pl.when(it < 4)
        def _():
            turn(it)

        @pl.when(it == 4)
        def _():
            remote(gain_ref, gains_ref.at[2 * x + oc], GAIN, GAIN, partner).wait_recv()
            for k in (1, 2, 3):
                gain_row_copy(k, (x + k) % NX, x).start()

        @pl.when((it == 1 + c) | (it == 3 + c))
        def _():
            join_chip((it - 1 - c) // 2)

        @pl.when((it == 2 + c) | (it == 4))
        def _():
            up_row(it // 4)

        @pl.when((it == 3 + c) | (it == 5))
        def _():
            up_low(it // 5)

        @pl.when((it == 5) | (it == 6))
        def _():
            up_high(it - 5)

        @pl.when((it == 6) | (it == 7))
        def _():
            down_high(it - 6)
            down_row(it - 6)

        @pl.when(it > 7)
        def _():
            down_chip(it - 8)

        @pl.when((it > 3) & (it < 8))
        def _():
            local_out(8 * ((it - 4) // 2) + (it - 4) % 2)

        return carry

    lax.fori_loop(0, 10, slot, 0)
    for i in range(8):
        remote(after.at[i], m_ref.at[8 * oc + i], BACK + i, BACK + i, partner).wait_recv()
    for k in (1, 2, 3):
        origin = (x + k) % NX
        gain_row_copy(k, origin, origin).wait_recv()

    gain_copy().wait_send()
    for k in (1, 2, 3):
        gain_row_copy(k, (x + k) % NX, x).wait_send()
    for i in range(8):
        pair_copy(i).wait_send()
        back_copy(after, i).wait_send()
    for e in range(2):
        for k in (1, 2, 3):
            row_copy(e, k, (x + k) % NX, x).wait_send()
            row_back(e, k, (x + k) % NX, x).wait_send()

        @pl.when(l != hub)
        def _():
            low_copy(e, hub, l).wait_send()

        @pl.when(is_hub)
        def _():
            for place in range(NL):
                @pl.when(l != place)
                def _():
                    low_back(e, place).wait_send()
            for k in (1, 2, 3):
                high_copy(e, k, (g + k) % NG, g).wait_send()

                @pl.when(y == 0)
                def _():
                    y_copy_first(e, k, k).wait_send()

                @pl.when((y > 0) & (y + k < NY))
                def _():
                    y_copy(e, k, (y + k) % NY, y).wait_send()


def states(keys, values, queries, betas, gain):
    wide, square = (D, 2 * D), (D, D)
    whole = pl.BlockSpec(memory_space=pltpu.VMEM)

    def vm(*shape):
        return pltpu.VMEM(shape, f32)

    return pl.pallas_call(
        states_kernel,
        in_specs=[whole] * 5,
        out_specs=[whole] * 3,
        out_shape=[
            jax.ShapeDtypeStruct((HEADS, T, 2 * D), f32),
            jax.ShapeDtypeStruct((HEADS, D, D), f32),
            jax.ShapeDtypeStruct((8, 2, D), f32),
        ],
        scratch_shapes=[
            vm(3, 8, *wide), vm(8, *wide),
            vm(2, NX, *wide), vm(2, 3, *wide), vm(2, *wide),
            vm(2, NL, *wide), vm(2, 3, *wide), vm(2, *wide),
            vm(2, NG, *wide), vm(2, 3, *wide), vm(2, *wide),
            vm(2, NY, *wide), vm(2, *square), vm(2, NL, *square), vm(2, *square),
            vm(2, NX, *square), vm(8, *square), vm(8, *square),
            pltpu.VMEM((HEADS, N, 2 * D), bf16), pltpu.VMEM((HEADS, N, 2 * D), bf16),
            pltpu.SemaphoreType.DMA((SEMS,)), pltpu.SemaphoreType.DMA((SEMS,)),
        ],
        compiler_params=pltpu.CompilerParams(
            collective_id=0, has_side_effects=True, vmem_limit_bytes=48 * 2**20
        ),
    )(keys, values, queries, betas, gain)


def by_head_kernel(k_ref, v_ref, q_ref, ko_ref, vo_ref, qo_ref, held, sem, q_sem):
    fetch = pltpu.make_async_copy(q_ref, held, q_sem)
    fetch.start()
    copies = [
        pltpu.make_async_copy(src.at[:, h], dst.at[h], sem.at[n, h])
        for h in range(HEADS)
        for n, (src, dst) in enumerate(((k_ref, ko_ref), (v_ref, vo_ref)))
    ]
    for copy in copies:
        copy.start()
    fetch.wait()
    qo_ref[...] = jnp.swapaxes(held[...].astype(f32), 0, 1).astype(bf16)
    for copy in copies:
        copy.wait()


def by_head(keys, values, queries):
    whole, away = pl.BlockSpec(memory_space=pltpu.VMEM), pl.BlockSpec(memory_space=pl.ANY)
    pairs = jax.ShapeDtypeStruct((HEADS, T, 2, D), bf16)
    k, v, q = pl.pallas_call(
        by_head_kernel,
        in_specs=[away] * 3,
        out_specs=[whole] * 3,
        out_shape=[pairs, pairs, jax.ShapeDtypeStruct((HEADS, T, D), bf16)],
        scratch_shapes=[
            pltpu.VMEM((T, HEADS, D), bf16), pltpu.SemaphoreType.DMA((2, HEADS)), pltpu.SemaphoreType.DMA,
        ],
        compiler_params=pltpu.CompilerParams(vmem_limit_bytes=50 * 2**20),
    )(keys, values, queries)
    return k.reshape(HEADS, N, D), v.reshape(HEADS, N, D), q


def output_kernel(qo_ref, m_ref, gains_ref, gate_ref, out_ref, rows):
    for h in range(HEADS):
        r = dot3(qo_ref[h, :, :D], m_ref[h]) + qo_ref[h, :, D:]
        scale = lax.rsqrt(jnp.mean(r * r, axis=-1, keepdims=True) + 1e-6)
        rows[h] = r * scale * gains_ref[h // 2, h % 2 : h % 2 + 1, :]
    gate = gate_ref[...].astype(f32)
    normed = jnp.swapaxes(rows[...], 0, 1)
    out_ref[...] = (normed * (gate / (1.0 + jnp.exp(-gate)))).astype(bf16)


def outputs(qo, m, gains, gate):
    whole = pl.BlockSpec(memory_space=pltpu.VMEM)
    return pl.pallas_call(
        output_kernel,
        in_specs=[whole] * 4,
        out_specs=whole,
        out_shape=jax.ShapeDtypeStruct((T, HEADS, D), bf16),
        scratch_shapes=[pltpu.VMEM((HEADS, T, D), f32)],
        compiler_params=pltpu.CompilerParams(vmem_limit_bytes=48 * 2**20),
    )(qo, m, gains, gate)


def local(queries, keys, values, betas, gate, gain):
    keys_h, values_h, queries_h = by_head(keys, values, queries)
    betas_h = jnp.transpose(betas, (0, 2, 1)).reshape(N, HEADS).astype(f32)
    qo, m, gains = states(keys_h, values_h, queries_h, betas_h, gain)
    return outputs(qo, m, gains, gate)


def solution(mesh):
    return jax.shard_map(
        local,
        mesh=mesh,
        in_specs=(
            P(("seq", "head"), None, None),
            P(("seq", "head"), None, None, None),
            P(("seq", "head"), None, None, None),
            P(("seq", "head"), None, None),
            P(("seq", "head"), None, None),
            P("head", None),
        ),
        out_specs=P(("seq", "head"), None, None),
        check_vma=False,
    )
```

```python
import functools
import jax, jax.numpy as jnp
from jax import lax
from jax.experimental import pallas as pl
from jax.experimental.pallas import tpu as pltpu
from jax.sharding import PartitionSpec as P
f32, bf16 = jnp.float32, jnp.bfloat16
D = 128
N = 256
T = 128
BASE = 16

def split(a):
    hi = a.astype(bf16)
    return hi, (a - hi.astype(f32)).astype(bf16)

def mm(a, b):
    return lax.dot_general(a, b, (((1,), (0,)), ((), ())), preferred_element_type=f32)

def mm_nt(a, b):
    return lax.dot_general(a, b, (((1,), (1,)), ((), ())), preferred_element_type=f32)

def mm_tn(a, b):
    return lax.dot_general(a, b, (((0,), (0,)), ((), ())), preferred_element_type=f32)

def dot3(a, b):
    ah, al = split(a)
    bh, bl = split(b)
    return dot3s(ah, al, bh, bl)

def dot3s(ah, al, bh, bl):
    if ah.shape[1] == 128:
        return mm(jnp.concatenate([ah, al], 1), jnp.concatenate([bh, bh], 0)) + mm(ah, bl)
    return mm(ah, bh) + (mm(al, bh) + mm(ah, bl))

def unit_lower_inverses(lows):
    n = len(lows)
    lane = lax.broadcasted_iota(jnp.int32, (BASE, 128), 1)
    row = lax.broadcasted_iota(jnp.int32, (BASE, 128), 0)
    blk = lane // BASE
    half = BASE // 2
    upper, lower = [], []
    for low in lows:
        z = jnp.zeros((BASE, 128), f32)
        for b in range(128 // BASE):
            z = jnp.where(blk == b, low[BASE * b:BASE * (b + 1), :], z)
        z = jnp.where(row > lane % BASE, z, 0.0)
        upper.append(z[:half])
        lower.append(z[half:])
    eye = jnp.where(row == lane % BASE, 1.0, 0.0).astype(f32)
    tops, ends = [eye[:half] for _ in lows], [eye[half:] for _ in lows]
    blk = blk[:half]
    for j in range(BASE - 1):
        idx = blk * BASE + j
        for i in range(n):
            pivot = tops[i][j:j + 1, :] if j < half else ends[i][j - half:j - half + 1, :]
            ends[i] = ends[i] - jnp.take_along_axis(lower[i], idx, axis=1, mode="promise_in_bounds") * pivot
            if j < half - 1:
                tops[i] = tops[i] - jnp.take_along_axis(upper[i], idx, axis=1, mode="promise_in_bounds") * pivot
    xs = [jnp.concatenate([top, end], 0) for top, end in zip(tops, ends)]
    blk = lane // BASE
    fulls = []
    for x in xs:
        fulls.append(jnp.concatenate([jnp.where(blk == b, x, 0.0) for b in range(128 // BASE)], axis=0))
    m = BASE
    r2 = lax.broadcasted_iota(jnp.int32, (128, 128), 0)
    c2 = lax.broadcasted_iota(jnp.int32, (128, 128), 1)
    while m < 128:
        offmask = ((r2 // m) % 2 == 1) & (c2 // m == r2 // m - 1)
        xos = [jnp.concatenate([x[m * (2 * b + 1):m * (2 * b + 2), :] for b in range(64 // m)], 0) for x in fulls]
        offs = [split(jnp.where(offmask, low, 0.0)) for low in lows]
        xos_s = [split(xo) for xo in xos]
        xs_s = [split(x) for x in fulls]
        ys = [dot3s(*xo, *off) for xo, off in zip(xos_s, offs)]
        ys = [split(y) for y in ys]
        zs = [xo - dot3s(*y, *x) for xo, y, x in zip(xos, ys, xs_s)]
        out = []
        for x, z in zip(fulls, zs):
            rows = []
            for b in range(64 // m):
                rows.append(x[m * 2 * b:m * (2 * b + 1), :])
                rows.append(z[m * b:m * (b + 1), :])
            out.append(jnp.concatenate(rows, 0))
        fulls = out
        m *= 2
    return fulls

MESH = pl.DeviceIdType.MESH
HEADS = 16
NX, NL, NG, NY = 4, 4, 4, 4
PAIR, ROW, LOW, HIGH, YS, LOW_BACK, ROW_BACK, BACK, GAIN, GAIN_ROW, SEMS = 0, 8, 16, 24, 32, 40, 48, 56, 64, 65, 69


def local_solves(keys, values, betas):
    hs = range(len(keys))
    r2 = lax.broadcasted_iota(jnp.int32, (128, 128), 0)
    c2 = lax.broadcasted_iota(jnp.int32, (128, 128), 1)
    eye = jnp.where(r2 == c2, 1.0, 0.0).astype(f32)
    lows, crosses, rights = [], [], []
    for k, v, beta in zip(keys, values, betas):
        kf = k.astype(f32)
        ssq = jnp.sum(kf * kf, axis=1, keepdims=True) + 1e-6
        p = beta / ssq
        bs = beta * lax.rsqrt(ssq)
        gram = mm_nt(k, k)
        lows.append(jnp.where(r2 > c2, p[:128] * gram[:128, :128], 0.0))
        lows.append(jnp.where(r2 > c2, p[128:] * gram[128:, 128:], 0.0))
        crosses.append(p[128:] * gram[128:, :128])
        rights.append(jnp.concatenate([p * kf, bs * v.astype(f32)], axis=1))
    invs = unit_lower_inverses(lows)
    y1 = [dot3(invs[2 * h], rights[h][:128]) for h in hs]
    rest = [rights[h][128:] - dot3(crosses[h], y1[h]) for h in hs]
    y2 = [dot3(invs[2 * h + 1], rest[h]) for h in hs]
    ys = [split(jnp.concatenate([y1[h], y2[h]], 0)) for h in hs]
    kys = [mm_tn(keys[h], ys[h][0]) + mm_tn(keys[h], ys[h][1]) for h in hs]
    return ys, [(eye - ky[:, :D], ky[:, D:]) for ky in kys]


def local_outputs(queries, keys, ys):
    vis = lax.broadcasted_iota(jnp.int32, (T, N), 1) <= 2 * lax.broadcasted_iota(jnp.int32, (T, N), 0) + 1
    scores = [split(jnp.where(vis, mm_nt(q, k), 0.0)) for q, k in zip(queries, keys)]
    sys_ = [dot3s(*s, *y) for s, y in zip(scores, ys)]
    return [(q.astype(f32) - sy[:, :D], sy[:, D:]) for q, sy in zip(queries, sys_)]


def compose(late, early):
    joined = dot3(late[:, :D], early)
    return jnp.concatenate([joined[:, :D], joined[:, D:] + late[:, D:]], axis=1)


def advance(pair, state):
    return dot3(pair[:, :D], state) + pair[:, D:]


def states_kernel(
    k_ref, v_ref, q_ref, b_ref, gain_ref, qo_ref, m_ref, gains_ref,
    pool, chip, row_in, row_pre, row_tot, low_in, low_pre, low_tot,
    high_in, high_pre, high_tot, y_in, start, low_out, low_state,
    row_out, chip_state, after, y_high, y_low, q_heads, send, recv,
):
    seq, head = lax.axis_index("seq"), lax.axis_index("head")
    x, c = head // 2, head % 2
    y, g, l = seq // (NG * NL), (seq // NL) % NG, seq % NL
    oc = 1 - c

    def meet(gg):
        return 2 - c + (((gg + 1) // 2) % 2) * (2 * c - 1)

    hub = meet(g)
    is_hub = l == hub

    def device(xx=None, cc=None, yy=None, gg=None, ll=None):
        xx, cc = x if xx is None else xx, c if cc is None else cc
        yy, gg, ll = y if yy is None else yy, g if gg is None else gg, l if ll is None else ll
        return {"seq": (yy * NG + gg) * NL + ll, "head": xx * 2 + cc}

    partner = device(cc=oc)

    def remote(src, dst, s, r, where):
        return pltpu.make_async_remote_copy(
            src_ref=src, dst_ref=dst, send_sem=send.at[s], recv_sem=recv.at[r],
            device_id=where, device_id_type=MESH,
        )

    barrier = pltpu.get_barrier_semaphore()

    def greet(peers):
        for peer in peers:
            pl.semaphore_signal(barrier, inc=1, device_id=peer, device_id_type=MESH)

    greet([partner] + [device(xx=(x + k) % NX) for k in (1, 2, 3)])

    @pl.when(is_hub)
    def _():
        greet([device(ll=(l + k) % NL) for k in (1, 2, 3)])
        greet([device(gg=(g + k) % NG, ll=meet((g + k) % NG)) for k in (1, 2, 3)])
        greet([device(yy=(y + k) % NY) for k in (1, 2, 3)])

    @pl.when(l != hub)
    def _():
        greet([device(ll=hub)])

    def peers_met():
        @pl.when(is_hub)
        def _():
            pl.semaphore_wait(barrier, 13)

        @pl.when(l != hub)
        def _():
            pl.semaphore_wait(barrier, 5)

    gains_ref[head] = gain_ref[...]

    def gain_copy():
        return remote(gain_ref, gains_ref.at[head], GAIN, GAIN, partner)

    def gain_row_copy(k, there, origin):
        rows = gains_ref.at[pl.ds(2 * origin, 2)]
        return remote(rows, rows, GAIN_ROW + k, GAIN_ROW + origin, device(xx=there))

    def pair_copy(i):
        return remote(pool.at[oc, i], pool.at[2, i], PAIR + i, PAIR + i, partner)

    def row_copy(e, k, there, origin):
        return remote(
            chip.at[2 * there + e], row_in.at[e, origin], ROW + 4 * e + k, ROW + 4 * e + origin, device(xx=there)
        )

    def low_copy(e, there, origin):
        return remote(row_tot.at[e], low_in.at[e, origin], LOW + 4 * e, LOW + 4 * e + origin, device(ll=there))

    def high_copy(e, k, there, origin):
        return remote(
            low_tot.at[e], high_in.at[e, origin], HIGH + 4 * e + k, HIGH + 4 * e + origin,
            device(gg=there, ll=meet(there)),
        )

    def y_copy(e, k, there, origin):
        return remote(high_tot.at[e], y_in.at[e, origin], YS + 4 * e + k, YS + 4 * e + origin, device(yy=there))

    def y_copy_first(e, k, there):
        part = pl.ds(D, D)
        return remote(
            high_tot.at[e, :, part], y_in.at[e, 0, :, part], YS + 4 * e + k, YS + 4 * e, device(yy=there)
        )

    def low_back(e, there):
        return remote(
            low_out.at[e, there], low_state.at[e], LOW_BACK + 4 * e + there, LOW_BACK + 4 * e, device(ll=there)
        )

    def row_back(e, k, there, origin):
        return remote(
            row_out.at[e, there], chip_state.at[2 * origin + e], ROW_BACK + 4 * e + k, ROW_BACK + 4 * e + origin,
            device(xx=there),
        )

    def back_copy(src, i):
        return remote(src.at[i], m_ref.at[8 * c + i], BACK + i, BACK + i, partner)

    def joint(parts, e, pre, tot):
        first = compose(parts[e, 1], parts[e, 0])
        last = compose(parts[e, 3], parts[e, 2])
        tot[e] = compose(last, first)
        pre[e, 0] = parts[e, 0]
        pre[e, 1] = first

    def third(parts, e, pre):
        pre[e, 2] = compose(parts[e, 2], pre[e, 1])

    def join_chip(e):
        for k in (2, 1, 3, 0):
            there = (x + k) % NX
            i = 2 * there + e
            pair_copy(i).wait_recv()
            joined = compose(pool[2 - c, i], pool[2 * c, i])
            if k:
                chip[i] = joined
                row_copy(e, k, there, x).start()
            else:
                row_in[e, x] = joined

    def up_row(e):
        for k in (1, 2, 3):
            origin = (x + k) % NX
            row_copy(e, 0, origin, origin).wait_recv()
        joint(row_in, e, row_pre, row_tot)

        @pl.when(l != hub)
        def _():
            low_copy(e, hub, l).start()

        @pl.when(is_hub)
        def _():
            low_in[e, l] = row_tot[e]

        third(row_in, e, row_pre)

    def up_low(e):
        @pl.when(is_hub)
        def _():
            for k in (1, 2, 3):
                origin = (l + k) % NL
                low_copy(e, origin, origin).wait_recv()
            joint(low_in, e, low_pre, low_tot)

            for k in (2, 1, 3):
                high_copy(e, k, (g + k) % NG, g).start()
            high_in[e, g] = low_tot[e]
            third(low_in, e, low_pre)

    def high_wait(e, s):
        high_copy(e, 0, s, s).wait_recv()

    def up_high(e):
        @pl.when(is_hub)
        def _():
            for k in (1, 2, 3):
                high_wait(e, (g + k) % NG)
            joint(high_in, e, high_pre, high_tot)
            for k in (2, 3, 1):
                @pl.when(y == 0)
                def _():
                    y_copy_first(e, k, k).start()

                @pl.when((y > 0) & (y + k < NY))
                def _():
                    y_copy(e, k, (y + k) % NY, y).start()

            third(high_in, e, high_pre)

    def down_high(e):
        @pl.when(is_hub)
        def _():
            start[e] = jnp.zeros((D, D), f32)

            @pl.when(y > 0)
            def _():
                y_copy_first(e, 0, 0).wait_recv()
                start[e] = y_in[e, 0, :, D:]

            for s in (1, 2):
                @pl.when(y > s)
                def _():
                    y_copy(e, 0, s, s).wait_recv()
                    start[e] = advance(y_in[e, s], start[e])

            @pl.when(g > 0)
            def _():
                start[e] = advance(high_pre[e, g - 1], start[e])

            begin = start[e]
            for place in range(NL):
                low_out[e, place] = begin if place == 0 else advance(low_pre[e, place - 1], begin)

                @pl.when(l != place)
                def _():
                    low_back(e, place).start()

                @pl.when(l == place)
                def _():
                    low_state[e] = low_out[e, place]

    def down_row(e):
        @pl.when(l != hub)
        def _():
            low_back(e, hub).wait_recv()
        begin = low_state[e]
        for place in range(NX):
            row_out[e, place] = begin if place == 0 else advance(row_pre[e, place - 1], begin)
        for k in (2, 1, 3):
            row_back(e, k, (x + k) % NX, x).start()
        chip_state[2 * x + e] = row_out[e, x]

    def down_chip(e):
        for k in (0, 1, 3, 2):
            origin = (x + k) % NX
            i = 2 * origin + e
            if k:
                row_back(e, 0, origin, origin).wait_recv()

            @pl.when(c == 1)
            def _():
                back_copy(chip_state, i).start()

            begin = chip_state[i]
            end = advance(pool[2 * c, i], begin)

            @pl.when(c == 0)
            def _():
                after[i] = end
                back_copy(after, i).start()
                m_ref[i] = begin

            @pl.when(c == 1)
            def _():
                m_ref[8 + i] = end

    lane = lax.broadcasted_iota(jnp.int32, (N, HEADS), 1)

    def turn(t):
        e, half = t // 2, t % 2
        here = [2 * v + e for v in range(NX)]
        betas = [
            jnp.sum(jnp.where(lane == 8 * half + i, b_ref[...], 0.0), axis=1, keepdims=True) for i in here
        ]
        keys = [k_ref[8 * half + i] for i in here]
        ys, maps = local_solves(keys, [v_ref[8 * half + i] for i in here], betas)
        for i, (a_part, b_part), (hi, lo) in zip(here, maps, ys):
            pool[half, i, :, :D] = a_part
            pool[half, i, :, D:] = b_part
            y_high[8 * half + i] = hi
            y_low[8 * half + i] = lo

        @pl.when(t == 0)
        def _():
            peers_met()

        @pl.when(half != c)
        def _():
            for i in here:
                pair_copy(i).start()

        @pl.when(t == 1)
        def _():
            gain_copy().start()

    def local_out(first):
        here = [first + 2 * v for v in range(NX)]
        outs = local_outputs(
            [q_heads[h] for h in here], [k_ref[h] for h in here], [(y_high[h], y_low[h]) for h in here]
        )
        for h, (q_part, o_part) in zip(here, outs):
            qo_ref[h, :, :D] = q_part
            qo_ref[h, :, D:] = o_part

    def slot(it, carry):
        @pl.when(it < 4)
        def _():
            turn(it)

        @pl.when(it == 4)
        def _():
            remote(gain_ref, gains_ref.at[2 * x + oc], GAIN, GAIN, partner).wait_recv()
            for k in (1, 2, 3):
                gain_row_copy(k, (x + k) % NX, x).start()

        @pl.when((it == 1 + c) | (it == 3 + c))
        def _():
            join_chip((it - 1 - c) // 2)

        @pl.when((it == 2 + c) | (it == 4))
        def _():
            up_row(it // 4)

        @pl.when((it == 3 + c) | (it == 5))
        def _():
            up_low(it // 5)

        @pl.when((it == 5) | (it == 6))
        def _():
            up_high(it - 5)

        @pl.when((it == 6) | (it == 7))
        def _():
            down_high(it - 6)
            down_row(it - 6)

        @pl.when(it > 7)
        def _():
            down_chip(it - 8)

        @pl.when(it == 4)
        def _():
            q_heads[...] = jnp.swapaxes(q_ref[...].astype(f32), 0, 1).astype(bf16)

        @pl.when((it > 3) & (it < 8))
        def _():
            local_out(8 * ((it - 4) // 2) + (it - 4) % 2)

        return carry

    lax.fori_loop(0, 10, slot, 0)
    for i in range(8):
        remote(after.at[i], m_ref.at[8 * oc + i], BACK + i, BACK + i, partner).wait_recv()
    for k in (1, 2, 3):
        origin = (x + k) % NX
        gain_row_copy(k, origin, origin).wait_recv()

    gain_copy().wait_send()
    for k in (1, 2, 3):
        gain_row_copy(k, (x + k) % NX, x).wait_send()
    for i in range(8):
        pair_copy(i).wait_send()
        back_copy(after, i).wait_send()
    for e in range(2):
        for k in (1, 2, 3):
            row_copy(e, k, (x + k) % NX, x).wait_send()
            row_back(e, k, (x + k) % NX, x).wait_send()

        @pl.when(l != hub)
        def _():
            low_copy(e, hub, l).wait_send()

        @pl.when(is_hub)
        def _():
            for place in range(NL):
                @pl.when(l != place)
                def _():
                    low_back(e, place).wait_send()
            for k in (1, 2, 3):
                high_copy(e, k, (g + k) % NG, g).wait_send()

                @pl.when(y == 0)
                def _():
                    y_copy_first(e, k, k).wait_send()

                @pl.when((y > 0) & (y + k < NY))
                def _():
                    y_copy(e, k, (y + k) % NY, y).wait_send()


def states(keys, values, queries, betas, gain):
    wide, square = (D, 2 * D), (D, D)
    whole = pl.BlockSpec(memory_space=pltpu.VMEM)

    def vm(*shape):
        return pltpu.VMEM(shape, f32)

    return pl.pallas_call(
        states_kernel,
        in_specs=[whole] * 5,
        out_specs=[whole] * 3,
        out_shape=[
            jax.ShapeDtypeStruct((HEADS, T, 2 * D), f32),
            jax.ShapeDtypeStruct((HEADS, D, D), f32),
            jax.ShapeDtypeStruct((8, 2, D), f32),
        ],
        scratch_shapes=[
            vm(3, 8, *wide), vm(8, *wide),
            vm(2, NX, *wide), vm(2, 3, *wide), vm(2, *wide),
            vm(2, NL, *wide), vm(2, 3, *wide), vm(2, *wide),
            vm(2, NG, *wide), vm(2, 3, *wide), vm(2, *wide),
            vm(2, NY, *wide), vm(2, *square), vm(2, NL, *square), vm(2, *square),
            vm(2, NX, *square), vm(8, *square), vm(8, *square),
            pltpu.VMEM((HEADS, N, 2 * D), bf16), pltpu.VMEM((HEADS, N, 2 * D), bf16), pltpu.VMEM((HEADS, T, D), bf16),
            pltpu.SemaphoreType.DMA((SEMS,)), pltpu.SemaphoreType.DMA((SEMS,)),
        ],
        compiler_params=pltpu.CompilerParams(
            collective_id=0, has_side_effects=True, vmem_limit_bytes=48 * 2**20
        ),
    )(keys, values, queries, betas, gain)


def by_head_kernel(k_ref, v_ref, ko_ref, vo_ref, sem):
    copies = [
        pltpu.make_async_copy(src.at[:, h], dst.at[h], sem.at[n, h])
        for h in range(HEADS)
        for n, (src, dst) in enumerate(((k_ref, ko_ref), (v_ref, vo_ref)))
    ]
    for copy in copies:
        copy.start()
    for copy in copies:
        copy.wait()


def by_head(keys, values):
    whole, away = pl.BlockSpec(memory_space=pltpu.VMEM), pl.BlockSpec(memory_space=pl.ANY)
    pairs = jax.ShapeDtypeStruct((HEADS, T, 2, D), bf16)
    k, v = pl.pallas_call(
        by_head_kernel,
        in_specs=[away] * 2,
        out_specs=[whole] * 2,
        out_shape=[pairs, pairs],
        scratch_shapes=[pltpu.SemaphoreType.DMA((2, HEADS))],
        compiler_params=pltpu.CompilerParams(vmem_limit_bytes=51 * 2**20),
    )(keys, values)
    return k.reshape(HEADS, N, D), v.reshape(HEADS, N, D)


def output_kernel(qo_ref, m_ref, gains_ref, gate_ref, out_ref, rows):
    for h in range(HEADS):
        r = dot3(qo_ref[h, :, :D], m_ref[h]) + qo_ref[h, :, D:]
        scale = lax.rsqrt(jnp.mean(r * r, axis=-1, keepdims=True) + 1e-6)
        rows[h] = r * scale * gains_ref[h // 2, h % 2 : h % 2 + 1, :]
    gate = gate_ref[...].astype(f32)
    normed = jnp.swapaxes(rows[...], 0, 1)
    out_ref[...] = (normed * (gate / (1.0 + jnp.exp(-gate)))).astype(bf16)


def outputs(qo, m, gains, gate):
    whole = pl.BlockSpec(memory_space=pltpu.VMEM)
    return pl.pallas_call(
        output_kernel,
        in_specs=[whole] * 4,
        out_specs=whole,
        out_shape=jax.ShapeDtypeStruct((T, HEADS, D), bf16),
        scratch_shapes=[pltpu.VMEM((HEADS, T, D), f32)],
        compiler_params=pltpu.CompilerParams(vmem_limit_bytes=48 * 2**20),
    )(qo, m, gains, gate)


def local(queries, keys, values, betas, gate, gain):
    keys_h, values_h = by_head(keys, values)
    betas_h = jnp.transpose(betas, (0, 2, 1)).reshape(N, HEADS).astype(f32)
    qo, m, gains = states(keys_h, values_h, queries, betas_h, gain)
    return outputs(qo, m, gains, gate)


def solution(mesh):
    return jax.shard_map(
        local,
        mesh=mesh,
        in_specs=(
            P(("seq", "head"), None, None),
            P(("seq", "head"), None, None, None),
            P(("seq", "head"), None, None, None),
            P(("seq", "head"), None, None),
            P(("seq", "head"), None, None),
            P("head", None),
        ),
        out_specs=P(("seq", "head"), None, None),
        check_vma=False,
    )
```
